32 devices in a mesh: seq: 8 (over y, x, core), chan: 4 (over z).
Axes of the slice: x: 2, y: 2, z: 4, core: 2. Of those that a mesh axis runs over, the one named last changes fastest.
Arguments:
- tokens: bfloat16 [8192, 1024], P(('seq', 'chan')), may hold values from -6 to 6
- doc_ids: int32 [8192], P('seq'), may hold values from 0 to 2, as said below
- cotangent: bfloat16 [8192, 1024], P(('seq', 'chan')), may hold values from -6 to 6
- norm_gain: float32 [1024], replicated, may hold values from 0.1 to 1.9
- gate_proj: bfloat16 [1024, 1536], P(None, 'chan'), may hold values from -0.1875 to 0.1875
- input_proj: bfloat16 [1024, 1536], P(None, 'chan'), may hold values from -0.1875 to 0.1875
- conv_weight: float32 [4, 1536], P(None, 'chan'), may hold values from -3 to 3
- conv_bias: float32 [1536], P('chan'), may hold values from -3 to 3
- recall_weight: float32 [16, 96, 96], P('chan'), may hold values from -0.625 to 0.625
- recall_bias: float32 [16, 96], P('chan'), may hold values from -4 to 4
- admit_weight: float32 [16, 96, 96], P('chan'), may hold values from -0.625 to 0.625
- admit_bias: float32 [16, 96], P('chan'), may hold values from -4 to 4
- decay_param: float32 [1536], P('chan'), may hold values from 2 to 9
- out_proj: bfloat16 [1536, 1024], P('chan'), may hold values from -0.625 to 0.625
- mlp_gain: float32 [1024], replicated, may hold values from 0.1 to 1.9
- mlp_gate: bfloat16 [1024, 3072], P(('seq', 'chan')), may hold values from -0.1875 to 0.1875
- mlp_up: bfloat16 [1024, 3072], P(('seq', 'chan')), may hold values from -0.1875 to 0.1875
- mlp_down: bfloat16 [1024, 3072], P(('seq', 'chan')), may hold values from -0.21875 to 0.21875
Outputs:
- block_out: bfloat16 [8192, 1024], P(('seq', 'chan'))
- grad_tokens: float32 [8192, 1024], P(('seq', 'chan'))
- grad_norm_gain: float32 [1024], replicated
- grad_gate_proj: float32 [1024, 1536], P(None, 'chan')
- grad_input_proj: float32 [1024, 1536], P(None, 'chan')
- grad_conv_weight: float32 [4, 1536], P(None, 'chan')
- grad_conv_bias: float32 [1536], P('chan')
- grad_recall_weight: float32 [16, 96, 96], P('chan')
- grad_recall_bias: float32 [16, 96], P('chan')
- grad_admit_weight: float32 [16, 96, 96], P('chan')
- grad_admit_bias: float32 [16, 96], P('chan')
- grad_decay_param: float32 [1536], P('chan')
- grad_out_proj: float32 [1536, 1024], P('chan')
- grad_mlp_gain: float32 [1024], replicated
- grad_mlp_gate: float32 [1024, 3072], P(('seq', 'chan'))
- grad_mlp_up: float32 [1024, 3072], P(('seq', 'chan'))
- grad_mlp_down: float32 [1024, 3072], P(('seq', 'chan'))
- gate_mean: float32 [1536], P('chan')
The draws below stay inside these ranges and needn't reach their ends.
Inputs may be any that keep to these rules, and one draw needn't show every extreme that they name: `doc_ids`: each token's document number within its sequence: 0 at a sequence's first token, never falling inside a sequence.
All inputs are finite; a program needn't handle non-finite values.
Results may differ from the reference program's by a relative error of at most 0.012.
Values may be sent and summed in bfloat16 or wider, within the bound.
No kernel may reach another device: no remote copies, remote signals or barrier semaphores. Data moves between devices by JAX's collectives and lax.ppermute only.
A program may use at most 320 MiB of HBM per device.

```python
import jax
import jax.numpy as jnp
from jax import lax

D = 1024
LRU = 1536
FF = 3072
HEADS = 16
CONV = 4
HEAD = 96
LENGTH = 1024
TOKENS = 8192


def draw_doc_ids(key, part):
    key = jax.random.fold_in(key, 7)
    number = TOKENS // LENGTH
    first_key, second_key = jax.random.split(key)
    first = jax.random.randint(first_key, (number, 1), 1, LENGTH // 8)
    second = jax.random.randint(second_key, (number, 1), LENGTH - LENGTH // 8, LENGTH)
    places = jnp.arange(LENGTH, dtype=jnp.int32)[None, :]
    labels = (places >= first).astype(jnp.int32) + (places >= second).astype(jnp.int32)
    return labels.reshape(TOKENS)


def block_levels(key, dims, cuts, least, top_value):
    level, own = 1.0, jax.random.fold_in(key, 6)
    for dim, shards_of in cuts:
        heights = jnp.exp(jax.random.uniform(jax.random.fold_in(own, dim), (shards_of,), jnp.float32, least / len(cuts), top_value / len(cuts)))
        level = level * jnp.repeat(heights, dims[dim] // shards_of).reshape([-1 if axis == dim else 1 for axis in range(len(dims))])
    return level


def centred(own_key, dims, scale, most, cuts=(), held_as=jnp.bfloat16):
    drawn = scale * jax.random.normal(own_key, dims, jnp.float32)
    if cuts:
        drawn = drawn * block_levels(own_key, dims, cuts, -0.22, 0.18)
    return jnp.clip(drawn, -most, most).astype(held_as)


def setup_inputs(seed: int = 0) -> dict:
    key_of = jax.random.split(jax.random.key(seed), 19)
    tokens = centred(key_of[0], (TOKENS, D), 1.0, 6.0, ((0, 32),))
    doc_ids = draw_doc_ids(jax.random.fold_in(key_of[18], 71), 0)
    cotangent = centred(key_of[2], (TOKENS, D), 1.0, 6.0, ((0, 32),))
    norm_gain = jnp.clip(1.0 + 0.18 * jax.random.normal(key_of[3], (D,), jnp.float32), 0.1, 1.9)
    gate_proj = centred(key_of[4], (D, LRU), D ** -0.5, 0.1875, ((1, 4),))
    input_proj = centred(key_of[5], (D, LRU), D ** -0.5, 0.1875, ((1, 4),))
    conv_weight = centred(key_of[6], (CONV, LRU), 0.5, 3.0, ((1, 4),), jnp.float32)
    conv_bias = centred(key_of[7], (LRU,), 0.5, 3.0, ((0, 4),), jnp.float32)
    recall_weight = centred(key_of[8], (HEADS, HEAD, HEAD), HEAD ** -0.5, 0.625, ((0, 4),), jnp.float32)
    recall_bias = centred(key_of[9], (HEADS, HEAD), 1.0, 4.0, ((0, 4),), jnp.float32)
    admit_weight = centred(key_of[10], (HEADS, HEAD, HEAD), HEAD ** -0.5, 0.625, ((0, 4),), jnp.float32)
    admit_bias = centred(key_of[11], (HEADS, HEAD), 1.0, 4.0, ((0, 4),), jnp.float32)
    decay_param = jnp.clip(2.0 + 7.0 * jax.random.uniform(key_of[12], (LRU,), jnp.float32) ** block_levels(key_of[12], (LRU,), ((0, 4),), -0.2, 0.2), 2.0, 9.0)
    out_proj = centred(key_of[13], (LRU, D), (LRU // 16) ** -0.5, 0.625, ((0, 4),))
    mlp_gain = jnp.clip(1.0 + 0.18 * jax.random.normal(key_of[14], (D,), jnp.float32), 0.1, 1.9)
    mlp_gate = centred(key_of[15], (D, FF), D ** -0.5, 0.1875, ((0, 32),))
    mlp_up = centred(key_of[16], (D, FF), D ** -0.5, 0.1875, ((0, 32),))
    mlp_down = centred(key_of[17], (D, FF), (FF // 4) ** -0.5, 0.21875, ((0, 32),))
    return {"tokens": tokens, "doc_ids": doc_ids, "cotangent": cotangent, "norm_gain": norm_gain, "gate_proj": gate_proj, "input_proj": input_proj, "conv_weight": conv_weight, "conv_bias": conv_bias, "recall_weight": recall_weight, "recall_bias": recall_bias, "admit_weight": admit_weight, "admit_bias": admit_bias, "decay_param": decay_param, "out_proj": out_proj, "mlp_gain": mlp_gain, "mlp_gate": mlp_gate, "mlp_up": mlp_up, "mlp_down": mlp_down}


EPS = 1e-06
STRENGTH = 8.0
HIGHEST = lax.Precision.HIGHEST

@jax.custom_vjp
def low(v):
    return lax.optimization_barrier(v.astype(jnp.bfloat16)).astype(jnp.float32)

@jax.custom_vjp
def low_back(v):
    return v

def low_keep(v):
    return (low(v), None)

def low_pass(kept, grad):
    return (grad,)

def back_keep(v):
    return (v, None)

def back_low(kept, grad):
    return (low(grad),)
low.defvjp(low_keep, low_pass)
low_back.defvjp(back_keep, back_low)

def normalize(values, gain):
    scale = lax.rsqrt(lax.optimization_barrier(jnp.mean(values * values, axis=-1, keepdims=True)) + EPS)
    return values * scale * gain

def combine(early, late):
    return (early[0] * late[0], late[0] * early[1] + late[1])

def mixer(gated_in, inputs, doc_ids, conv_weight, conv_bias, recall_weight, recall_bias, admit_weight, admit_bias, decay_param):
    count, width = inputs.shape
    heads, block = recall_bias.shape
    places = jnp.arange(count) % LENGTH
    prior = jnp.concatenate([doc_ids[:1], doc_ids[:-1]])
    keeper = ((places > 0) & (doc_ids == prior)).astype(jnp.float32)
    conv = conv_bias + conv_weight[0] * inputs
    for shift in range(1, conv_weight.shape[0]):
        moved = jnp.concatenate([jnp.zeros((shift, width), jnp.float32), inputs[:count - shift]])
        moved_doc = jnp.concatenate([jnp.full((shift,), -1, jnp.int32), doc_ids[:count - shift]])
        valid = ((places >= shift) & (doc_ids == moved_doc)).astype(jnp.float32)
        conv = conv + conv_weight[shift] * moved * valid[:, None]
    grouped = conv.reshape(count, heads, block)
    recall = jax.nn.sigmoid(jnp.einsum('rhc,hcd->rhd', grouped, recall_weight, precision=HIGHEST).reshape(count, width) + recall_bias.reshape(width))
    admit = jax.nn.sigmoid(jnp.einsum('rhc,hcd->rhd', grouped, admit_weight, precision=HIGHEST).reshape(count, width) + admit_bias.reshape(width))
    log_decay = -STRENGTH * recall * jax.nn.softplus(-decay_param)
    decay = jnp.exp(log_decay)
    inject = jnp.sqrt(-jnp.expm1(2.0 * log_decay)) * admit * conv
    carried, state = lax.associative_scan(combine, (decay * keeper[:, None], inject), axis=0)
    return (jax.nn.gelu(gated_in) * state, lax.optimization_barrier(jnp.sum(decay, axis=0)))

def block(params, resid, doc_ids):
    norm_gain, gate_proj, input_proj, conv_weight, conv_bias, recall_weight, recall_bias, admit_weight, admit_bias, decay_param, out_proj, mlp_gain, mlp_gate, mlp_up, mlp_down = params
    normed = low(normalize(resid, norm_gain))
    gated_in = low_back(low(jnp.dot(normed, gate_proj, precision=HIGHEST)))
    inputs = low_back(low(jnp.dot(normed, input_proj, precision=HIGHEST)))
    mixed, decay_sum = mixer(gated_in, inputs, doc_ids, conv_weight, conv_bias, recall_weight, recall_bias, admit_weight, admit_bias, decay_param)
    branch_in = low_back(low(mixed))
    branch = low_back(jnp.dot(branch_in, out_proj, precision=HIGHEST))
    middle = resid + branch
    second = low(normalize(middle, mlp_gain))
    gate = low_back(jnp.dot(second, mlp_gate, precision=HIGHEST))
    upward = low_back(jnp.dot(second, mlp_up, precision=HIGHEST))
    hidden = low(jax.nn.gelu(gate) * upward)
    result = low_back(jnp.dot(hidden, mlp_down.T, precision=HIGHEST))
    return (middle + result, decay_sum)

def reference(tokens, doc_ids, cotangent, norm_gain, gate_proj, input_proj, conv_weight, conv_bias, recall_weight, recall_bias, admit_weight, admit_bias, decay_param, out_proj, mlp_gain, mlp_gate, mlp_up, mlp_down):
    params = tuple((item.astype(jnp.float32) for item in (norm_gain, gate_proj, input_proj, conv_weight, conv_bias, recall_weight, recall_bias, admit_weight, admit_bias, decay_param, out_proj, mlp_gain, mlp_gate, mlp_up, mlp_down)))
    number = TOKENS // LENGTH
    rows = tokens.astype(jnp.float32).reshape(number, LENGTH, D)
    docs = doc_ids.reshape(number, LENGTH)
    cots = cotangent.astype(jnp.float32).reshape(number, LENGTH, D)

    def step(carry, batch):
        grads, decay_total = carry
        resid, docs_one, cot_one = batch

        def forward(weights, values):
            return block(weights, values, docs_one)
        output, pull, decay_sum = jax.vjp(forward, params, resid, has_aux=True)
        weight_grads, token_grads = pull(cot_one)
        grads = jax.tree.map(jnp.add, grads, weight_grads)
        return ((grads, decay_total + decay_sum), (output.astype(jnp.bfloat16), token_grads))
    start = (jax.tree.map(jnp.zeros_like, params), jnp.zeros((LRU,), jnp.float32))
    (grads, decay_total), (outputs, token_grads) = lax.scan(step, start, (rows, docs, cots))
    return (outputs.reshape(TOKENS, D), token_grads.reshape(TOKENS, D), grads[0], grads[1], grads[2], grads[3], grads[4], grads[5], grads[6], grads[7], grads[8], grads[9], grads[10], grads[11], grads[12], grads[13], grads[14], decay_total / TOKENS)
```

```python
import functools

import jax
import jax.numpy as jnp
from jax import lax
from jax.experimental import pallas as pl
from jax.experimental.pallas import tpu as pltpu
from jax.sharding import PartitionSpec as P

LENGTH = 1024
EPS = 1e-06
STRENGTH = 8.0
HALO = 16
GELU_A = 0.7978845608028654
GELU_B = 0.044715
BF16 = jnp.bfloat16
F32 = jnp.float32
VMEM_BYTES = 60 * 1024 * 1024


def mm(left, right, left_dim, right_dim):
    return lax.dot_general(
        left, right, (((left_dim,), (right_dim,)), ((), ())), preferred_element_type=F32
    )


def gelu_parts(value):
    square = value * value
    th = jnp.tanh(GELU_A * value * (1.0 + GELU_B * square))
    half = 0.5 * (1.0 + th)
    slope = half + 0.5 * value * (1.0 - th * th) * (GELU_A * (1.0 + 3.0 * GELU_B * square))
    return value * half, slope


def gelu(value):
    th = jnp.tanh(GELU_A * value * (1.0 + GELU_B * value * value))
    return 0.5 * value * (1.0 + th)


def one_minus_exp(v):
    series = v * (
        1.0
        - v
        * (1 / 2)
        * (
            1.0
            - v
            * (1 / 3)
            * (1.0 - v * (1 / 4) * (1.0 - v * (1 / 5) * (1.0 - v * (1 / 6) * (1.0 - v * (1 / 7)))))
        )
    )
    return jnp.where(v < 0.4, series, 1.0 - jnp.exp(-v))


def rows_index(shape):
    return lax.broadcasted_iota(jnp.int32, shape, 0)


def scan_down(a, b):
    count = a.shape[0]
    index = rows_index(a.shape)
    step = 1
    while step < count:
        if step < 8:
            inside = index >= step
            a_prev = jnp.where(inside, pltpu.roll(a, step, 0), 1.0)
            b_prev = jnp.where(inside, pltpu.roll(b, step, 0), 0.0)
        else:
            a_prev = jnp.concatenate([jnp.ones_like(a[:step]), a[: count - step]], axis=0)
            b_prev = jnp.concatenate([jnp.zeros_like(b[:step]), b[: count - step]], axis=0)
        b = b + a * b_prev
        a = a * a_prev
        step *= 2
    return a, b


def scan_up(a, b):
    count = a.shape[0]
    index = rows_index(a.shape)
    step = 1
    while step < count:
        if step < 8:
            inside = index < count - step
            a_next = jnp.where(inside, pltpu.roll(a, count - step, 0), 1.0)
            b_next = jnp.where(inside, pltpu.roll(b, count - step, 0), 0.0)
        else:
            a_next = jnp.concatenate([a[step:], jnp.ones_like(a[:step])], axis=0)
            b_next = jnp.concatenate([b[step:], jnp.zeros_like(b[:step])], axis=0)
        b = b + a * b_next
        a = a * a_next
        step *= 2
    return a, b


def block_diagonal(flat, head, dtype):
    width = flat.shape[1]
    tall = jnp.concatenate([flat] * (width // head), axis=0)
    shape = (width, width)
    row = lax.broadcasted_iota(jnp.int32, shape, 0) // head
    col = lax.broadcasted_iota(jnp.int32, shape, 1) // head
    return jnp.where(row == col, tall, 0.0).astype(dtype)


def fold_diagonal(square, head):
    width = square.shape[0]
    row = lax.broadcasted_iota(jnp.int32, square.shape, 0) // head
    col = lax.broadcasted_iota(jnp.int32, square.shape, 1) // head
    kept = jnp.where(row == col, square, 0.0)
    total = kept[:head]
    for start in range(head, width, head):
        total = total + kept[start : start + head]
    return total


def vmem():
    return pl.BlockSpec(memory_space=pltpu.VMEM)


def smem():
    return pl.BlockSpec(memory_space=pltpu.SMEM)


def params(**more):
    return pltpu.CompilerParams(vmem_limit_bytes=VMEM_BYTES, **more)


def mix_local_kernel(own, head, pieces, me_ref, nx_ref, mask_ref, gates_ref, vec_ref, *rest):
    weight_refs, rest = rest[:pieces], rest[pieces:]
    weights, inputs_out, gated_out, kept_out, scan_out, edge_out = rest[-6:]
    if own:
        weights[0] = weight_refs[0][...]
    else:
        block = weight_refs[0].shape[1]
        for rel in range(pieces):
            start = pl.multiple_of((me_ref[0] ^ rel) * block, block)
            for part in range(3):
                weights[0, part, pl.ds(start, block), :] = weight_refs[rel][part]
    count = mask_ref.shape[0]
    gated = mm(nx_ref[HALO:], weights[0, 0], 1, 0).astype(BF16)
    gated_out[0] = gated
    inputs = mm(nx_ref[...], weights[0, 1], 1, 0).astype(BF16)
    inputs_out[0] = inputs
    wide = inputs.astype(F32)
    vec = vec_ref[...]
    conv = vec[4:5] + vec[0:1] * wide[HALO:]
    for shift in range(1, 4):
        moved = pltpu.roll(wide, shift, 0)[HALO:]
        conv = conv + vec[shift : shift + 1] * (moved * mask_ref[:, shift : shift + 1])
    low = conv.astype(BF16)
    width = conv.shape[1]
    recall_weight = block_diagonal(gates_ref[:, :width], head, BF16)
    admit_weight = block_diagonal(gates_ref[:, width:], head, BF16)
    recall = jax.nn.sigmoid(mm(low, recall_weight, 1, 0) + vec[5:6])
    admit = jax.nn.sigmoid(mm(low, admit_weight, 1, 0) + vec[6:7])
    rate = STRENGTH * recall * vec[7:8]
    decay = jnp.exp(-rate)
    inject = jnp.sqrt(one_minus_exp(2.0 * rate)) * admit * conv
    product, state = scan_down(decay * mask_ref[:, 1:2], inject)
    kept_out[0, 0] = conv
    kept_out[0, 1] = recall
    kept_out[0, 2] = admit
    scan_out[0, 0] = product
    scan_out[0, 1] = state
    edge_out[0, 0:1] = product[count - 1 :]
    edge_out[0, 1:2] = state[count - 1 :]
    edge_out[0, 2:3] = jnp.sum(decay, axis=0, keepdims=True)


def mix_local(shard, shards, head, me, nx, mask, gates, vec, weights, stacks):
    count = mask.shape[0]
    width = vec.shape[1]
    model = nx.shape[1]
    own = shard == 0
    pieces = len(weights)
    shapes = [
        ((shards, 3, model, width), BF16),
        ((shards, count + HALO, width), BF16),
        ((shards, count, width), BF16),
        ((shards, 3, count, width), F32),
        ((shards, 2, count, width), F32),
        ((shards, 8, width), F32),
    ]

    def at(shape):
        tail = (0,) * (len(shape) - 1)
        return pl.BlockSpec((1,) + shape[1:], lambda i: (shard,) + tail)

    first = [me, nx, mask, gates, vec, *weights]
    in_specs = [smem()] + [vmem()] * (len(first) - 1)
    aliases = {}
    if stacks is not None:
        aliases = {len(first) + i: i for i in range(len(stacks))}
        in_specs += [pl.BlockSpec(memory_space=pl.ANY)] * len(stacks)
        first += list(stacks)
    flops = 2 * (2 * count + HALO) * model * width + 4 * count * width * width
    return pl.pallas_call(
        functools.partial(mix_local_kernel, own, head, pieces),
        grid=(1,),
        out_shape=[jax.ShapeDtypeStruct(shape, dtype) for shape, dtype in shapes],
        in_specs=in_specs,
        out_specs=[at(shape) for shape, _ in shapes],
        input_output_aliases=aliases,
        compiler_params=params(),
        cost_estimate=pl.CostEstimate(
            flops=flops, bytes_accessed=8 * 1024 * 1024, transcendentals=6 * count * width
        ),
        name="mix_local",
    )(*first)


def carried(edges):
    total = edges[-1][0, 1:2]
    for edge in edges[-2::-1]:
        total = edge[0, 1:2] + edge[0, 0:1] * total
    return total


def branch_kernel(
    depth, scan_ref, gated_ref, weight_ref, resid_ref, gain_ref, *rest
):
    edges = rest[:depth]
    carry_out, branch_in_out, middle_out, second_out, acc = rest[depth:]
    step = pl.program_id(0)

    @pl.when(step == 0)
    def _():
        acc[...] = resid_ref[...].astype(F32)

    carry = carried(edges)
    carry_out[0] = jnp.broadcast_to(carry, carry_out.shape[1:])
    state = scan_ref[0, 1] + scan_ref[0, 0] * carry
    mixed = (gelu(gated_ref[0].astype(F32)) * state).astype(BF16)
    branch_in_out[0] = mixed
    acc[...] += mm(mixed, weight_ref[0, 0], 1, 1)

    @pl.when(step == pl.num_programs(0) - 1)
    def _():
        middle = acc[...]
        middle_out[...] = middle
        scale = lax.rsqrt(jnp.mean(middle * middle, axis=1, keepdims=True) + EPS)
        second_out[...] = (middle * scale * gain_ref[...]).astype(BF16)


def branch(scan, gated, weights, tokens, gain, edges):
    shards, _, count, width = scan.shape
    model = tokens.shape[1]

    def edge_spec(shift):
        return pl.BlockSpec((1, 8, width), lambda s: ((s + shards - shift % shards) % shards, 0, 0))

    return pl.pallas_call(
        functools.partial(branch_kernel, len(edges)),
        grid=(shards,),
        out_shape=[
            jax.ShapeDtypeStruct((shards, 8, width), F32),
            jax.ShapeDtypeStruct((shards, count, width), BF16),
            jax.ShapeDtypeStruct((count, model), F32),
            jax.ShapeDtypeStruct((count, model), BF16),
        ],
        in_specs=[
            pl.BlockSpec((1, 2, count, width), lambda s: (s, 0, 0, 0)),
            pl.BlockSpec((1, count, width), lambda s: (s, 0, 0)),
            pl.BlockSpec((1, 1, model, width), lambda s: (s, 2, 0, 0)),
            pl.BlockSpec((count, model), lambda s: (0, 0)),
            pl.BlockSpec((1, model), lambda s: (0, 0)),
        ]
        + [edge_spec(i + 1) for i in range(len(edges))],
        out_specs=[
            pl.BlockSpec((1, 8, width), lambda s: (s, 0, 0)),
            pl.BlockSpec((1, count, width), lambda s: (s, 0, 0)),
            pl.BlockSpec((count, model), lambda s: (0, 0)),
            pl.BlockSpec((count, model), lambda s: (0, 0)),
        ],
        scratch_shapes=[pltpu.VMEM((count, model), F32)],
        compiler_params=params(),
        name="mix_branch",
    )(scan, gated, weights, tokens, gain, *edges)


def mlp_kernel(
    sec_a, sec_b, cot_a, cot_b, weight_ref, gate_grad_out, up_grad_out, hidden_out, grad_a, grad_b
):
    second = jnp.concatenate([sec_a[...], sec_b[...]], axis=0)
    cot = jnp.concatenate([cot_a[...], cot_b[...]], axis=0)
    gate = mm(second, weight_ref[0], 1, 0)
    upward = mm(second, weight_ref[1], 1, 0)
    hidden_grad = mm(cot, weight_ref[2], 1, 0)
    act, slope = gelu_parts(gate)
    hidden_out[...] = (act * upward).astype(BF16)
    gate_grad = (hidden_grad * upward * slope).astype(BF16)
    up_grad = (hidden_grad * act).astype(BF16)
    gate_grad_out[...] = gate_grad
    up_grad_out[...] = up_grad
    back = mm(gate_grad, weight_ref[0], 1, 1) + mm(up_grad, weight_ref[1], 1, 1)
    count = sec_a.shape[0]
    grad_a[...] = back[:count].astype(BF16)
    grad_b[...] = back[count:].astype(BF16)


def mlp_block(sec_a, sec_b, cot_a, cot_b, weights):
    count, model = sec_a.shape
    width = weights.shape[2]
    wide = jax.ShapeDtypeStruct((2 * count, width), BF16)
    tall = jax.ShapeDtypeStruct((count, model), BF16)
    return pl.pallas_call(
        mlp_kernel,
        out_shape=[wide, wide, wide, tall, tall],
        in_specs=[vmem()] * 5,
        out_specs=[vmem()] * 5,
        compiler_params=params(),
        cost_estimate=pl.CostEstimate(
            flops=20 * count * model * width,
            bytes_accessed=8 * 1024 * 1024,
            transcendentals=2 * count * width,
        ),
        name="mlp_block",
    )(sec_a, sec_b, cot_a, cot_b, weights)


def mlp_grads_kernel(blocks, model, weight_ref, *rest):
    seconds, rest = rest[: 2 * blocks], rest[2 * blocks :]
    cots, rest = rest[: 2 * blocks], rest[2 * blocks :]
    gate_grads, rest = rest[:blocks], rest[blocks:]
    up_grads, rest = rest[:blocks], rest[blocks:]
    hiddens, rest = rest[:blocks], rest[blocks:]
    grads_out, rest = rest[0], rest[1:]
    results, acc = rest[: 2 * blocks], rest[2 * blocks]
    count = seconds[0].shape[0]
    for block in range(blocks):
        second = jnp.concatenate([seconds[2 * block][...], seconds[2 * block + 1][...]], axis=0)
        cot = jnp.concatenate([cots[2 * block][...], cots[2 * block + 1][...]], axis=0)
        hidden = hiddens[block][...]
        terms = (
            mm(second, gate_grads[block][...], 0, 0),
            mm(second, up_grads[block][...], 0, 0),
            mm(cot, hidden, 0, 0),
        )
        for part, term in enumerate(terms):
            if block == 0:
                acc[part] = term
            else:
                acc[part] += term
        result = mm(hidden, weight_ref[0], 1, 1)
        results[2 * block][...] = result[:count].astype(BF16)
        results[2 * block + 1][...] = result[count:].astype(BF16)
    shards, group, _, piece, _ = grads_out.shape
    for shard in range(shards):
        for owner in range(group):
            start = (owner * shards + shard) * piece
            for part in range(3):
                grads_out[shard, owner, part] = acc[part, start : start + piece].astype(BF16)


def mlp_grads(weights, seconds, cots, gate_grads, up_grads, hiddens, shards):
    group = len(seconds)
    count, model = seconds[0].shape
    width = weights.shape[2]
    piece = model // (group * shards)
    return pl.pallas_call(
        functools.partial(mlp_grads_kernel, group // 2, model),
        grid=(1,),
        out_shape=[jax.ShapeDtypeStruct((shards, group, 3, piece, width), BF16)]
        + [jax.ShapeDtypeStruct((count, model), BF16)] * group,
        in_specs=[pl.BlockSpec((1, model, width), lambda i: (2, 0, 0))]
        + [vmem()] * (2 * group + 3 * (group // 2)),
        out_specs=[vmem()] * (1 + group),
        scratch_shapes=[pltpu.VMEM((3, model, width), F32)],
        compiler_params=params(),
        cost_estimate=pl.CostEstimate(
            flops=8 * count * group * model * width,
            bytes_accessed=20 * 1024 * 1024,
            transcendentals=0,
        ),
        name="mlp_grads",
    )(weights, *seconds, *cots, *gate_grads, *up_grads, *hiddens)


def split_rows(me, values, own_out, other_out, lead):
    half, _, _, block, _ = own_out.shape
    for j in range(half):
        for out, rel in ((own_out, 2 * j), (other_out, 2 * j + 1)):
            start = pl.multiple_of((me ^ rel) * block, block)
            out[j, 0, lead] = values[pl.ds(start, block), :]


def adjoint_kernel(
    me_ref,
    grad_ref,
    normed_ref,
    weight_ref,
    gated_ref,
    scan_ref,
    kept_ref,
    carry_ref,
    branch_in_ref,
    mask_ref,
    rate_ref,
    gate_back_out,
    adjoint_out,
    edge_out,
    own_out,
    other_out,
    whole,
):
    grad = grad_ref[...]
    into = mm(grad, weight_ref[0, 0], 1, 0).astype(BF16).astype(F32)
    act, slope = gelu_parts(gated_ref[0].astype(F32))
    state = scan_ref[0, 1] + scan_ref[0, 0] * carry_ref[0, 0:1]
    gate_back = (into * state * slope).astype(BF16)
    gate_back_out[0] = gate_back
    decay = jnp.exp(-STRENGTH * kept_ref[0, 0] * rate_ref[0]) * mask_ref[:, 1:2]
    count = decay.shape[0]
    shifted = jnp.where(
        rows_index(decay.shape) < count - 1, pltpu.roll(decay, count - 1, 0), 1.0
    )
    product, value = scan_up(shifted, into * act)
    adjoint_out[0, 0] = product
    adjoint_out[0, 1] = value
    edge_out[0] = jnp.broadcast_to(decay[0:1] * value[0:1], edge_out.shape[1:])
    whole[...] = mm(normed_ref[...], gate_back, 0, 0).astype(BF16)
    split_rows(me_ref[0], whole, own_out, other_out, 0)
    whole[...] = mm(grad, branch_in_ref[0], 0, 0).astype(BF16)
    split_rows(me_ref[0], whole, own_out, other_out, 1)


def adjoint(me, grad, normed, weights, gated, scan, kept, carry, branch_in, mask, rate, group):
    shards, _, count, width = scan.shape
    model = grad.shape[1]
    block = model // group

    def flat(*shape):
        return pl.BlockSpec(shape, lambda s: (0,) * len(shape))

    def at(*shape):
        return pl.BlockSpec((1,) + shape, lambda s: (s,) + (0,) * len(shape))

    split = jax.ShapeDtypeStruct((group // 2, shards, 2, block, width), BF16)
    split_spec = pl.BlockSpec((group // 2, 1, 2, block, width), lambda s: (0, s, 0, 0, 0))
    return pl.pallas_call(
        adjoint_kernel,
        grid=(shards,),
        out_shape=[
            jax.ShapeDtypeStruct((shards, count, width), BF16),
            jax.ShapeDtypeStruct((shards, 2, count, width), F32),
            jax.ShapeDtypeStruct((shards, 8, width), F32),
            split,
            split,
        ],
        in_specs=[
            smem(),
            flat(count, model),
            flat(count, model),
            pl.BlockSpec((1, 1, model, width), lambda s: (s, 2, 0, 0)),
            at(count, width),
            at(2, count, width),
            pl.BlockSpec((1, 1, count, width), lambda s: (s, 1, 0, 0)),
            at(8, width),
            at(count, width),
            flat(*mask.shape),
            at(1, width),
        ],
        out_specs=[at(count, width), at(2, count, width), at(8, width), split_spec, split_spec],
        scratch_shapes=[pltpu.VMEM((model, width), BF16)],
        compiler_params=params(),
        cost_estimate=pl.CostEstimate(
            flops=6 * count * model * width * shards,
            bytes_accessed=24 * 1024 * 1024,
            transcendentals=4 * count * width * shards,
        ),
        name="mix_adjoint",
    )(me, grad, normed, weights, gated, scan, kept, carry, branch_in, mask, rate)


def mix_back_kernel(
    head,
    depth,
    me_ref,
    nx_ref,
    gate_weight_ref,
    input_weight_ref,
    inputs_ref,
    gate_back_ref,
    kept_ref,
    scan_ref,
    adjoint_ref,
    carry_ref,
    mask_ref,
    gates_ref,
    vec_ref,
    edge_ref,
    *rest,
):
    backs, decays = rest[:depth], rest[depth : 2 * depth - 1]
    own_out, other_out, normed_grad_out, whole, acc = rest[2 * depth - 1 :]
    step = pl.program_id(0)
    count = mask_ref.shape[0]
    width = vec_ref.shape[2]
    vec = vec_ref[0]
    incoming = backs[-1][0, 0:1]
    for back, edge in zip(backs[-2::-1], decays[::-1], strict=True):
        incoming = back[0, 0:1] + edge[0, 0:1] * incoming
    adj = adjoint_ref[0, 1] + adjoint_ref[0, 0] * incoming
    carry = carry_ref[0, 0:1]
    state = scan_ref[0, 1] + scan_ref[0, 0] * carry
    before = jnp.where(rows_index(state.shape) == 0, carry, pltpu.roll(state, 1, 0))
    conv, recall, admit = kept_ref[0, 0], kept_ref[0, 1], kept_ref[0, 2]
    speed = STRENGTH * vec[7:8]
    rate = recall * speed
    decay = jnp.exp(-rate)
    size = jnp.sqrt(one_minus_exp(2.0 * rate))
    sized = adj * size
    pulled = adj * admit
    log_grad = decay * (adj * before * mask_ref[:, 1:2] - pulled * conv * decay / size)
    recall_grad = -speed * log_grad * recall * (1.0 - recall)
    admit_grad = sized * conv * admit * (1.0 - admit)
    conv_grad = sized * admit
    recall_low = recall_grad.astype(BF16)
    admit_low = admit_grad.astype(BF16)
    recall_weight = block_diagonal(gates_ref[0, :, :width], head, BF16)
    admit_weight = block_diagonal(gates_ref[0, :, width:], head, BF16)
    conv_grad = conv_grad + mm(recall_low, recall_weight, 1, 1) + mm(admit_low, admit_weight, 1, 1)
    wide = inputs_ref[0].astype(F32)
    blank = jnp.zeros((HALO, width), F32)
    reach = jnp.concatenate([blank, vec[0:1] * conv_grad], axis=0)
    tap_grads = [jnp.sum(conv_grad * wide[HALO:], axis=0, keepdims=True)]
    for shift in range(1, 4):
        masked = conv_grad * mask_ref[:, shift : shift + 1]
        moved = pltpu.roll(wide, shift, 0)[HALO:]
        tap_grads.append(jnp.sum(masked * moved, axis=0, keepdims=True))
        back = jnp.concatenate([blank, vec[shift : shift + 1] * masked], axis=0)
        reach = reach + pltpu.roll(back, count + HALO - shift, 0)
    input_back = reach.astype(BF16)
    conv_low = conv.astype(BF16)
    model = nx_ref.shape[1]
    whole[:model] = mm(nx_ref[...], input_back, 0, 0).astype(BF16)
    whole[model : model + head] = fold_diagonal(mm(conv_low, recall_low, 0, 0), head).astype(BF16)
    whole[model + head : model + 2 * head] = fold_diagonal(
        mm(conv_low, admit_low, 0, 0), head
    ).astype(BF16)
    rows = tap_grads + [
        jnp.sum(conv_grad, axis=0, keepdims=True),
        jnp.sum(recall_grad, axis=0, keepdims=True),
        jnp.sum(admit_grad, axis=0, keepdims=True),
        jnp.sum(recall * log_grad, axis=0, keepdims=True),
        edge_ref[0, 2:3],
    ]
    rows.append(jnp.zeros((whole.shape[0] - model - 2 * head - len(rows), width), F32))
    whole[model + 2 * head :] = jnp.concatenate(rows, axis=0).astype(BF16)
    half, _, block, _ = own_out.shape
    main = model // (2 * half)
    extra = block - main
    for j in range(half):
        for out, rel in ((own_out, 2 * j), (other_out, 2 * j + 1)):
            owner = me_ref[0] ^ rel
            start = pl.multiple_of(owner * main, main)
            out[j, 0, :main] = whole[pl.ds(start, main), :]
            start = pl.multiple_of(model + owner * extra, extra)
            out[j, 0, main:] = whole[pl.ds(start, extra), :]
    through_gate = mm(gate_back_ref[0], gate_weight_ref[0, 0], 1, 1)
    through_input = mm(input_back, input_weight_ref[0, 0], 1, 1)

    @pl.when(step == 0)
    def _():
        acc[...] = through_input

    @pl.when(step > 0)
    def _():
        acc[...] += through_input

    acc[HALO:] += through_gate

    @pl.when(step == pl.num_programs(0) - 1)
    def _():
        normed_grad_out[...] = acc[...]


def mix_back(
    me, nx, weights, inputs, gate_back, kept, scan, adj, carry, mask, gates, vec, edge, backs, ahead, group
):
    shards, _, count, width = scan.shape
    model = nx.shape[1]
    head = gates.shape[1]
    depth = len(backs)
    tall = model + 256
    block = tall // group

    def flat(*shape):
        return pl.BlockSpec(shape, lambda s: (0,) * len(shape))

    def at(*shape):
        return pl.BlockSpec((1,) + shape, lambda s: (s,) + (0,) * len(shape))

    def ahead_spec(shift):
        return pl.BlockSpec((1, 8, width), lambda s: ((s + shift) % shards, 0, 0))

    split = jax.ShapeDtypeStruct((group // 2, shards, block, width), BF16)
    split_spec = pl.BlockSpec((group // 2, 1, block, width), lambda s: (0, s, 0, 0))
    return pl.pallas_call(
        functools.partial(mix_back_kernel, head, depth),
        grid=(shards,),
        out_shape=[split, split, jax.ShapeDtypeStruct((count + HALO, model), F32)],
        in_specs=[
            smem(),
            flat(count + HALO, model),
            pl.BlockSpec((1, 1, model, width), lambda s: (s, 0, 0, 0)),
            pl.BlockSpec((1, 1, model, width), lambda s: (s, 1, 0, 0)),
            at(count + HALO, width),
            at(count, width),
            at(3, count, width),
            at(2, count, width),
            at(2, count, width),
            at(8, width),
            flat(*mask.shape),
            at(head, 2 * width),
            at(8, width),
            at(8, width),
        ]
        + [ahead_spec(i + 1) for i in range(depth)]
        + [ahead_spec(i + 1) for i in range(depth - 1)],
        out_specs=[split_spec, split_spec, flat(count + HALO, model)],
        scratch_shapes=[
            pltpu.VMEM((tall, width), BF16),
            pltpu.VMEM((count + HALO, model), F32),
        ],
        compiler_params=params(),
        cost_estimate=pl.CostEstimate(
            flops=6 * count * model * width * shards,
            bytes_accessed=24 * 1024 * 1024,
            transcendentals=4 * count * width * shards,
        ),
        name="mix_back",
    )(
        me, nx, weights, weights, inputs, gate_back, kept, scan, adj, carry, mask, gates, vec, edge,
        *backs, *ahead
    )


def on_device(
    tokens,
    doc_ids,
    cotangent,
    norm_gain,
    gate_proj,
    input_proj,
    conv_weight,
    conv_bias,
    recall_weight,
    recall_bias,
    admit_weight,
    admit_bias,
    decay_param,
    out_proj,
    mlp_gain,
    mlp_gate,
    mlp_up,
    mlp_down,
):
    count, model = tokens.shape
    width = gate_proj.shape[1]
    heads, head, _ = recall_weight.shape
    hidden_width = mlp_gate.shape[1]
    piece = mlp_gate.shape[0]
    group = lax.axis_size("seq")
    shards = lax.axis_size("chan")
    block = model // group
    rank = lax.axis_index("seq")
    place = lax.axis_index("chan")
    me = rank.reshape(1).astype(jnp.int32)

    def flip(values, rel):
        return lax.ppermute(values, "seq", [(i, i ^ rel) for i in range(group)])

    def along(values, shift):
        return lax.ppermute(values, "chan", [(i, (i + shift) % shards) for i in range(shards)])

    def spread(values):
        held = [None] * group
        for rel in range(0, group, 2):
            held[rel] = values if rel == 0 else flip(values, rel)
        for rel in range(0, group, 2):
            held[rel + 1] = flip(held[rel], 1)
        return held

    def gather_sum(values):
        total = None
        for rel in range(0, group, 2):
            other = flip(values[rel + 1], 1)
            both = values[rel].astype(F32) + other.astype(F32)
            if rel:
                both = flip(both.astype(BF16), rel).astype(F32)
            total = both if total is None else total + both
        return total

    stacked = jnp.stack([gate_proj, input_proj, out_proj.T])
    mine = lax.dynamic_slice_in_dim(stacked, rank * block, block, 1)
    order = [0] + [s for i in range(1, shards // 2 + 1) for s in dict.fromkeys((i, shards - i))]
    at_shard = {}
    for shard in order[1:]:
        if shard == 1:
            at_shard[1] = along(mine, 1)
        elif shard <= shards // 2:
            at_shard[shard] = along(at_shard[shard - 1], 1)
        elif shard == shards - 1:
            at_shard[shard] = along(mine, -1)
        else:
            at_shard[shard] = along(at_shard[shard + 1], -1)
    weight_pieces = {0: [stacked]}
    for shard in order[1:]:
        weight_pieces[shard] = spread(at_shard[shard])

    speed = jax.nn.softplus(-decay_param)
    vec = jnp.concatenate(
        [
            conv_weight,
            conv_bias[None],
            recall_bias.reshape(1, width),
            admit_bias.reshape(1, width),
            speed[None],
        ]
    )
    gates = jnp.concatenate(
        [
            recall_weight.transpose(1, 0, 2).reshape(head, width),
            admit_weight.transpose(1, 0, 2).reshape(head, width),
        ],
        axis=1,
    ).astype(BF16)
    vecs = [vec] + [along(vec, s) for s in range(1, shards)]
    gates_all = [gates] + [along(gates, s) for s in range(1, shards)]

    offset = place * count
    spots = (offset + jnp.arange(count)) % LENGTH
    padded = jnp.concatenate([jnp.full((HALO,), -1, jnp.int32), doc_ids])
    here = lax.dynamic_slice_in_dim(padded, offset + HALO, count)
    columns = [jnp.ones((count,), F32)]
    for shift in range(1, 4):
        moved = lax.dynamic_slice_in_dim(padded, offset + HALO - shift, count)
        columns.append(((spots >= shift) & (here == moved)).astype(F32))
    columns += [jnp.zeros((count,), F32)] * 4
    mask = jnp.stack(columns, axis=1)

    resid = tokens.astype(F32)
    scale_one = lax.rsqrt(jnp.mean(resid * resid, axis=1, keepdims=True) + EPS)
    normed = (resid * scale_one * norm_gain).astype(BF16)
    nx = jnp.concatenate([along(normed[count - HALO :], 1), normed])

    slices = jnp.stack([mlp_gate, mlp_up, mlp_down])
    own_width = hidden_width // group
    slices = slices.reshape(3, piece, group, own_width).transpose(2, 0, 1, 3)
    slices = lax.all_to_all(slices, "seq", 0, 0, tiled=True)
    slices = lax.all_gather(slices, "chan", axis=0)
    mlp_weights = slices.transpose(2, 1, 0, 3, 4).reshape(3, model, own_width)

    cots = spread(cotangent)

    stacks = None
    for shard in order:
        stacks = mix_local(
            shard,
            shards,
            head,
            me,
            nx,
            mask,
            gates_all[shard],
            vecs[shard],
            weight_pieces[shard],
            stacks,
        )
    weights, inputs, gated, kept, scan, edge = stacks
    depth = LENGTH // count - 1
    behind = [along(edge, i + 1) for i in range(depth)]
    carry, branch_in, middle, second = branch(
        scan, gated, weights, tokens, mlp_gain.reshape(1, model), behind
    )
    ahead = [along(edge, -(i + 1)) for i in range(depth - 1)]

    seconds = spread(second)
    gate_grads, up_grads, hiddens, backs = [], [], [], []
    for rel in range(0, group, 2):
        gate_grad, up_grad, hidden, back_a, back_b = mlp_block(
            seconds[rel], seconds[rel + 1], cots[rel], cots[rel + 1], mlp_weights
        )
        gate_grads.append(gate_grad)
        up_grads.append(up_grad)
        hiddens.append(hidden)
        backs += [back_a, back_b]
    second_grad = gather_sum(backs)
    grads, *results = mlp_grads(
        mlp_weights, seconds, cots, gate_grads, up_grads, hiddens, shards
    )
    block_out = (middle + gather_sum(results)).astype(BF16)
    grads = lax.psum_scatter(grads, "chan", scatter_dimension=0)
    grads = lax.all_to_all(grads, "seq", 0, 0, tiled=True)
    grads = grads.transpose(1, 2, 0, 3).reshape(3, piece, hidden_width).astype(F32)

    def norm_back(grad, values, gain):
        scale = lax.rsqrt(jnp.mean(values * values, axis=1, keepdims=True) + EPS)
        scaled = grad * gain
        inner = jnp.mean(scaled * values, axis=1, keepdims=True)
        return (
            scale * scaled - values * (scale * scale * scale * inner),
            jnp.sum(grad * values * scale, axis=0),
        )

    back, gain_two = norm_back(second_grad, middle, mlp_gain)
    middle_grad = cotangent.astype(F32) + back
    branch_grad = middle_grad.astype(BF16)

    rate = jnp.stack([v[7:8] for v in vecs])
    gate_back, adj, edge_back, own_one, other_one = adjoint(
        me, branch_grad, normed, weights, gated, scan, kept, carry, branch_in, mask, rate, group
    )
    edges_back = [along(edge_back, -(i + 1)) for i in range(depth)]
    own_two, other_two, normed_grad = mix_back(
        me,
        nx,
        weights,
        inputs,
        gate_back,
        kept,
        scan,
        adj,
        carry,
        mask,
        jnp.stack(gates_all),
        jnp.stack(vecs),
        edge,
        edges_back,
        ahead,
        group,
    )

    def reduce(own, other):
        chip = own.astype(F32) + flip(other, 1).astype(F32)
        total = chip[0]
        for j in range(1, group // 2):
            total = total + flip(chip[j].astype(BF16), 2 * j).astype(F32)
        result = total[0]
        for s in range(1, shards):
            result = result + along(total[s].astype(BF16), -s).astype(F32)
        return result.astype(BF16)

    def assemble(values):
        held = jnp.stack(spread(values))
        index = jnp.arange(group) ^ rank
        return held[index]

    one = assemble(reduce(own_one, other_one))
    two = assemble(reduce(own_two, other_two))
    grad_gate = one[:, 0].reshape(model, width).astype(F32)
    grad_out = one[:, 1].reshape(model, width).T.astype(F32)
    grad_input = two[:, :block].reshape(model, width).astype(F32)
    small = two[:, block:].reshape(256, width).astype(F32)
    grad_recall = small[:head].reshape(head, heads, head).transpose(1, 0, 2)
    grad_admit = small[head : 2 * head].reshape(head, heads, head).transpose(1, 0, 2)
    lines = small[2 * head :]

    halo_grad = along(normed_grad[:HALO].astype(BF16), -1).astype(F32)
    inside = (place + 1) * count % LENGTH != 0
    normed_grad = normed_grad[HALO:]
    tail = normed_grad[count - HALO :] + jnp.where(inside, halo_grad, 0.0)
    normed_grad = jnp.concatenate([normed_grad[: count - HALO], tail])
    token_part, gain_one = norm_back(normed_grad, resid, norm_gain)
    grad_tokens = middle_grad + token_part
    gains = jnp.stack([gain_one, gain_two])
    rel = 1
    while rel < group:
        gains = gains + flip(gains, rel)
        rel *= 2
    rel = 1
    while rel < shards:
        gains = gains + lax.ppermute(gains, "chan", [(i, i ^ rel) for i in range(shards)])
        rel *= 2
    total_rows = count * group * shards
    return (
        block_out,
        grad_tokens,
        gains[0],
        grad_gate,
        grad_input,
        lines[:4],
        lines[4],
        grad_recall,
        lines[5].reshape(heads, head),
        grad_admit,
        lines[6].reshape(heads, head),
        lines[7] * STRENGTH * jax.nn.sigmoid(-decay_param),
        grad_out,
        gains[1],
        grads[0],
        grads[1],
        grads[2],
        lines[8] / total_rows,
    )


def solution(mesh):
    in_specs = (
        P(("seq", "chan"), None),
        P("seq"),
        P(("seq", "chan"), None),
        P(),
        P(None, "chan"),
        P(None, "chan"),
        P(None, "chan"),
        P("chan"),
        P("chan", None, None),
        P("chan", None),
        P("chan", None, None),
        P("chan", None),
        P("chan"),
        P("chan", None),
        P(),
        P(("seq", "chan"), None),
        P(("seq", "chan"), None),
        P(("seq", "chan"), None),
    )
    out_specs = (
        P(("seq", "chan"), None),
        P(("seq", "chan"), None),
        P(),
        P(None, "chan"),
        P(None, "chan"),
        P(None, "chan"),
        P("chan"),
        P("chan", None, None),
        P("chan", None),
        P("chan", None, None),
        P("chan", None),
        P("chan"),
        P("chan", None),
        P(),
        P(("seq", "chan"), None),
        P(("seq", "chan"), None),
        P(("seq", "chan"), None),
        P("chan"),
    )
    return jax.shard_map(
        on_device, mesh=mesh, in_specs=in_specs, out_specs=out_specs, check_vma=False
    )
```

```python
import functools

import jax
import jax.numpy as jnp
from jax import lax
from jax.experimental import pallas as pl
from jax.experimental.pallas import tpu as pltpu
from jax.sharding import PartitionSpec as P

LENGTH = 1024
EPS = 1e-06
STRENGTH = 8.0
HALO = 16
TABLE = 256
COST = 0.3
GELU_A = 0.7978845608028654
GELU_B = 0.044715
BF16 = jnp.bfloat16
F32 = jnp.float32
MIB = 1024 * 1024


def mm(left, right, left_dim, right_dim):
    return lax.dot_general(
        left, right, (((left_dim,), (right_dim,)), ((), ())), preferred_element_type=F32
    )


def gelu_parts(value):
    square = value * value
    th = jnp.tanh(GELU_A * value * (1.0 + GELU_B * square))
    half = 0.5 * (1.0 + th)
    slope = half + 0.5 * value * (1.0 - th * th) * (GELU_A * (1.0 + 3.0 * GELU_B * square))
    return value * half, slope


def gelu(value):
    th = jnp.tanh(GELU_A * value * (1.0 + GELU_B * value * value))
    return 0.5 * value * (1.0 + th)


def one_minus_exp(v):
    series = v * (
        1.0
        - v
        * (1 / 2)
        * (
            1.0
            - v
            * (1 / 3)
            * (1.0 - v * (1 / 4) * (1.0 - v * (1 / 5) * (1.0 - v * (1 / 6) * (1.0 - v * (1 / 7)))))
        )
    )
    return jnp.where(v < 0.4, series, 1.0 - jnp.exp(-v))


def rows_index(shape):
    return lax.broadcasted_iota(jnp.int32, shape, 0)


def scan_down(a, b):
    count = a.shape[0]
    index = rows_index(a.shape)
    step = 1
    while step < count:
        if step < 8:
            inside = index >= step
            a_prev = jnp.where(inside, pltpu.roll(a, step, 0), 1.0)
            b_prev = jnp.where(inside, pltpu.roll(b, step, 0), 0.0)
        else:
            a_prev = jnp.concatenate([jnp.ones_like(a[:step]), a[: count - step]], axis=0)
            b_prev = jnp.concatenate([jnp.zeros_like(b[:step]), b[: count - step]], axis=0)
        b = b + a * b_prev
        a = a * a_prev
        step *= 2
    return a, b


def scan_up(a, b):
    count = a.shape[0]
    index = rows_index(a.shape)
    step = 1
    while step < count:
        if step < 8:
            inside = index < count - step
            a_next = jnp.where(inside, pltpu.roll(a, count - step, 0), 1.0)
            b_next = jnp.where(inside, pltpu.roll(b, count - step, 0), 0.0)
        else:
            a_next = jnp.concatenate([a[step:], jnp.ones_like(a[:step])], axis=0)
            b_next = jnp.concatenate([b[step:], jnp.zeros_like(b[:step])], axis=0)
        b = b + a * b_next
        a = a * a_next
        step *= 2
    return a, b


def block_diagonal(flat, head, dtype):
    width = flat.shape[1]
    tall = jnp.concatenate([flat] * (width // head), axis=0)
    shape = (width, width)
    row = lax.broadcasted_iota(jnp.int32, shape, 0) // head
    col = lax.broadcasted_iota(jnp.int32, shape, 1) // head
    return jnp.where(row == col, tall, 0.0).astype(dtype)


def fold_diagonal(square, head):
    width = square.shape[0]
    row = lax.broadcasted_iota(jnp.int32, square.shape, 0) // head
    col = lax.broadcasted_iota(jnp.int32, square.shape, 1) // head
    kept = jnp.where(row == col, square, 0.0)
    total = kept[:head]
    for start in range(head, width, head):
        total = total + kept[start : start + head]
    return total


def vmem():
    return pl.BlockSpec(memory_space=pltpu.VMEM)


def smem():
    return pl.BlockSpec(memory_space=pltpu.SMEM)


def launch(
    kernel,
    inputs,
    in_specs,
    micros,
    after=(),
    carry=(),
    prefetch=0,
    grid=(),
    out_shape=(),
    out_specs=(),
    scratch_shapes=(),
    aliases=None,
    name=None,
    vmem_mib=60,
):
    count, extra, through = len(inputs), len(after), len(carry)
    made = len(out_shape)
    aliases = dict(aliases or {})
    for i in range(through):
        aliases[count + extra + i] = made + i

    def body(*refs):
        first = count + extra + through
        kernel(*refs[:count], *refs[first : first + made], *refs[first + made + through :])

    anywhere = pl.BlockSpec(memory_space=pl.ANY)
    return pl.pallas_call(
        body,
        out_shape=list(out_shape) + [jax.ShapeDtypeStruct(c.shape, c.dtype) for c in carry],
        grid_spec=pltpu.PrefetchScalarGridSpec(
            num_scalar_prefetch=prefetch,
            grid=grid,
            in_specs=list(in_specs) + [anywhere] * (extra + through),
            out_specs=list(out_specs) + [anywhere] * through,
            scratch_shapes=scratch_shapes,
        ),
        input_output_aliases=aliases,
        compiler_params=pltpu.CompilerParams(vmem_limit_bytes=vmem_mib * MIB),
        cost_estimate=pl.CostEstimate(
            flops=int(micros * 1.1e9 * COST), bytes_accessed=int(micros * 3.5e6 * COST), transcendentals=0
        ),
        name=name,
    )(*inputs, *after, *carry)


def split_features(core, source, own_out, other_out):
    half = own_out.shape[1]
    block = 128
    quads = half // block
    for quad in range(quads):
        for out, who in ((own_out, core), (other_out, 1 - core)):
            start = pl.multiple_of((quad * 2 + who) * block, block)
            out[:, quad * block : (quad + 1) * block] = source[:, pl.ds(start, block)]


def pack_kernel(*refs):
    *pieces, out = refs
    for i, ref in enumerate(pieces):
        out[i] = ref[0]


def pack(pieces, carry, after):
    return launch(
        pack_kernel,
        pieces,
        [vmem()] * len(pieces),
        0.1,
        after,
        carry,
        out_shape=[jax.ShapeDtypeStruct((len(pieces),) + pieces[0].shape[1:], pieces[0].dtype)],
        out_specs=[vmem()],
        name="pack",
        vmem_mib=8,
    )


def fence(carry, after=()):
    return launch(lambda *refs: None, [], [], 0.01, after, carry, name="fence", vmem_mib=1)


def prepare_kernel(
    slots_ref,
    gate_ref,
    input_ref,
    out_ref,
    recall_ref,
    recall_bias_ref,
    admit_ref,
    admit_bias_ref,
    taps_ref,
    bias_ref,
    decay_ref,
    weights,
    table_out,
    pieces_out,
    table,
):
    weights[0] = gate_ref[...]
    weights[1] = input_ref[...]
    weights[2] = out_ref[...].T
    heads, head, _ = recall_ref.shape
    for h in range(heads):
        cols = slice(h * head, (h + 1) * head)
        table[:head, cols] = recall_ref[h]
        table[head : 2 * head, cols] = admit_ref[h]
    side = jnp.concatenate
    lines = side(
        [
            taps_ref[...],
            bias_ref[...].reshape(1, -1),
            side([recall_bias_ref[h : h + 1] for h in range(heads)], axis=1),
            side([admit_bias_ref[h : h + 1] for h in range(heads)], axis=1),
            jax.nn.softplus(-decay_ref[...].reshape(1, -1)),
        ],
        axis=0,
    )
    high = lines.astype(BF16).astype(F32)
    rest = lines - high
    mid = rest.astype(BF16).astype(F32)
    table[2 * head : 2 * head + 8] = high
    table[2 * head + 8 : 2 * head + 16] = mid
    table[2 * head + 16 : 2 * head + 24] = rest - mid
    table[2 * head + 24 :] = jnp.zeros((table.shape[0] - 2 * head - 24, table.shape[1]), F32)
    table_out[...] = table[...].astype(BF16)
    count, rows, _ = pieces_out.shape
    block = pieces_block(weights.shape[1], rows)
    extra = rows - 3 * block
    for k in range(count):
        start = pl.multiple_of(slots_ref[k] * block, block)
        for part in range(3):
            pieces_out[k, part * block : (part + 1) * block] = weights[part, pl.ds(start, block), :]
        start = pl.multiple_of(slots_ref[k] * extra, extra)
        pieces_out[k, 3 * block :] = table_out[pl.ds(start, extra), :]

def norm_kernel(core_ref, ends_ref, tokens_ref, gain_ref, normed_out, *halves_out):
    for ref, rows in ((ends_ref, slice(0, HALO)), (tokens_ref, slice(HALO, None))):
        values = ref[...].astype(F32)
        scale = lax.rsqrt(jnp.mean(values * values, axis=1, keepdims=True) + EPS)
        normed_out[rows] = (values * scale * gain_ref[...]).astype(BF16)
    if halves_out:
        split_features(core_ref[0], normed_out, *halves_out)


def norm(core, ends, tokens, gain, group):
    count, model = tokens.shape
    halves = half_shapes(HALO + count, model, group)
    return launch(
        norm_kernel,
        [core, ends, tokens, gain.reshape(1, model)],
        [smem()] + [vmem()] * 3,
        0.1,
        out_shape=[jax.ShapeDtypeStruct((HALO + count, model), BF16)] + halves,
        out_specs=[vmem()] * (1 + len(halves)),
        name="norm",
        vmem_mib=16,
    )


def pieces_block(model, rows):
    return rows * model // (3 * model + TABLE)


def half_shapes(rows, model, group):
    return [jax.ShapeDtypeStruct((rows, model // 2), BF16)] * (2 if model // group == 128 else 0)


def prepare(slots, gate, inputs, out, recall, recall_bias, admit, admit_bias, taps, bias, decay, group):
    model, width = gate.shape
    rows = (3 * model + TABLE) // group
    return launch(
        prepare_kernel,
        [slots, gate, inputs, out, recall, recall_bias, admit, admit_bias, taps, bias, decay],
        [smem()] + [vmem()] * 10,
        0.1,
        out_shape=[
            jax.ShapeDtypeStruct((3, model, width), BF16),
            jax.ShapeDtypeStruct((TABLE, width), BF16),
            jax.ShapeDtypeStruct((slots.shape[0], rows, width), BF16),
        ],
        out_specs=[vmem()] * 3,
        scratch_shapes=[pltpu.VMEM((TABLE, width), F32)],
        name="prepare",
    )


def mix_local_kernel(own, head, counts, stacked, slots_ref, normed_ref, mask_ref, *rest):
    piece_refs, rest = rest[: len(counts)], rest[len(counts) :]
    weights, inputs_out, gated_out, kept_out, scan_out, edge_out, gates_out, vec_out = rest[
        stacked : stacked + 8
    ]
    (table,) = rest[stacked + 8 :]
    model = normed_ref.shape[1]
    if own:
        weights[0] = piece_refs[0][...]
        table[...] = piece_refs[1][...].astype(F32)
    else:
        number = 0
        for ref, many in zip(piece_refs, counts, strict=True):
            rows = ref.shape[1]
            block = pieces_block(model, rows)
            extra = rows - 3 * block
            for k in range(many):
                slot = slots_ref[number]
                number += 1
                start = pl.multiple_of(slot * block, block)
                for part in range(3):
                    weights[0, part, pl.ds(start, block), :] = ref[
                        k, part * block : (part + 1) * block
                    ]
                start = pl.multiple_of(slot * extra, extra)
                table[pl.ds(start, extra), :] = ref[k, 3 * block :].astype(F32)
    count = mask_ref.shape[0]
    vec = table[2 * head : 2 * head + 8] + (
        table[2 * head + 8 : 2 * head + 16] + table[2 * head + 16 : 2 * head + 24]
    )
    vec_out[0] = vec
    gates_out[0] = table[: 2 * head].astype(BF16)
    gated = mm(normed_ref[HALO:], weights[0, 0], 1, 0).astype(BF16)
    gated_out[0] = gated
    inputs = mm(normed_ref[...], weights[0, 1], 1, 0).astype(BF16)
    inputs_out[0] = inputs
    wide = inputs.astype(F32)
    conv = vec[4:5] + vec[0:1] * wide[HALO:]
    for shift in range(1, 4):
        moved = pltpu.roll(wide, shift, 0)[HALO:]
        conv = conv + vec[shift : shift + 1] * (moved * mask_ref[:, shift : shift + 1])
    low = conv.astype(BF16)
    recall_weight = block_diagonal(table[:head], head, BF16)
    admit_weight = block_diagonal(table[head : 2 * head], head, BF16)
    recall = jax.nn.sigmoid(mm(low, recall_weight, 1, 0) + vec[5:6])
    admit = jax.nn.sigmoid(mm(low, admit_weight, 1, 0) + vec[6:7])
    rate = STRENGTH * recall * vec[7:8]
    decay = jnp.exp(-rate)
    inject = jnp.sqrt(one_minus_exp(2.0 * rate)) * admit * conv
    product, state = scan_down(decay * mask_ref[:, 1:2], inject)
    kept_out[0, 0] = conv
    kept_out[0, 1] = recall
    kept_out[0, 2] = admit
    scan_out[0, 0] = product
    scan_out[0, 1] = state
    edge_out[0, 0:1] = product[count - 1 :]
    edge_out[0, 1:2] = state[count - 1 :]
    edge_out[0, 2:3] = jnp.sum(decay, axis=0, keepdims=True)


def mix_local(shard, shards, head, slots, normed, mask, pieces, stacks, after=(), carry=()):
    count = mask.shape[0]
    model = normed.shape[1]
    width = pieces[0].shape[-1]
    own = shard == 0
    counts = [p.shape[0] for p in pieces]
    shapes = [
        ((shards, 3, model, width), BF16),
        ((shards, count + HALO, width), BF16),
        ((shards, count, width), BF16),
        ((shards, 3, count, width), F32),
        ((shards, 2, count, width), F32),
        ((shards, 8, width), F32),
        ((shards, 2 * head, width), BF16),
        ((shards, 8, width), F32),
    ]

    def at(shape):
        tail = (0,) * (len(shape) - 1)
        return pl.BlockSpec((1,) + shape[1:], lambda i: (shard,) + tail)

    first = [slots, normed, mask, *pieces]
    in_specs = [smem()] + [vmem()] * (len(first) - 1)
    aliases = {}
    if stacks is not None:
        aliases = {len(first) + i: i for i in range(len(stacks))}
        in_specs += [pl.BlockSpec(memory_space=pl.ANY)] * len(stacks)
        first += list(stacks)
    outs = launch(
        functools.partial(mix_local_kernel, own, head, counts, len(aliases)),
        first,
        in_specs,
        5.7,
        after=after,
        carry=carry,
        grid=(1,),
        out_shape=[jax.ShapeDtypeStruct(shape, dtype) for shape, dtype in shapes],
        out_specs=[at(shape) for shape, _ in shapes],
        scratch_shapes=[pltpu.VMEM((TABLE, width), F32)],
        aliases=aliases,
        name="mix_local",
    )
    return outs[:8], outs[8:]


def carried(edges):
    total = edges[-1][0, 1:2]
    for edge in edges[-2::-1]:
        total = edge[0, 1:2] + edge[0, 0:1] * total
    return total


def branch_kernel(
    depth, scan_ref, gated_ref, weight_ref, resid_ref, gain_ref, *rest
):
    edges = rest[:depth]
    carry_out, branch_in_out, middle_out, second_out, again_out, acc = rest[depth:]
    step = pl.program_id(0)

    @pl.when(step == 0)
    def _():
        acc[...] = resid_ref[...].astype(F32)

    carry = carried(edges)
    carry_out[0] = jnp.broadcast_to(carry, carry_out.shape[1:])
    state = scan_ref[0, 1] + scan_ref[0, 0] * carry
    mixed = (gelu(gated_ref[0].astype(F32)) * state).astype(BF16)
    branch_in_out[0] = mixed
    acc[...] += mm(mixed, weight_ref[0, 0], 1, 1)

    @pl.when(step == pl.num_programs(0) - 1)
    def _():
        middle = acc[...]
        middle_out[...] = middle
        scale = lax.rsqrt(jnp.mean(middle * middle, axis=1, keepdims=True) + EPS)
        second = (middle * scale * gain_ref[...]).astype(BF16)
        second_out[...] = second
        again_out[...] = second


def branch(scan, gated, weights, tokens, gain, edges, after):
    shards, _, count, width = scan.shape
    model = tokens.shape[1]

    def edge_spec(shift):
        return pl.BlockSpec((1, 8, width), lambda s: ((s + shards - shift % shards) % shards, 0, 0))

    return launch(
        functools.partial(branch_kernel, len(edges)),
        [scan, gated, weights, tokens, gain, *edges],
        [
            pl.BlockSpec((1, 2, count, width), lambda s: (s, 0, 0, 0)),
            pl.BlockSpec((1, count, width), lambda s: (s, 0, 0)),
            pl.BlockSpec((1, 1, model, width), lambda s: (s, 2, 0, 0)),
            pl.BlockSpec((count, model), lambda s: (0, 0)),
            pl.BlockSpec((1, model), lambda s: (0, 0)),
        ]
        + [edge_spec(i + 1) for i in range(len(edges))],
        0.1,
        after,
        grid=(shards,),
        out_shape=[
            jax.ShapeDtypeStruct((shards, 8, width), F32),
            jax.ShapeDtypeStruct((shards, count, width), BF16),
            jax.ShapeDtypeStruct((count, model), F32),
            jax.ShapeDtypeStruct((count, model), BF16),
            jax.ShapeDtypeStruct((count, model), BF16),
        ],
        out_specs=[
            pl.BlockSpec((1, 8, width), lambda s: (s, 0, 0)),
            pl.BlockSpec((1, count, width), lambda s: (s, 0, 0)),
            pl.BlockSpec((count, model), lambda s: (0, 0)),
            pl.BlockSpec((count, model), lambda s: (0, 0)),
            pl.BlockSpec((count, model), lambda s: (0, 0)),
        ],
        scratch_shapes=[pltpu.VMEM((count, model), F32)],
        name="mix_branch",
    )


def arrange_kernel(core_ref, own_ref, other_ref, out_ref):
    shards, quads, _, piece, _ = own_ref.shape
    for ref, core in ((own_ref, core_ref[0]), (other_ref, 1 - core_ref[0])):
        for shard in range(shards):
            for quad in range(quads):
                start = pl.multiple_of(((quad * 2 + core) * shards + shard) * piece, piece)
                for part in range(3):
                    out_ref[part, pl.ds(start, piece), :] = ref[shard, quad, part]


def arrange(core, own, other, after):
    shards, quads, _, piece, width = own.shape
    if piece % 16:
        both = jnp.where(core[0] == 0, jnp.stack([own, other]), jnp.stack([other, own]))
        return both.transpose(3, 2, 0, 1, 4, 5).reshape(3, 2 * shards * quads * piece, width)
    return launch(
        arrange_kernel,
        [core, own, other],
        [smem(), vmem(), vmem()],
        0.1,
        after,
        out_shape=[jax.ShapeDtypeStruct((3, 2 * shards * quads * piece, width), BF16)],
        out_specs=[vmem()],
        name="mlp_arrange",
        vmem_mib=16,
    )[0]


def mlp_tiles(width):
    tile = 256 if width % 256 == 0 else width
    return [slice(start, start + tile) for start in range(0, width, tile)]


def mlp_kernel(
    second_ref,
    cot_ref,
    weight_ref,
    gate_grad_out,
    up_grad_out,
    hidden_out,
    back_out,
):
    second = second_ref[...]
    cot = cot_ref[...]
    total = None
    for cols in mlp_tiles(weight_ref.shape[2]):
        gate_weight, up_weight = weight_ref[0, :, cols], weight_ref[1, :, cols]
        gate = mm(second, gate_weight, 1, 0)
        upward = mm(second, up_weight, 1, 0)
        hidden_grad = mm(cot, weight_ref[2, :, cols], 1, 0)
        act, slope = gelu_parts(gate)
        hidden_out[:, cols] = (act * upward).astype(BF16)
        gate_grad = (hidden_grad * upward * slope).astype(BF16)
        up_grad = (hidden_grad * act).astype(BF16)
        gate_grad_out[:, cols] = gate_grad
        up_grad_out[:, cols] = up_grad
        back = mm(gate_grad, gate_weight, 1, 1) + mm(up_grad, up_weight, 1, 1)
        total = back if total is None else total + back
    back_out[...] = total.astype(BF16)


def mlp_block(second, cot, weights, after, carry):
    count, model = second.shape
    width = weights.shape[-1]
    wide = jax.ShapeDtypeStruct((count, width), BF16)
    return launch(
        mlp_kernel,
        [second, cot, weights],
        [vmem()] * 3,
        7.4,
        after,
        carry,
        out_shape=[wide, wide, wide, jax.ShapeDtypeStruct((count, model), BF16)],
        out_specs=[vmem()] * 4,
        name="mlp_block",
        vmem_mib=16,
    )


def mlp_grads_kernel(quads, quad_ref, core_ref, weight_ref, *rest):
    cots, rest = rest[:quads], rest[quads:]
    seconds, rest = rest[:quads], rest[quads:]
    gate_grads, rest = rest[:quads], rest[quads:]
    up_grads, rest = rest[:quads], rest[quads:]
    hiddens, rest = rest[:quads], rest[quads:]
    *grads_out, results_out, second, cot, left, whole_ref = rest
    count = seconds[0].shape[0]
    rows = [slice(rel * count, (rel + 1) * count) for rel in range(quads)]
    for rel in range(quads):
        second[rows[rel]] = seconds[rel][...]
        cot[rows[rel]] = cots[rel][...]
    total = None
    for cols in mlp_tiles(weight_ref.shape[2]):
        for part, (base, group) in enumerate(
            ((second, gate_grads), (second, up_grads), (cot, hiddens))
        ):
            for rel in range(quads):
                left[rows[rel]] = group[rel][:, cols]
            whole = mm(base[...], left[...], 0, 0).astype(BF16)
            if len(grads_out) == 1:
                grads_out[0][part, :, cols] = whole
                continue
            whole_ref[...] = whole
            shards, _, _, piece, _ = grads_out[0].shape
            for out, core in zip(grads_out, (core_ref[0], 1 - core_ref[0]), strict=True):
                for shard in range(shards):
                    for quad in range(quads):
                        start = pl.multiple_of(((quad * 2 + core) * shards + shard) * piece, piece)
                        out[shard, quad, part, :, cols] = whole_ref[pl.ds(start, piece), :]
        result = mm(left[...], weight_ref[2, :, cols], 1, 1)
        total = result if total is None else total + result
    for rel in range(quads):
        results_out[quad_ref[0] ^ rel] = total[rows[rel]].astype(BF16)


def mlp_grads(quad, core, weights, cots, seconds, gate_grads, up_grads, hiddens, shards):
    quads = len(seconds)
    count, model = seconds[0].shape
    width = weights.shape[2]
    tile = mlp_tiles(width)[0].stop
    piece = model // (quads * 2 * shards)
    shapes = [(shards, quads, 3, piece, width)] * 2 if piece % 16 == 0 else [(3, model, width)]
    *grads, results = launch(
        functools.partial(mlp_grads_kernel, quads),
        [quad, core, weights, *cots, *seconds, *gate_grads, *up_grads, *hiddens],
        [smem()] * 2 + [vmem()] * (1 + 5 * quads),
        15.0,
        out_shape=[jax.ShapeDtypeStruct(shape, BF16) for shape in shapes]
        + [jax.ShapeDtypeStruct((quads, count, model), BF16)],
        out_specs=[vmem()] * (1 + len(shapes)),
        scratch_shapes=[
            pltpu.VMEM((quads * count, model), BF16),
            pltpu.VMEM((quads * count, model), BF16),
            pltpu.VMEM((quads * count, tile), BF16),
            pltpu.VMEM((model, tile), BF16),
        ],
        name="mlp_grads",
        vmem_mib=32,
    )
    if piece % 16:
        both = grads[0].reshape(3, quads, 2, shards, piece, width).transpose(2, 3, 1, 0, 4, 5)
        grads = [lax.dynamic_index_in_dim(both, who, 0, False) for who in (core[0], 1 - core[0])]
    return *grads, results


def add_kernel(a_ref, b_ref, out_ref):
    out_ref[...] = (a_ref[...].astype(F32) + b_ref[...].astype(F32)).astype(BF16)


def add_pair(a, b, after=()):
    return launch(
        add_kernel,
        [a, b],
        [vmem()] * 2,
        0.1,
        after,
        out_shape=[jax.ShapeDtypeStruct(a.shape, BF16)],
        out_specs=[vmem()],
        name="add_pair",
        vmem_mib=16,
    )[0]


def middle_kernel(blocks, back_ref, *rest):
    (*backs, values_ref, cot_ref, gain_ref, core_ref), outs = rest[: blocks + 3], rest[blocks + 3 :]
    middle_grad_out, low_out, gain_out, *halves_out = outs
    grad = back_ref[...].astype(F32)
    for ref in backs:
        grad = grad + ref[...].astype(F32)
    values = values_ref[...]
    scale = lax.rsqrt(jnp.mean(values * values, axis=1, keepdims=True) + EPS)
    scaled = grad * gain_ref[...]
    inner = jnp.mean(scaled * values, axis=1, keepdims=True)
    total = cot_ref[...].astype(F32) + scale * scaled - values * (scale * scale * scale * inner)
    middle_grad_out[...] = total
    low_out[...] = total.astype(BF16)
    if halves_out:
        split_features(core_ref[0], low_out, *halves_out)
    gain_out[...] = jnp.sum(grad * values * scale, axis=0, keepdims=True)


def middle_back(backs, values, cot, gain, core, group, after, carry):
    count, model = values.shape
    halves = half_shapes(count, model, group)
    return launch(
        functools.partial(middle_kernel, len(backs)),
        [*backs, values, cot, gain.reshape(1, model), core],
        [vmem()] * (len(backs) + 3) + [smem()],
        0.1,
        after,
        carry,
        out_shape=[
            jax.ShapeDtypeStruct((count, model), F32),
            jax.ShapeDtypeStruct((count, model), BF16),
            jax.ShapeDtypeStruct((1, model), F32),
        ]
        + halves,
        out_specs=[vmem()] * (3 + len(halves)),
        name="middle_back",
        vmem_mib=16,
    )


def tokens_kernel(
    inside_ref, grad_ref, halo_ref, tokens_ref, gain_ref, middle_grad_ref, gain_two_ref, out, lines_out
):
    grad = grad_ref[HALO:]
    count = grad.shape[0]
    last = jnp.where(inside_ref[0] > 0, halo_ref[...].astype(F32), 0.0)
    grad = jnp.concatenate([grad[: count - HALO], grad[count - HALO :] + last], axis=0)
    values = tokens_ref[...].astype(F32)
    scale = lax.rsqrt(jnp.mean(values * values, axis=1, keepdims=True) + EPS)
    scaled = grad * gain_ref[...]
    inner = jnp.mean(scaled * values, axis=1, keepdims=True)
    out[...] = middle_grad_ref[...] + scale * scaled - values * (scale * scale * scale * inner)
    both = (jnp.sum(grad * values * scale, axis=0, keepdims=True), gain_two_ref[...])
    lines_out[...] = pack_gains(both, lines_out.shape[1])


def gain_chunk(model, width):
    chunk = 128
    while chunk * 2 <= width:
        chunk *= 2
    while chunk > width:
        chunk //= 2
    return chunk


def gain_lines(model, width):
    return 4 * (model // gain_chunk(model, width))


def pack_gains(both, width):
    chunk = gain_chunk(both[0].shape[1], width)
    lines = []
    for value in both:
        high = value.astype(BF16).astype(F32)
        for term in (high, value - high):
            lines += [term[:, i : i + chunk] for i in range(0, term.shape[1], chunk)]
    lines = jnp.concatenate(lines, axis=0)
    if chunk < width:
        blank = jnp.zeros((lines.shape[0], width - chunk), F32)
        lines = jnp.concatenate([lines, blank], axis=1)
    return lines.astype(BF16)


def unpack_gains(lines, model):
    chunk = gain_chunk(model, lines.shape[1])
    many = model // chunk
    lines = lines.astype(F32)
    both = []
    for i in range(2):
        value = lines[2 * i * many : (2 * i + 1) * many] + lines[
            (2 * i + 1) * many : (2 * i + 2) * many
        ]
        both.append(
            jnp.concatenate([value[j : j + 1, :chunk] for j in range(many)], axis=1)
        )
    return both


def tokens_back(inside, grad, halo, tokens, gain, middle_grad, gain_two, width):
    count, model = tokens.shape
    return launch(
        tokens_kernel,
        [inside, grad, halo, tokens, gain.reshape(1, model), middle_grad, gain_two],
        [smem()] + [vmem()] * 6,
        0.1,
        out_shape=[
            jax.ShapeDtypeStruct((count, model), F32),
            jax.ShapeDtypeStruct((gain_lines(model, width), width), BF16),
        ],
        out_specs=[vmem()] * 2,
        name="tokens_back",
        vmem_mib=16,
    )


def adjoint_kernel(
    grad_ref,
    weight_ref,
    gated_ref,
    scan_ref,
    kept_ref,
    carry_ref,
    mask_ref,
    vec_ref,
    gate_back_out,
    adjoint_out,
    edge_out,
):
    into = mm(grad_ref[...], weight_ref[0, 0], 1, 0).astype(BF16).astype(F32)
    act, slope = gelu_parts(gated_ref[0].astype(F32))
    state = scan_ref[0, 1] + scan_ref[0, 0] * carry_ref[0, 0:1]
    gate_back_out[0] = (into * state * slope).astype(BF16)
    decay = jnp.exp(-STRENGTH * kept_ref[0, 0] * vec_ref[0, 7:8]) * mask_ref[:, 1:2]
    count = decay.shape[0]
    shifted = jnp.where(
        rows_index(decay.shape) < count - 1, pltpu.roll(decay, count - 1, 0), 1.0
    )
    product, value = scan_up(shifted, into * act)
    adjoint_out[0, 0] = product
    adjoint_out[0, 1] = value
    edge_out[0] = jnp.broadcast_to(decay[0:1] * value[0:1], edge_out.shape[1:])


def adjoint(grad, weights, gated, scan, kept, carry, mask, vec, through):
    shards, _, count, width = scan.shape
    model = grad.shape[1]

    def flat(*shape):
        return pl.BlockSpec(shape, lambda s: (0,) * len(shape))

    def at(*shape):
        return pl.BlockSpec((1,) + shape, lambda s: (s,) + (0,) * len(shape))

    return launch(
        adjoint_kernel,
        [grad, weights, gated, scan, kept, carry, mask, vec],
        [
            flat(count, model),
            pl.BlockSpec((1, 1, model, width), lambda s: (s, 2, 0, 0)),
            at(count, width),
            at(2, count, width),
            pl.BlockSpec((1, 1, count, width), lambda s: (s, 1, 0, 0)),
            at(8, width),
            flat(*mask.shape),
            at(8, width),
        ],
        0.1,
        carry=through,
        grid=(shards,),
        out_shape=[
            jax.ShapeDtypeStruct((shards, count, width), BF16),
            jax.ShapeDtypeStruct((shards, 2, count, width), F32),
            jax.ShapeDtypeStruct((shards, 8, width), F32),
        ],
        out_specs=[at(count, width), at(2, count, width), at(8, width)],
        name="mix_adjoint",
    )


def outer_kernel(groups, core_ref, *rest):
    pairs, rest = rest[: 4 * groups], rest[4 * groups :]
    *smalls, out, left, right, small = rest
    count = pairs[0].shape[0]
    quads, shards = out.shape[:2]
    block = left.shape[1] // quads
    for group in range(groups):
        left_ref, left_other, right_ref, right_other = pairs[4 * group : 4 * group + 4]
        left[:count] = left_ref[...]
        left[count:] = left_other[...]
        for s in range(shards):
            right[:count] = right_ref[s]
            right[count:] = right_other[s]
            total = mm(left[...], right[...], 0, 0).astype(BF16)
            for quad in range(quads):
                out[quad, s, group * block : (group + 1) * block] = total[
                    quad * block : (quad + 1) * block
                ]
    if smalls:
        extra = out.shape[2] - groups * block
        for s in range(shards):
            small[...] = (smalls[0][s].astype(F32) + smalls[1][s].astype(F32)).astype(BF16)
            for quad in range(quads):
                start = pl.multiple_of((quad * 2 + core_ref[0]) * extra, extra)
                out[quad, s, groups * block :] = small[pl.ds(start, extra), :]


def outer(core, quads, pairs, smalls=(), after=(), carry=()):
    shards, count, width = pairs[2].shape
    model = pairs[0].shape[1]
    groups = len(pairs) // 4
    rows = groups * model // quads + (TABLE // (2 * quads) if smalls else 0)
    return launch(
        functools.partial(outer_kernel, groups),
        [core, *pairs, *smalls],
        [smem()] + [vmem()] * (len(pairs) + len(smalls)),
        0.1,
        after,
        carry,
        out_shape=[jax.ShapeDtypeStruct((quads, shards, rows, width), BF16)],
        out_specs=[vmem()],
        scratch_shapes=[
            pltpu.VMEM((2 * count, model), BF16),
            pltpu.VMEM((2 * count, width), BF16),
            pltpu.VMEM((TABLE, width), BF16),
        ],
        name="mix_outer",
        vmem_mib=16,
    )


def mix_back_kernel(
    head,
    depth,
    gate_weight_ref,
    input_weight_ref,
    inputs_ref,
    gate_back_ref,
    kept_ref,
    scan_ref,
    adjoint_ref,
    carry_ref,
    mask_ref,
    gates_ref,
    vec_ref,
    edge_ref,
    *rest,
):
    backs, decays = rest[:depth], rest[depth : 2 * depth - 1]
    input_back_out, small_out, normed_grad_out, acc = rest[2 * depth - 1 :]
    step = pl.program_id(0)
    count = mask_ref.shape[0]
    width = vec_ref.shape[2]
    vec = vec_ref[0]
    incoming = backs[-1][0, 0:1]
    for back, edge in zip(backs[-2::-1], decays[::-1], strict=True):
        incoming = back[0, 0:1] + edge[0, 0:1] * incoming
    adj = adjoint_ref[0, 1] + adjoint_ref[0, 0] * incoming
    carry = carry_ref[0, 0:1]
    state = scan_ref[0, 1] + scan_ref[0, 0] * carry
    before = jnp.where(rows_index(state.shape) == 0, carry, pltpu.roll(state, 1, 0))
    conv, recall, admit = kept_ref[0, 0], kept_ref[0, 1], kept_ref[0, 2]
    speed = STRENGTH * vec[7:8]
    rate = recall * speed
    decay = jnp.exp(-rate)
    size = jnp.sqrt(one_minus_exp(2.0 * rate))
    sized = adj * size
    pulled = adj * admit
    log_grad = decay * (adj * before * mask_ref[:, 1:2] - pulled * conv * decay / size)
    recall_grad = -speed * log_grad * recall * (1.0 - recall)
    admit_grad = sized * conv * admit * (1.0 - admit)
    conv_grad = sized * admit
    recall_low = recall_grad.astype(BF16)
    admit_low = admit_grad.astype(BF16)
    gates = gates_ref[0].astype(F32)
    recall_weight = block_diagonal(gates[:head], head, BF16)
    admit_weight = block_diagonal(gates[head:], head, BF16)
    conv_grad = conv_grad + mm(recall_low, recall_weight, 1, 1) + mm(admit_low, admit_weight, 1, 1)
    wide = inputs_ref[0].astype(F32)
    blank = jnp.zeros((HALO, width), F32)
    reach = jnp.concatenate([blank, vec[0:1] * conv_grad], axis=0)
    tap_grads = [jnp.sum(conv_grad * wide[HALO:], axis=0, keepdims=True)]
    for shift in range(1, 4):
        masked = conv_grad * mask_ref[:, shift : shift + 1]
        moved = pltpu.roll(wide, shift, 0)[HALO:]
        tap_grads.append(jnp.sum(masked * moved, axis=0, keepdims=True))
        back = jnp.concatenate([blank, vec[shift : shift + 1] * masked], axis=0)
        reach = reach + pltpu.roll(back, count + HALO - shift, 0)
    input_back = reach.astype(BF16)
    conv_low = conv.astype(BF16)
    input_back_out[0] = input_back
    small_out[0, :head] = fold_diagonal(mm(conv_low, recall_low, 0, 0), head).astype(BF16)
    small_out[0, head : 2 * head] = fold_diagonal(mm(conv_low, admit_low, 0, 0), head).astype(BF16)
    rows = tap_grads + [
        jnp.sum(conv_grad, axis=0, keepdims=True),
        jnp.sum(recall_grad, axis=0, keepdims=True),
        jnp.sum(admit_grad, axis=0, keepdims=True),
        jnp.sum(recall * log_grad, axis=0, keepdims=True),
        edge_ref[0, 2:3],
    ]
    rows.append(jnp.zeros((TABLE - 2 * head - len(rows), width), F32))
    small_out[0, 2 * head :] = jnp.concatenate(rows, axis=0).astype(BF16)
    through_gate = mm(gate_back_ref[0], gate_weight_ref[0, 0], 1, 1)
    through_input = mm(input_back, input_weight_ref[0, 0], 1, 1)

    @pl.when(step == 0)
    def _():
        acc[...] = through_input

    @pl.when(step > 0)
    def _():
        acc[...] += through_input

    acc[HALO:] += through_gate

    @pl.when(step == pl.num_programs(0) - 1)
    def _():
        normed_grad_out[...] = acc[...]


def mix_back(
    weights, inputs, gate_back, kept, scan, adj, carry, mask, gates, vec, edge, backs, ahead, after
):
    shards, _, count, width = scan.shape
    model = weights.shape[2]
    head = gates.shape[1] // 2
    depth = len(backs)

    def flat(*shape):
        return pl.BlockSpec(shape, lambda s: (0,) * len(shape))

    def at(*shape):
        return pl.BlockSpec((1,) + shape, lambda s: (s,) + (0,) * len(shape))

    def ahead_spec(shift):
        return pl.BlockSpec((1, 8, width), lambda s: ((s + shift) % shards, 0, 0))

    return launch(
        functools.partial(mix_back_kernel, head, depth),
        [
            weights, weights, inputs, gate_back, kept, scan, adj, carry, mask, gates, vec,
            edge, *backs, *ahead,
        ],
        [
            pl.BlockSpec((1, 1, model, width), lambda s: (s, 0, 0, 0)),
            pl.BlockSpec((1, 1, model, width), lambda s: (s, 1, 0, 0)),
            at(count + HALO, width),
            at(count, width),
            at(3, count, width),
            at(2, count, width),
            at(2, count, width),
            at(8, width),
            flat(*mask.shape),
            at(2 * head, width),
            at(8, width),
            at(8, width),
        ]
        + [ahead_spec(i + 1) for i in range(depth)]
        + [ahead_spec(i + 1) for i in range(depth - 1)],
        0.1,
        after,
        grid=(shards,),
        out_shape=[
            jax.ShapeDtypeStruct((shards, count + HALO, width), BF16),
            jax.ShapeDtypeStruct((shards, TABLE, width), BF16),
            jax.ShapeDtypeStruct((count + HALO, model), F32),
        ],
        out_specs=[at(count + HALO, width), at(TABLE, width), flat(count + HALO, model)],
        scratch_shapes=[pltpu.VMEM((count + HALO, model), F32)],
        name="mix_back",
    )


def home_kernel(groups, shards, place_ref, *rest):
    parts, (out, lines) = rest[: groups * shards], rest[groups * shards :]
    start = 0
    for group in range(groups):
        refs = parts[group * shards : (group + 1) * shards]
        size = refs[0].shape[0]
        if group == groups - 1:
            size -= lines.shape[1]
        total = refs[0][:size].astype(F32)
        for ref in refs[1:]:
            total = total + ref[:size].astype(F32)
        out[start : start + size] = total.astype(BF16)
        start += size
    for s in range(shards):
        lines[s] = refs[s][size:].astype(F32)
    model = lines.shape[1] // 4 * gain_chunk(0, lines.shape[2])
    total = None
    for owner in range(shards):
        which = lax.rem(owner - place_ref[0] + shards, shards)
        value = unpack_gains(lines[which], model)
        total = value if total is None else [a + b for a, b in zip(total, value, strict=True)]
    out[start:] = pack_gains(total, lines.shape[2])


def home_sum(place, groups, extra):
    shards = len(groups[0])
    rows = sum(group[0].shape[0] for group in groups)
    width = groups[0][0].shape[1]
    return launch(
        functools.partial(home_kernel, len(groups), shards),
        [place, *[part for group in groups for part in group]],
        [smem()] + [vmem()] * (len(groups) * shards),
        0.1,
        out_shape=[jax.ShapeDtypeStruct((rows, width), BF16)],
        out_specs=[vmem()],
        scratch_shapes=[pltpu.VMEM((shards, extra, width), F32)],
        name="home_sum",
        vmem_mib=16,
    )[0]


def assemble_kernel(
    rows_total,
    core_ref,
    own_ref,
    other_ref,
    decay_ref,
    gate_out,
    out_out,
    input_out,
    recall_out,
    admit_out,
    recall_bias_out,
    admit_bias_out,
    taps_out,
    bias_out,
    decay_out,
    mean_out,
    gain_one_out,
    gain_two_out,
    whole,
    small,
):
    quads, rows, _ = own_ref.shape
    model = gate_out.shape[0]
    block = model // (2 * quads)
    extra = TABLE // (2 * quads)
    for quad in range(quads):
        for ref, who in ((own_ref, core_ref[0]), (other_ref, 1 - core_ref[0])):
            start = pl.multiple_of((quad * 2 + who) * block, block)
            gate_out[pl.ds(start, block), :] = ref[quad, :block].astype(F32)
            whole[pl.ds(start, block), :] = ref[quad, block : 2 * block].astype(F32)
            input_out[pl.ds(start, block), :] = ref[quad, 2 * block : 3 * block].astype(F32)
            start = pl.multiple_of((quad * 2 + who) * extra, extra)
            small[pl.ds(start, extra), :] = ref[quad, 3 * block : 3 * block + extra].astype(F32)
    out_out[...] = whole[...].T
    heads, head, _ = recall_out.shape
    lines = small[2 * head : 2 * head + 16]
    for h in range(heads):
        cols = slice(h * head, (h + 1) * head)
        recall_out[h] = small[:head, cols]
        admit_out[h] = small[head : 2 * head, cols]
        recall_bias_out[h : h + 1] = lines[5:6, cols]
        admit_bias_out[h : h + 1] = lines[6:7, cols]
    taps_out[...] = lines[:4]
    bias_out[...] = lines[4]
    decay_out[...] = lines[7] * (STRENGTH * jax.nn.sigmoid(-decay_ref[...]))
    mean_out[...] = lines[8] * (1.0 / rows_total)
    gains = None
    for ref in (own_ref, other_ref):
        part = None
        for quad in range(quads):
            value = unpack_gains(ref[quad, 3 * block + extra :], model)
            part = value if part is None else [a + b for a, b in zip(part, value, strict=True)]
        gains = part if gains is None else [a + b for a, b in zip(gains, part, strict=True)]
    gain_one_out[...] = gains[0].reshape(model)
    gain_two_out[...] = gains[1].reshape(model)


def assemble(core, own, other, decay, model, heads, head, rows_total):
    width = own.shape[2]
    shapes = [
        (model, width),
        (width, model),
        (model, width),
        (heads, head, head),
        (heads, head, head),
        (heads, head),
        (heads, head),
        (4, width),
        (width,),
        (width,),
        (width,),
        (model,),
        (model,),
    ]
    return launch(
        functools.partial(assemble_kernel, rows_total),
        [core, own, other, decay],
        [smem(), vmem(), vmem(), vmem()],
        0.1,
        out_shape=[jax.ShapeDtypeStruct(shape, F32) for shape in shapes],
        out_specs=[vmem()] * len(shapes),
        scratch_shapes=[pltpu.VMEM((model, width), F32), pltpu.VMEM((TABLE, width), F32)],
        name="assemble",
        vmem_mib=16,
    )


def on_device(
    tokens,
    doc_ids,
    cotangent,
    norm_gain,
    gate_proj,
    input_proj,
    conv_weight,
    conv_bias,
    recall_weight,
    recall_bias,
    admit_weight,
    admit_bias,
    decay_param,
    out_proj,
    mlp_gain,
    mlp_gate,
    mlp_up,
    mlp_down,
):
    count, model = tokens.shape
    width = gate_proj.shape[1]
    heads, head, _ = recall_weight.shape
    hidden_width = mlp_gate.shape[1]
    piece = mlp_gate.shape[0]
    quads = lax.axis_size("quad")
    shards = lax.axis_size("chan")
    group = 2 * quads
    quad = lax.axis_index("quad").astype(jnp.int32)
    core = lax.axis_index("core").astype(jnp.int32)
    place = lax.axis_index("chan").astype(jnp.int32)
    quad_one, core_one = quad.reshape(1), core.reshape(1)

    def hop(values, rel):
        return lax.ppermute(values, "quad", [(i, i ^ rel) for i in range(quads)])

    def swap(values):
        return lax.ppermute(values, "core", [(0, 1), (1, 0)])

    def along(values, shift):
        return lax.ppermute(values, "chan", [(i, (i + shift) % shards) for i in range(shards)])

    def share(values):
        every = jnp.broadcast_to(values[None], (quads,) + values.shape)
        return lax.all_to_all(every, "quad", 0, 0, tiled=True)

    slots = (quad * 2 + core).reshape(1)
    arriving = jnp.stack([(quad ^ rel) * 2 for rel in range(quads)])
    arriving = jnp.concatenate([arriving + core, arriving + 1 - core])

    def halves(values, made):
        if made:
            return made
        rows = values.shape[0]
        split = values.reshape(rows, quads, 2, model // group)
        return [
            lax.dynamic_index_in_dim(split, who, 2, False).reshape(rows, model // 2)
            for who in (core, 1 - core)
        ]

    ends = along(tokens[count - HALO :], 1)
    own_weights, own_table, pieces = prepare(
        slots,
        gate_proj,
        input_proj,
        out_proj,
        recall_weight,
        recall_bias,
        admit_weight,
        admit_bias,
        conv_weight,
        conv_bias,
        decay_param,
        group,
    )
    arrived = along(pieces, 1)
    normed, *made = norm(core_one, ends, tokens, norm_gain, group)

    offset = place * count
    spots = (offset + jnp.arange(count)) % LENGTH
    padded = jnp.concatenate([jnp.full((HALO,), -1, jnp.int32), doc_ids])
    here = lax.dynamic_slice_in_dim(padded, offset + HALO, count)
    columns = [jnp.ones((count,), F32)]
    for shift in range(1, 4):
        moved = lax.dynamic_slice_in_dim(padded, offset + HALO - shift, count)
        columns.append(((spots >= shift) & (here == moved)).astype(F32))
    columns += [jnp.zeros((count,), F32)] * 4
    mask = jnp.stack(columns, axis=1)

    own_width = hidden_width // quads
    slices = jnp.stack([mlp_gate, mlp_up, mlp_down])
    slices = slices.reshape(3, piece, quads, own_width).transpose(2, 0, 1, 3)
    def local(shard, weight_pieces, stacks, after=()):
        return mix_local(
            shard, shards, head, arriving, normed, mask, weight_pieces, stacks, after
        )

    normed_own, normed_other = halves(normed, made)
    normed_other = swap(normed_other)
    stacks, _ = local(0, [own_weights, own_table], None)
    (slices,) = fence([slices], [pieces])
    slices = lax.all_to_all(slices, "quad", 0, 0, tiled=True)
    near = quads // 2 + 1
    cots = [cotangent] + [hop(cotangent, rel) for rel in range(1, near)]
    gathered, waits, edges, shard_pieces = None, [normed_other, *cots[1:]], [stacks[5]], []
    for s in range(1, shards + 1):
        onward = [arrived] if s < shards else [cotangent]
        if s == min(2, shards - 1):
            onward.append(slices)
        if s == 1:
            arrived, *onward = fence(onward, waits)
        else:
            packed, arrived, *onward = pack(held, onward, [edges[s - 2]])
            stacks, _ = local(s - 1, [packed, swap(packed)], stacks)
            edges.append(stacks[5])
        if onward:
            gathered = lax.all_gather(onward[0], "chan", axis=0)
        if s == shards:
            cots += [hop(arrived, rel) for rel in range(near, quads)]
            break
        held = [arrived] + [hop(arrived, rel) for rel in range(1, quads)]
        if s < shards - 1:
            arrived = along(arrived, 1)
    weights, inputs, gated, kept, scan, edge, gates, vec = stacks
    (edge,) = fence([edge], cots[near:])
    depth = LENGTH // count - 1
    behind = [along(edge, i + 1) for i in range(depth)]
    (gathered,) = fence([gathered], behind)
    carry, branch_in, middle, second, again = branch(
        scan, gated, weights, tokens, mlp_gain.reshape(1, model), behind, []
    )
    mlp_weights = arrange(core_one, gathered, swap(gathered), [second])
    ahead = [along(edge, -(i + 1)) for i in range(depth - 1)]
    branch_in_other = swap(branch_in)

    gate_grads, up_grads, hiddens, backs, seconds = [], [], [], [], []
    for rel in range(quads):
        if rel == 0:
            seconds.append(second)
        else:
            seconds.append(hop(second if rel < near else again, rel))
        gate_grad, up_grad, hidden, back, *carry_on = mlp_block(
            seconds[rel], cots[rel], mlp_weights,
            backs[-1:] if rel else [*ahead, branch_in_other], [] if rel else [again],
        )
        if rel == 0:
            (again,) = carry_on
        gate_grads.append(gate_grad)
        up_grads.append(up_grad)
        hiddens.append(hidden)
        backs.append(back)
    backs = [hop(back, rel) if rel else back for rel, back in enumerate(backs)]
    own_grads, other_grads, results = mlp_grads(
        quad_one, core_one, mlp_weights, cots, seconds, gate_grads, up_grads, hiddens, shards
    )
    results = lax.all_to_all(results, "quad", 0, 0, tiled=True)
    middle_grad, branch_grad, gain_two, *made, own_grads, other_grads = middle_back(
        backs, middle, cotangent, mlp_gain, core_one, group, [], [own_grads, other_grads]
    )

    def reduce(chip):
        return jnp.sum(lax.all_to_all(chip, "quad", 0, 0, tiled=True).astype(F32), axis=0)

    grad_own, grad_other = halves(branch_grad, made)
    block_out = (middle + jnp.sum(results.astype(F32), axis=0)).astype(BF16)
    gate_back, adj, edge_back, own_grads = adjoint(
        branch_grad, weights, gated, scan, kept, carry, mask, vec, [own_grads]
    )
    edges_back = [along(edge_back, -(i + 1)) for i in range(depth)]
    (chip_one,) = outer(
        core_one,
        quads,
        [
            normed_own[HALO:],
            normed_other[HALO:],
            gate_back,
            swap(gate_back),
            grad_own,
            swap(grad_other),
            branch_in,
            branch_in_other,
        ],
        after=[*edges_back, results],
    )
    grads = add_pair(own_grads, swap(other_grads))
    grads = lax.psum_scatter(grads, "chan", scatter_dimension=0)

    def home(totals):
        return [totals[0]] + [along(totals[s].astype(BF16), -s) for s in range(1, shards)]

    sum_one = reduce(chip_one)
    input_back, small, normed_grad = mix_back(
        weights, inputs, gate_back, kept, scan, adj, carry, mask, gates, vec, edge, edges_back, ahead,
        [chip_one],
    )

    halo_grad = along(normed_grad[:HALO].astype(BF16), -1)
    inside = ((place + 1) * count % LENGTH != 0).astype(jnp.int32).reshape(1)
    grad_tokens, lines = tokens_back(
        inside, normed_grad, halo_grad, tokens, norm_gain, middle_grad, gain_two, width
    )
    (chip_two,) = outer(
        core_one,
        quads,
        [normed_own, normed_other, input_back, swap(input_back)],
        [small, swap(small)],
        [sum_one, lines],
    )
    home_one = home(sum_one)
    extra = lines.shape[0]
    totals = reduce(chip_two)
    totals, grads = fence([totals, grads], home_one[1:])
    grads = lax.all_to_all(grads, "quad", 0, 0, tiled=True)
    grads = grads.transpose(1, 2, 0, 3).reshape(3, piece, hidden_width).astype(F32)
    totals = jnp.concatenate(
        [totals, jnp.broadcast_to(lines.astype(F32)[None], (shards, extra, width))], axis=1
    )
    everything = home_sum(place.reshape(1), [home_one, home(totals)], extra)
    (everything,) = fence([everything], [grads])
    own = share(everything)
    (
        grad_gate,
        grad_out,
        grad_input,
        grad_recall,
        grad_admit,
        grad_recall_bias,
        grad_admit_bias,
        grad_taps,
        grad_bias,
        grad_decay,
        gate_mean,
        gain_one,
        gain_two,
    ) = assemble(
        core_one, own, swap(own), decay_param, model, heads, head, count * group * shards
    )

    return (
        block_out,
        grad_tokens,
        gain_one,
        grad_gate,
        grad_input,
        grad_taps,
        grad_bias,
        grad_recall,
        grad_recall_bias,
        grad_admit,
        grad_admit_bias,
        grad_decay,
        grad_out,
        gain_two,
        grads[0],
        grads[1],
        grads[2],
        gate_mean,
    )


def solution(mesh):
    in_specs = (
        P(("quad", "core", "chan"), None),
        P(("quad", "core")),
        P(("quad", "core", "chan"), None),
        P(),
        P(None, "chan"),
        P(None, "chan"),
        P(None, "chan"),
        P("chan"),
        P("chan", None, None),
        P("chan", None),
        P("chan", None, None),
        P("chan", None),
        P("chan"),
        P("chan", None),
        P(),
        P(("quad", "core", "chan"), None),
        P(("quad", "core", "chan"), None),
        P(("quad", "core", "chan"), None),
    )
    out_specs = (
        P(("quad", "core", "chan"), None),
        P(("quad", "core", "chan"), None),
        P(),
        P(None, "chan"),
        P(None, "chan"),
        P(None, "chan"),
        P("chan"),
        P("chan", None, None),
        P("chan", None),
        P("chan", None, None),
        P("chan", None),
        P("chan"),
        P("chan", None),
        P(),
        P(("quad", "core", "chan"), None),
        P(("quad", "core", "chan"), None),
        P(("quad", "core", "chan"), None),
        P("chan"),
    )
    devices = mesh.devices
    quads, shards = devices.shape[0] // 2, devices.shape[1]
    split = jax.sharding.Mesh(devices.reshape(quads, 2, shards), ("quad", "core", "chan"))
    return jax.shard_map(
        on_device, mesh=split, in_specs=in_specs, out_specs=out_specs, check_vma=False
    )
```

```python
import functools

import jax
import jax.numpy as jnp
from jax import lax
from jax.experimental import pallas as pl
from jax.experimental.pallas import tpu as pltpu
from jax.sharding import PartitionSpec as P

LENGTH = 1024
EPS = 1e-06
STRENGTH = 8.0
HALO = 16
TABLE = 256
COST = 0.3
GELU_A = 0.7978845608028654
GELU_B = 0.044715
BF16 = jnp.bfloat16
F32 = jnp.float32
MIB = 1024 * 1024


def mm(left, right, left_dim, right_dim):
    return lax.dot_general(
        left, right, (((left_dim,), (right_dim,)), ((), ())), preferred_element_type=F32
    )


def gelu_parts(value):
    square = value * value
    th = jnp.tanh(GELU_A * value * (1.0 + GELU_B * square))
    half = 0.5 * (1.0 + th)
    slope = half + 0.5 * value * (1.0 - th * th) * (GELU_A * (1.0 + 3.0 * GELU_B * square))
    return value * half, slope


def gelu(value):
    th = jnp.tanh(GELU_A * value * (1.0 + GELU_B * value * value))
    return 0.5 * value * (1.0 + th)


def one_minus_exp(v):
    series = v * (
        1.0
        - v
        * (1 / 2)
        * (
            1.0
            - v
            * (1 / 3)
            * (1.0 - v * (1 / 4) * (1.0 - v * (1 / 5) * (1.0 - v * (1 / 6) * (1.0 - v * (1 / 7)))))
        )
    )
    return jnp.where(v < 0.4, series, 1.0 - jnp.exp(-v))


def rows_index(shape):
    return lax.broadcasted_iota(jnp.int32, shape, 0)


def scan_down(a, b):
    count = a.shape[0]
    index = rows_index(a.shape)
    step = 1
    while step < count:
        if step < 8:
            inside = index >= step
            a_prev = jnp.where(inside, pltpu.roll(a, step, 0), 1.0)
            b_prev = jnp.where(inside, pltpu.roll(b, step, 0), 0.0)
        else:
            a_prev = jnp.concatenate([jnp.ones_like(a[:step]), a[: count - step]], axis=0)
            b_prev = jnp.concatenate([jnp.zeros_like(b[:step]), b[: count - step]], axis=0)
        b = b + a * b_prev
        a = a * a_prev
        step *= 2
    return a, b


def scan_up(a, b):
    count = a.shape[0]
    index = rows_index(a.shape)
    step = 1
    while step < count:
        if step < 8:
            inside = index < count - step
            a_next = jnp.where(inside, pltpu.roll(a, count - step, 0), 1.0)
            b_next = jnp.where(inside, pltpu.roll(b, count - step, 0), 0.0)
        else:
            a_next = jnp.concatenate([a[step:], jnp.ones_like(a[:step])], axis=0)
            b_next = jnp.concatenate([b[step:], jnp.zeros_like(b[:step])], axis=0)
        b = b + a * b_next
        a = a * a_next
        step *= 2
    return a, b


def block_diagonal(flat, head, dtype):
    width = flat.shape[1]
    tall = jnp.concatenate([flat] * (width // head), axis=0)
    shape = (width, width)
    row = lax.broadcasted_iota(jnp.int32, shape, 0) // head
    col = lax.broadcasted_iota(jnp.int32, shape, 1) // head
    return jnp.where(row == col, tall, 0.0).astype(dtype)


def fold_diagonal(square, head):
    width = square.shape[0]
    row = lax.broadcasted_iota(jnp.int32, square.shape, 0) // head
    col = lax.broadcasted_iota(jnp.int32, square.shape, 1) // head
    kept = jnp.where(row == col, square, 0.0)
    total = kept[:head]
    for start in range(head, width, head):
        total = total + kept[start : start + head]
    return total


def vmem():
    return pl.BlockSpec(memory_space=pltpu.VMEM)


def smem():
    return pl.BlockSpec(memory_space=pltpu.SMEM)


def launch(
    kernel,
    inputs,
    in_specs,
    micros,
    after=(),
    carry=(),
    prefetch=0,
    grid=(),
    out_shape=(),
    out_specs=(),
    scratch_shapes=(),
    aliases=None,
    name=None,
    vmem_mib=60,
):
    count, extra, through = len(inputs), len(after), len(carry)
    made = len(out_shape)
    aliases = dict(aliases or {})
    for i in range(through):
        aliases[count + extra + i] = made + i

    def body(*refs):
        first = count + extra + through
        kernel(*refs[:count], *refs[first : first + made], *refs[first + made + through :])

    anywhere = pl.BlockSpec(memory_space=pl.ANY)
    return pl.pallas_call(
        body,
        out_shape=list(out_shape) + [jax.ShapeDtypeStruct(c.shape, c.dtype) for c in carry],
        grid_spec=pltpu.PrefetchScalarGridSpec(
            num_scalar_prefetch=prefetch,
            grid=grid,
            in_specs=list(in_specs) + [anywhere] * (extra + through),
            out_specs=list(out_specs) + [anywhere] * through,
            scratch_shapes=scratch_shapes,
        ),
        input_output_aliases=aliases,
        compiler_params=pltpu.CompilerParams(vmem_limit_bytes=vmem_mib * MIB),
        cost_estimate=pl.CostEstimate(
            flops=int(micros * 1.1e9 * COST), bytes_accessed=int(micros * 3.5e6 * COST), transcendentals=0
        ),
        name=name,
    )(*inputs, *after, *carry)


def split_features(core, source, own_out, other_out):
    half = own_out.shape[1]
    block = 128
    quads = half // block
    for quad in range(quads):
        for out, who in ((own_out, core), (other_out, 1 - core)):
            start = pl.multiple_of((quad * 2 + who) * block, block)
            out[:, quad * block : (quad + 1) * block] = source[:, pl.ds(start, block)]


def pack_kernel(*refs):
    *pieces, out = refs
    for i, ref in enumerate(pieces):
        out[i] = ref[0]


def pack(pieces, carry, after):
    return launch(
        pack_kernel,
        pieces,
        [vmem()] * len(pieces),
        0.1,
        after,
        carry,
        out_shape=[jax.ShapeDtypeStruct((len(pieces),) + pieces[0].shape[1:], pieces[0].dtype)],
        out_specs=[vmem()],
        name="pack",
        vmem_mib=8,
    )


def fence(carry, after=()):
    return launch(lambda *refs: None, [], [], 0.01, after, carry, name="fence", vmem_mib=60)


def prepare_kernel(
    slots_ref,
    gate_ref,
    input_ref,
    out_ref,
    recall_ref,
    recall_bias_ref,
    admit_ref,
    admit_bias_ref,
    taps_ref,
    bias_ref,
    decay_ref,
    weights,
    table_out,
    pieces_out,
    table,
):
    weights[0] = gate_ref[...]
    weights[1] = input_ref[...]
    weights[2] = out_ref[...].T
    heads, head, _ = recall_ref.shape
    for h in range(heads):
        cols = slice(h * head, (h + 1) * head)
        table[:head, cols] = recall_ref[h]
        table[head : 2 * head, cols] = admit_ref[h]
    side = jnp.concatenate
    lines = side(
        [
            taps_ref[...],
            bias_ref[...].reshape(1, -1),
            side([recall_bias_ref[h : h + 1] for h in range(heads)], axis=1),
            side([admit_bias_ref[h : h + 1] for h in range(heads)], axis=1),
            jax.nn.softplus(-decay_ref[...].reshape(1, -1)),
        ],
        axis=0,
    )
    high = lines.astype(BF16).astype(F32)
    rest = lines - high
    mid = rest.astype(BF16).astype(F32)
    table[2 * head : 2 * head + 8] = high
    table[2 * head + 8 : 2 * head + 16] = mid
    table[2 * head + 16 : 2 * head + 24] = rest - mid
    table[2 * head + 24 :] = jnp.zeros((table.shape[0] - 2 * head - 24, table.shape[1]), F32)
    table_out[...] = table[...].astype(BF16)
    count, rows, _ = pieces_out.shape
    block = pieces_block(weights.shape[1], rows)
    extra = rows - 3 * block
    for k in range(count):
        start = pl.multiple_of(slots_ref[k] * block, block)
        for part in range(3):
            pieces_out[k, part * block : (part + 1) * block] = weights[part, pl.ds(start, block), :]
        start = pl.multiple_of(slots_ref[k] * extra, extra)
        pieces_out[k, 3 * block :] = table_out[pl.ds(start, extra), :]

def norm_kernel(core_ref, ends_ref, tokens_ref, gain_ref, normed_out, *halves_out):
    for ref, rows in ((ends_ref, slice(0, HALO)), (tokens_ref, slice(HALO, None))):
        values = ref[...].astype(F32)
        scale = lax.rsqrt(jnp.mean(values * values, axis=1, keepdims=True) + EPS)
        normed_out[rows] = (values * scale * gain_ref[...]).astype(BF16)
    if halves_out:
        split_features(core_ref[0], normed_out, *halves_out)


def norm(core, ends, tokens, gain, group):
    count, model = tokens.shape
    halves = half_shapes(HALO + count, model, group)
    return launch(
        norm_kernel,
        [core, ends, tokens, gain.reshape(1, model)],
        [smem()] + [vmem()] * 3,
        0.1,
        out_shape=[jax.ShapeDtypeStruct((HALO + count, model), BF16)] + halves,
        out_specs=[vmem()] * (1 + len(halves)),
        name="norm",
        vmem_mib=16,
    )


def pieces_block(model, rows):
    return rows * model // (3 * model + TABLE)


def half_shapes(rows, model, group):
    return [jax.ShapeDtypeStruct((rows, model // 2), BF16)] * (2 if model // group == 128 else 0)


def prepare(slots, gate, inputs, out, recall, recall_bias, admit, admit_bias, taps, bias, decay, group):
    model, width = gate.shape
    rows = (3 * model + TABLE) // group
    return launch(
        prepare_kernel,
        [slots, gate, inputs, out, recall, recall_bias, admit, admit_bias, taps, bias, decay],
        [smem()] + [vmem()] * 10,
        0.1,
        out_shape=[
            jax.ShapeDtypeStruct((3, model, width), BF16),
            jax.ShapeDtypeStruct((TABLE, width), BF16),
            jax.ShapeDtypeStruct((slots.shape[0], rows, width), BF16),
        ],
        out_specs=[vmem()] * 3,
        scratch_shapes=[pltpu.VMEM((TABLE, width), F32)],
        name="prepare",
    )


def mix_local_kernel(own, head, counts, stacked, slots_ref, normed_ref, mask_ref, *rest):
    piece_refs, rest = rest[: len(counts)], rest[len(counts) :]
    weights, inputs_out, gated_out, kept_out, scan_out, edge_out, gates_out, vec_out = rest[
        stacked : stacked + 8
    ]
    (table,) = rest[stacked + 8 :]
    model = normed_ref.shape[1]
    if own:
        weights[0] = piece_refs[0][...]
        table[...] = piece_refs[1][...].astype(F32)
    else:
        number = 0
        for ref, many in zip(piece_refs, counts, strict=True):
            rows = ref.shape[1]
            block = pieces_block(model, rows)
            extra = rows - 3 * block
            for k in range(many):
                slot = slots_ref[number]
                number += 1
                start = pl.multiple_of(slot * block, block)
                for part in range(3):
                    weights[0, part, pl.ds(start, block), :] = ref[
                        k, part * block : (part + 1) * block
                    ]
                start = pl.multiple_of(slot * extra, extra)
                table[pl.ds(start, extra), :] = ref[k, 3 * block :].astype(F32)
    count = mask_ref.shape[0]
    vec = table[2 * head : 2 * head + 8] + (
        table[2 * head + 8 : 2 * head + 16] + table[2 * head + 16 : 2 * head + 24]
    )
    vec_out[0] = vec
    gates_out[0] = table[: 2 * head].astype(BF16)
    gated = mm(normed_ref[HALO:], weights[0, 0], 1, 0).astype(BF16)
    gated_out[0] = gated
    inputs = mm(normed_ref[...], weights[0, 1], 1, 0).astype(BF16)
    inputs_out[0] = inputs
    wide = inputs.astype(F32)
    conv = vec[4:5] + vec[0:1] * wide[HALO:]
    for shift in range(1, 4):
        moved = pltpu.roll(wide, shift, 0)[HALO:]
        conv = conv + vec[shift : shift + 1] * (moved * mask_ref[:, shift : shift + 1])
    low = conv.astype(BF16)
    recall_weight = block_diagonal(table[:head], head, BF16)
    admit_weight = block_diagonal(table[head : 2 * head], head, BF16)
    recall = jax.nn.sigmoid(mm(low, recall_weight, 1, 0) + vec[5:6])
    admit = jax.nn.sigmoid(mm(low, admit_weight, 1, 0) + vec[6:7])
    rate = STRENGTH * recall * vec[7:8]
    decay = jnp.exp(-rate)
    inject = jnp.sqrt(one_minus_exp(2.0 * rate)) * admit * conv
    product, state = scan_down(decay * mask_ref[:, 1:2], inject)
    kept_out[0, 0] = conv
    kept_out[0, 1] = recall
    kept_out[0, 2] = admit
    scan_out[0, 0] = product
    scan_out[0, 1] = state
    edge_out[0, 0:1] = product[count - 1 :]
    edge_out[0, 1:2] = state[count - 1 :]
    edge_out[0, 2:3] = jnp.sum(decay, axis=0, keepdims=True)


def mix_local(shard, shards, head, slots, normed, mask, pieces, stacks, after=(), carry=()):
    count = mask.shape[0]
    model = normed.shape[1]
    width = pieces[0].shape[-1]
    own = shard == 0
    counts = [p.shape[0] for p in pieces]
    shapes = [
        ((shards, 3, model, width), BF16),
        ((shards, count + HALO, width), BF16),
        ((shards, count, width), BF16),
        ((shards, 3, count, width), F32),
        ((shards, 2, count, width), F32),
        ((shards, 8, width), F32),
        ((shards, 2 * head, width), BF16),
        ((shards, 8, width), F32),
    ]

    def at(shape):
        tail = (0,) * (len(shape) - 1)
        return pl.BlockSpec((1,) + shape[1:], lambda i: (shard,) + tail)

    first = [slots, normed, mask, *pieces]
    in_specs = [smem()] + [vmem()] * (len(first) - 1)
    aliases = {}
    if stacks is not None:
        aliases = {len(first) + i: i for i in range(len(stacks))}
        in_specs += [pl.BlockSpec(memory_space=pl.ANY)] * len(stacks)
        first += list(stacks)
    outs = launch(
        functools.partial(mix_local_kernel, own, head, counts, len(aliases)),
        first,
        in_specs,
        5.7,
        after=after,
        carry=carry,
        grid=(1,),
        out_shape=[jax.ShapeDtypeStruct(shape, dtype) for shape, dtype in shapes],
        out_specs=[at(shape) for shape, _ in shapes],
        scratch_shapes=[pltpu.VMEM((TABLE, width), F32)],
        aliases=aliases,
        name="mix_local",
    )
    return outs[:8], outs[8:]


def carried(edges):
    total = edges[-1][0, 1:2]
    for edge in edges[-2::-1]:
        total = edge[0, 1:2] + edge[0, 0:1] * total
    return total


def branch_kernel(
    depth, scan_ref, gated_ref, weight_ref, resid_ref, gain_ref, *rest
):
    edges = rest[:depth]
    carry_out, branch_in_out, middle_out, second_out, again_out, acc = rest[depth:]
    step = pl.program_id(0)

    @pl.when(step == 0)
    def _():
        acc[...] = resid_ref[...].astype(F32)

    carry = carried(edges)
    carry_out[0] = jnp.broadcast_to(carry, carry_out.shape[1:])
    state = scan_ref[0, 1] + scan_ref[0, 0] * carry
    mixed = (gelu(gated_ref[0].astype(F32)) * state).astype(BF16)
    branch_in_out[0] = mixed
    acc[...] += mm(mixed, weight_ref[0, 0], 1, 1)

    @pl.when(step == pl.num_programs(0) - 1)
    def _():
        middle = acc[...]
        middle_out[...] = middle
        scale = lax.rsqrt(jnp.mean(middle * middle, axis=1, keepdims=True) + EPS)
        second = (middle * scale * gain_ref[...]).astype(BF16)
        second_out[...] = second
        again_out[...] = second


def branch(scan, gated, weights, tokens, gain, edges, after):
    shards, _, count, width = scan.shape
    model = tokens.shape[1]

    def edge_spec(shift):
        return pl.BlockSpec((1, 8, width), lambda s: ((s + shards - shift % shards) % shards, 0, 0))

    return launch(
        functools.partial(branch_kernel, len(edges)),
        [scan, gated, weights, tokens, gain, *edges],
        [
            pl.BlockSpec((1, 2, count, width), lambda s: (s, 0, 0, 0)),
            pl.BlockSpec((1, count, width), lambda s: (s, 0, 0)),
            pl.BlockSpec((1, 1, model, width), lambda s: (s, 2, 0, 0)),
            pl.BlockSpec((count, model), lambda s: (0, 0)),
            pl.BlockSpec((1, model), lambda s: (0, 0)),
        ]
        + [edge_spec(i + 1) for i in range(len(edges))],
        0.1,
        after,
        grid=(shards,),
        out_shape=[
            jax.ShapeDtypeStruct((shards, 8, width), F32),
            jax.ShapeDtypeStruct((shards, count, width), BF16),
            jax.ShapeDtypeStruct((count, model), F32),
            jax.ShapeDtypeStruct((count, model), BF16),
            jax.ShapeDtypeStruct((count, model), BF16),
        ],
        out_specs=[
            pl.BlockSpec((1, 8, width), lambda s: (s, 0, 0)),
            pl.BlockSpec((1, count, width), lambda s: (s, 0, 0)),
            pl.BlockSpec((count, model), lambda s: (0, 0)),
            pl.BlockSpec((count, model), lambda s: (0, 0)),
            pl.BlockSpec((count, model), lambda s: (0, 0)),
        ],
        scratch_shapes=[pltpu.VMEM((count, model), F32)],
        name="mix_branch",
    )


def arrange_kernel(core_ref, own_ref, other_ref, out_ref):
    shards, quads, _, piece, _ = own_ref.shape
    for ref, core in ((own_ref, core_ref[0]), (other_ref, 1 - core_ref[0])):
        for shard in range(shards):
            for quad in range(quads):
                start = pl.multiple_of(((quad * 2 + core) * shards + shard) * piece, piece)
                for part in range(3):
                    out_ref[part, pl.ds(start, piece), :] = ref[shard, quad, part]


def arrange(core, own, other, after):
    shards, quads, _, piece, width = own.shape
    if piece % 16:
        both = jnp.where(core[0] == 0, jnp.stack([own, other]), jnp.stack([other, own]))
        return both.transpose(3, 2, 0, 1, 4, 5).reshape(3, 2 * shards * quads * piece, width)
    return launch(
        arrange_kernel,
        [core, own, other],
        [smem(), vmem(), vmem()],
        0.1,
        after,
        out_shape=[jax.ShapeDtypeStruct((3, 2 * shards * quads * piece, width), BF16)],
        out_specs=[vmem()],
        name="mlp_arrange",
        vmem_mib=16,
    )[0]


def mlp_tiles(width):
    tile = 256 if width % 256 == 0 else width
    return [slice(start, start + tile) for start in range(0, width, tile)]


def mlp_kernel(
    second_ref,
    cot_ref,
    weight_ref,
    gate_grad_out,
    up_grad_out,
    hidden_out,
    back_out,
):
    second = second_ref[...]
    cot = cot_ref[...]
    total = None
    for cols in mlp_tiles(weight_ref.shape[2]):
        gate_weight, up_weight = weight_ref[0, :, cols], weight_ref[1, :, cols]
        gate = mm(second, gate_weight, 1, 0)
        upward = mm(second, up_weight, 1, 0)
        hidden_grad = mm(cot, weight_ref[2, :, cols], 1, 0)
        act, slope = gelu_parts(gate)
        hidden_out[:, cols] = (act * upward).astype(BF16)
        gate_grad = (hidden_grad * upward * slope).astype(BF16)
        up_grad = (hidden_grad * act).astype(BF16)
        gate_grad_out[:, cols] = gate_grad
        up_grad_out[:, cols] = up_grad
        back = mm(gate_grad, gate_weight, 1, 1) + mm(up_grad, up_weight, 1, 1)
        total = back if total is None else total + back
    back_out[...] = total.astype(BF16)


def mlp_block(second, cot, weights, after, carry):
    count, model = second.shape
    width = weights.shape[-1]
    wide = jax.ShapeDtypeStruct((count, width), BF16)
    return launch(
        mlp_kernel,
        [second, cot, weights],
        [vmem()] * 3,
        7.4,
        after,
        carry,
        out_shape=[wide, wide, wide, jax.ShapeDtypeStruct((count, model), BF16)],
        out_specs=[vmem()] * 4,
        name="mlp_block",
        vmem_mib=16,
    )


def mlp_grads_kernel(quads, quad_ref, core_ref, weight_ref, *rest):
    cots, rest = rest[:quads], rest[quads:]
    seconds, rest = rest[:quads], rest[quads:]
    gate_grads, rest = rest[:quads], rest[quads:]
    up_grads, rest = rest[:quads], rest[quads:]
    hiddens, rest = rest[:quads], rest[quads:]
    *grads_out, results_out, second, cot, left, whole_ref = rest
    count = seconds[0].shape[0]
    rows = [slice(rel * count, (rel + 1) * count) for rel in range(quads)]
    for rel in range(quads):
        second[rows[rel]] = seconds[rel][...]
        cot[rows[rel]] = cots[rel][...]
    total = None
    for cols in mlp_tiles(weight_ref.shape[2]):
        for part, (base, group) in enumerate(
            ((second, gate_grads), (second, up_grads), (cot, hiddens))
        ):
            for rel in range(quads):
                left[rows[rel]] = group[rel][:, cols]
            whole = mm(base[...], left[...], 0, 0).astype(BF16)
            if len(grads_out) == 1:
                grads_out[0][part, :, cols] = whole
                continue
            whole_ref[...] = whole
            shards, _, _, piece, _ = grads_out[0].shape
            for out, core in zip(grads_out, (core_ref[0], 1 - core_ref[0]), strict=True):
                for shard in range(shards):
                    for quad in range(quads):
                        start = pl.multiple_of(((quad * 2 + core) * shards + shard) * piece, piece)
                        out[shard, quad, part, :, cols] = whole_ref[pl.ds(start, piece), :]
        result = mm(left[...], weight_ref[2, :, cols], 1, 1)
        total = result if total is None else total + result
    for rel in range(quads):
        results_out[quad_ref[0] ^ rel] = total[rows[rel]].astype(BF16)


def mlp_grads(quad, core, weights, cots, seconds, gate_grads, up_grads, hiddens, shards):
    quads = len(seconds)
    count, model = seconds[0].shape
    width = weights.shape[2]
    tile = mlp_tiles(width)[0].stop
    piece = model // (quads * 2 * shards)
    shapes = [(shards, quads, 3, piece, width)] * 2 if piece % 16 == 0 else [(3, model, width)]
    *grads, results = launch(
        functools.partial(mlp_grads_kernel, quads),
        [quad, core, weights, *cots, *seconds, *gate_grads, *up_grads, *hiddens],
        [smem()] * 2 + [vmem()] * (1 + 5 * quads),
        15.0,
        out_shape=[jax.ShapeDtypeStruct(shape, BF16) for shape in shapes]
        + [jax.ShapeDtypeStruct((quads, count, model), BF16)],
        out_specs=[vmem()] * (1 + len(shapes)),
        scratch_shapes=[
            pltpu.VMEM((quads * count, model), BF16),
            pltpu.VMEM((quads * count, model), BF16),
            pltpu.VMEM((quads * count, tile), BF16),
            pltpu.VMEM((model, tile), BF16),
        ],
        name="mlp_grads",
        vmem_mib=32,
    )
    if piece % 16:
        both = grads[0].reshape(3, quads, 2, shards, piece, width).transpose(2, 3, 1, 0, 4, 5)
        grads = [lax.dynamic_index_in_dim(both, who, 0, False) for who in (core[0], 1 - core[0])]
    return *grads, results


def add_kernel(a_ref, b_ref, out_ref):
    out_ref[...] = (a_ref[...].astype(F32) + b_ref[...].astype(F32)).astype(BF16)


def add_pair(a, b, after=()):
    return launch(
        add_kernel,
        [a, b],
        [vmem()] * 2,
        0.1,
        after,
        out_shape=[jax.ShapeDtypeStruct(a.shape, BF16)],
        out_specs=[vmem()],
        name="add_pair",
        vmem_mib=16,
    )[0]


def middle_kernel(blocks, back_ref, *rest):
    (*backs, values_ref, cot_ref, gain_ref, core_ref), outs = rest[: blocks + 3], rest[blocks + 3 :]
    middle_grad_out, low_out, gain_out, *halves_out = outs
    grad = back_ref[...].astype(F32)
    for ref in backs:
        grad = grad + ref[...].astype(F32)
    values = values_ref[...]
    scale = lax.rsqrt(jnp.mean(values * values, axis=1, keepdims=True) + EPS)
    scaled = grad * gain_ref[...]
    inner = jnp.mean(scaled * values, axis=1, keepdims=True)
    total = cot_ref[...].astype(F32) + scale * scaled - values * (scale * scale * scale * inner)
    middle_grad_out[...] = total
    low_out[...] = total.astype(BF16)
    if halves_out:
        split_features(core_ref[0], low_out, *halves_out)
    gain_out[...] = jnp.sum(grad * values * scale, axis=0, keepdims=True)


def middle_back(backs, values, cot, gain, core, group, after, carry):
    count, model = values.shape
    halves = half_shapes(count, model, group)
    return launch(
        functools.partial(middle_kernel, len(backs)),
        [*backs, values, cot, gain.reshape(1, model), core],
        [vmem()] * (len(backs) + 3) + [smem()],
        0.1,
        after,
        carry,
        out_shape=[
            jax.ShapeDtypeStruct((count, model), F32),
            jax.ShapeDtypeStruct((count, model), BF16),
            jax.ShapeDtypeStruct((1, model), F32),
        ]
        + halves,
        out_specs=[vmem()] * (3 + len(halves)),
        name="middle_back",
        vmem_mib=16,
    )


def tokens_kernel(
    inside_ref, grad_ref, halo_ref, tokens_ref, gain_ref, middle_grad_ref, gain_two_ref, out, lines_out
):
    grad = grad_ref[HALO:]
    count = grad.shape[0]
    last = jnp.where(inside_ref[0] > 0, halo_ref[...].astype(F32), 0.0)
    grad = jnp.concatenate([grad[: count - HALO], grad[count - HALO :] + last], axis=0)
    values = tokens_ref[...].astype(F32)
    scale = lax.rsqrt(jnp.mean(values * values, axis=1, keepdims=True) + EPS)
    scaled = grad * gain_ref[...]
    inner = jnp.mean(scaled * values, axis=1, keepdims=True)
    out[...] = middle_grad_ref[...] + scale * scaled - values * (scale * scale * scale * inner)
    both = (jnp.sum(grad * values * scale, axis=0, keepdims=True), gain_two_ref[...])
    lines_out[...] = pack_gains(both, lines_out.shape[1])


def gain_chunk(model, width):
    chunk = 128
    while chunk * 2 <= width:
        chunk *= 2
    while chunk > width:
        chunk //= 2
    return chunk


def gain_lines(model, width):
    return 4 * (model // gain_chunk(model, width))


def pack_gains(both, width):
    chunk = gain_chunk(both[0].shape[1], width)
    lines = []
    for value in both:
        high = value.astype(BF16).astype(F32)
        for term in (high, value - high):
            lines += [term[:, i : i + chunk] for i in range(0, term.shape[1], chunk)]
    lines = jnp.concatenate(lines, axis=0)
    if chunk < width:
        blank = jnp.zeros((lines.shape[0], width - chunk), F32)
        lines = jnp.concatenate([lines, blank], axis=1)
    return lines.astype(BF16)


def unpack_gains(lines, model):
    chunk = gain_chunk(model, lines.shape[1])
    many = model // chunk
    lines = lines.astype(F32)
    both = []
    for i in range(2):
        value = lines[2 * i * many : (2 * i + 1) * many] + lines[
            (2 * i + 1) * many : (2 * i + 2) * many
        ]
        both.append(
            jnp.concatenate([value[j : j + 1, :chunk] for j in range(many)], axis=1)
        )
    return both


def tokens_back(inside, grad, halo, tokens, gain, middle_grad, gain_two, width):
    count, model = tokens.shape
    return launch(
        tokens_kernel,
        [inside, grad, halo, tokens, gain.reshape(1, model), middle_grad, gain_two],
        [smem()] + [vmem()] * 6,
        0.1,
        out_shape=[
            jax.ShapeDtypeStruct((count, model), F32),
            jax.ShapeDtypeStruct((gain_lines(model, width), width), BF16),
        ],
        out_specs=[vmem()] * 2,
        name="tokens_back",
        vmem_mib=16,
    )


def adjoint_kernel(
    grad_ref,
    weight_ref,
    gated_ref,
    scan_ref,
    kept_ref,
    carry_ref,
    mask_ref,
    vec_ref,
    gate_back_out,
    adjoint_out,
    edge_out,
):
    into = mm(grad_ref[...], weight_ref[0, 0], 1, 0).astype(BF16).astype(F32)
    act, slope = gelu_parts(gated_ref[0].astype(F32))
    state = scan_ref[0, 1] + scan_ref[0, 0] * carry_ref[0, 0:1]
    gate_back_out[0] = (into * state * slope).astype(BF16)
    decay = jnp.exp(-STRENGTH * kept_ref[0, 0] * vec_ref[0, 7:8]) * mask_ref[:, 1:2]
    count = decay.shape[0]
    shifted = jnp.where(
        rows_index(decay.shape) < count - 1, pltpu.roll(decay, count - 1, 0), 1.0
    )
    product, value = scan_up(shifted, into * act)
    adjoint_out[0, 0] = product
    adjoint_out[0, 1] = value
    edge_out[0] = jnp.broadcast_to(decay[0:1] * value[0:1], edge_out.shape[1:])


def adjoint(grad, weights, gated, scan, kept, carry, mask, vec, through):
    shards, _, count, width = scan.shape
    model = grad.shape[1]

    def flat(*shape):
        return pl.BlockSpec(shape, lambda s: (0,) * len(shape))

    def at(*shape):
        return pl.BlockSpec((1,) + shape, lambda s: (s,) + (0,) * len(shape))

    return launch(
        adjoint_kernel,
        [grad, weights, gated, scan, kept, carry, mask, vec],
        [
            flat(count, model),
            pl.BlockSpec((1, 1, model, width), lambda s: (s, 2, 0, 0)),
            at(count, width),
            at(2, count, width),
            pl.BlockSpec((1, 1, count, width), lambda s: (s, 1, 0, 0)),
            at(8, width),
            flat(*mask.shape),
            at(8, width),
        ],
        0.1,
        carry=through,
        grid=(shards,),
        out_shape=[
            jax.ShapeDtypeStruct((shards, count, width), BF16),
            jax.ShapeDtypeStruct((shards, 2, count, width), F32),
            jax.ShapeDtypeStruct((shards, 8, width), F32),
        ],
        out_specs=[at(count, width), at(2, count, width), at(8, width)],
        name="mix_adjoint",
    )


def outer_kernel(groups, core_ref, *rest):
    pairs, rest = rest[: 4 * groups], rest[4 * groups :]
    *smalls, out, left, right, small = rest
    count = pairs[2].shape[1]
    quads, shards = out.shape[:2]
    block = left.shape[1] // quads
    for group in range(groups):
        left_ref, left_other, right_ref, right_other = pairs[4 * group : 4 * group + 4]
        left[:count] = left_ref[left_ref.shape[0] - count :]
        left[count:] = left_other[left_ref.shape[0] - count :]
        for s in range(shards):
            right[:count] = right_ref[s]
            right[count:] = right_other[s]
            total = mm(left[...], right[...], 0, 0).astype(BF16)
            for quad in range(quads):
                out[quad, s, group * block : (group + 1) * block] = total[
                    quad * block : (quad + 1) * block
                ]
    if smalls:
        extra = out.shape[2] - groups * block
        for s in range(shards):
            small[...] = (smalls[0][s].astype(F32) + smalls[1][s].astype(F32)).astype(BF16)
            for quad in range(quads):
                start = pl.multiple_of((quad * 2 + core_ref[0]) * extra, extra)
                out[quad, s, groups * block :] = small[pl.ds(start, extra), :]


def outer(core, quads, pairs, smalls=(), after=(), carry=()):
    shards, count, width = pairs[2].shape
    model = pairs[0].shape[1]
    groups = len(pairs) // 4
    rows = groups * model // quads + (TABLE // (2 * quads) if smalls else 0)
    return launch(
        functools.partial(outer_kernel, groups),
        [core, *pairs, *smalls],
        [smem()] + [vmem()] * (len(pairs) + len(smalls)),
        0.1,
        after,
        carry,
        out_shape=[jax.ShapeDtypeStruct((quads, shards, rows, width), BF16)],
        out_specs=[vmem()],
        scratch_shapes=[
            pltpu.VMEM((2 * count, model), BF16),
            pltpu.VMEM((2 * count, width), BF16),
            pltpu.VMEM((TABLE, width), BF16),
        ],
        name="mix_outer",
    )


def mix_back_kernel(
    head,
    depth,
    gate_weight_ref,
    input_weight_ref,
    inputs_ref,
    gate_back_ref,
    kept_ref,
    scan_ref,
    adjoint_ref,
    carry_ref,
    mask_ref,
    gates_ref,
    vec_ref,
    edge_ref,
    *rest,
):
    backs, decays = rest[:depth], rest[depth : 2 * depth - 1]
    input_back_out, small_out, normed_grad_out, acc = rest[2 * depth - 1 :]
    step = pl.program_id(0)
    count = mask_ref.shape[0]
    width = vec_ref.shape[2]
    vec = vec_ref[0]
    incoming = backs[-1][0, 0:1]
    for back, edge in zip(backs[-2::-1], decays[::-1], strict=True):
        incoming = back[0, 0:1] + edge[0, 0:1] * incoming
    adj = adjoint_ref[0, 1] + adjoint_ref[0, 0] * incoming
    carry = carry_ref[0, 0:1]
    state = scan_ref[0, 1] + scan_ref[0, 0] * carry
    before = jnp.where(rows_index(state.shape) == 0, carry, pltpu.roll(state, 1, 0))
    conv, recall, admit = kept_ref[0, 0], kept_ref[0, 1], kept_ref[0, 2]
    speed = STRENGTH * vec[7:8]
    rate = recall * speed
    decay = jnp.exp(-rate)
    size = jnp.sqrt(one_minus_exp(2.0 * rate))
    sized = adj * size
    pulled = adj * admit
    log_grad = decay * (adj * before * mask_ref[:, 1:2] - pulled * conv * decay / size)
    recall_grad = -speed * log_grad * recall * (1.0 - recall)
    admit_grad = sized * conv * admit * (1.0 - admit)
    conv_grad = sized * admit
    recall_low = recall_grad.astype(BF16)
    admit_low = admit_grad.astype(BF16)
    gates = gates_ref[0].astype(F32)
    recall_weight = block_diagonal(gates[:head], head, BF16)
    admit_weight = block_diagonal(gates[head:], head, BF16)
    conv_grad = conv_grad + mm(recall_low, recall_weight, 1, 1) + mm(admit_low, admit_weight, 1, 1)
    wide = inputs_ref[0].astype(F32)
    blank = jnp.zeros((HALO, width), F32)
    reach = jnp.concatenate([blank, vec[0:1] * conv_grad], axis=0)
    tap_grads = [jnp.sum(conv_grad * wide[HALO:], axis=0, keepdims=True)]
    for shift in range(1, 4):
        masked = conv_grad * mask_ref[:, shift : shift + 1]
        moved = pltpu.roll(wide, shift, 0)[HALO:]
        tap_grads.append(jnp.sum(masked * moved, axis=0, keepdims=True))
        back = jnp.concatenate([blank, vec[shift : shift + 1] * masked], axis=0)
        reach = reach + pltpu.roll(back, count + HALO - shift, 0)
    input_back = reach.astype(BF16)
    conv_low = conv.astype(BF16)
    input_back_out[0] = input_back
    small_out[0, :head] = fold_diagonal(mm(conv_low, recall_low, 0, 0), head).astype(BF16)
    small_out[0, head : 2 * head] = fold_diagonal(mm(conv_low, admit_low, 0, 0), head).astype(BF16)
    rows = tap_grads + [
        jnp.sum(conv_grad, axis=0, keepdims=True),
        jnp.sum(recall_grad, axis=0, keepdims=True),
        jnp.sum(admit_grad, axis=0, keepdims=True),
        jnp.sum(recall * log_grad, axis=0, keepdims=True),
        edge_ref[0, 2:3],
    ]
    rows.append(jnp.zeros((TABLE - 2 * head - len(rows), width), F32))
    small_out[0, 2 * head :] = jnp.concatenate(rows, axis=0).astype(BF16)
    through_gate = mm(gate_back_ref[0], gate_weight_ref[0, 0], 1, 1)
    through_input = mm(input_back, input_weight_ref[0, 0], 1, 1)

    @pl.when(step == 0)
    def _():
        acc[...] = through_input

    @pl.when(step > 0)
    def _():
        acc[...] += through_input

    acc[HALO:] += through_gate

    @pl.when(step == pl.num_programs(0) - 1)
    def _():
        normed_grad_out[...] = acc[...]


def mix_back(
    weights, inputs, gate_back, kept, scan, adj, carry, mask, gates, vec, edge, backs, ahead, after
):
    shards, _, count, width = scan.shape
    model = weights.shape[2]
    head = gates.shape[1] // 2
    depth = len(backs)

    def flat(*shape):
        return pl.BlockSpec(shape, lambda s: (0,) * len(shape))

    def at(*shape):
        return pl.BlockSpec((1,) + shape, lambda s: (s,) + (0,) * len(shape))

    def ahead_spec(shift):
        return pl.BlockSpec((1, 8, width), lambda s: ((s + shift) % shards, 0, 0))

    return launch(
        functools.partial(mix_back_kernel, head, depth),
        [
            weights, weights, inputs, gate_back, kept, scan, adj, carry, mask, gates, vec,
            edge, *backs, *ahead,
        ],
        [
            pl.BlockSpec((1, 1, model, width), lambda s: (s, 0, 0, 0)),
            pl.BlockSpec((1, 1, model, width), lambda s: (s, 1, 0, 0)),
            at(count + HALO, width),
            at(count, width),
            at(3, count, width),
            at(2, count, width),
            at(2, count, width),
            at(8, width),
            flat(*mask.shape),
            at(2 * head, width),
            at(8, width),
            at(8, width),
        ]
        + [ahead_spec(i + 1) for i in range(depth)]
        + [ahead_spec(i + 1) for i in range(depth - 1)],
        0.1,
        after,
        grid=(shards,),
        out_shape=[
            jax.ShapeDtypeStruct((shards, count + HALO, width), BF16),
            jax.ShapeDtypeStruct((shards, TABLE, width), BF16),
            jax.ShapeDtypeStruct((count + HALO, model), F32),
        ],
        out_specs=[at(count + HALO, width), at(TABLE, width), flat(count + HALO, model)],
        scratch_shapes=[pltpu.VMEM((count + HALO, model), F32)],
        name="mix_back",
    )


def home_kernel(groups, shards, place_ref, *rest):
    parts, rest = rest[: groups * shards], rest[groups * shards :]
    if len(rest) == 1:
        (out,) = rest
        start = 0
        for group in range(groups):
            refs = parts[group * shards : (group + 1) * shards]
            size = refs[0].shape[0]
            total = refs[0][...].astype(F32)
            for ref in refs[1:]:
                total = total + ref[...].astype(F32)
            out[start : start + size] = total.astype(BF16)
            start += size
        return
    grads_ref, out, lines = rest
    rows = parts[0].shape[0]
    size = rows - lines.shape[1]
    total = parts[0][:size].astype(F32)
    for ref in parts[1:]:
        total = total + ref[:size].astype(F32)
    total = total.astype(BF16)
    for s in range(shards):
        lines[s] = parts[s][size:].astype(F32)
    model = lines.shape[1] // 4 * gain_chunk(0, lines.shape[2])
    gains = None
    for owner in range(shards):
        which = lax.rem(owner - place_ref[0] + shards, shards)
        value = unpack_gains(lines[which], model)
        gains = value if gains is None else [a + b for a, b in zip(gains, value, strict=True)]
    gains = pack_gains(gains, lines.shape[2])
    for quad in range(out.shape[0]):
        out[quad, :size] = total
        out[quad, size:rows] = gains
        out[quad, rows:] = grads_ref[quad]


def home_sum(place, groups, extra, grads=None, after=()):
    shards = len(groups[0])
    rows = sum(group[0].shape[0] for group in groups)
    width = groups[0][0].shape[1]
    inputs = [place, *[part for group in groups for part in group]]
    shape = (rows, width)
    if grads is not None:
        inputs.append(grads)
        shape = (grads.shape[0], rows + grads.shape[1], width)
    return launch(
        functools.partial(home_kernel, len(groups), shards),
        inputs,
        [smem()] + [vmem()] * (len(inputs) - 1),
        0.1,
        after,
        out_shape=[jax.ShapeDtypeStruct(shape, BF16)],
        out_specs=[vmem()],
        scratch_shapes=[pltpu.VMEM((shards, extra, width), F32)] if extra else [],
        name="home_sum",
        vmem_mib=16,
    )[0]


def assemble_one_kernel(core_ref, own_ref, other_ref, gate_out, out_out, whole):
    quads, rows, _ = own_ref.shape
    block = rows // 2
    for quad in range(quads):
        for ref, who in ((own_ref, core_ref[0]), (other_ref, 1 - core_ref[0])):
            start = pl.multiple_of((quad * 2 + who) * block, block)
            gate_out[pl.ds(start, block), :] = ref[quad, :block].astype(F32)
            whole[pl.ds(start, block), :] = ref[quad, block:].astype(F32)
    out_out[...] = whole[...].T


def assemble_one(core, own, other):
    quads, rows, width = own.shape
    model = quads * rows
    return launch(
        assemble_one_kernel,
        [core, own, other],
        [smem(), vmem(), vmem()],
        0.1,
        out_shape=[
            jax.ShapeDtypeStruct((model, width), F32),
            jax.ShapeDtypeStruct((width, model), F32),
        ],
        out_specs=[vmem()] * 2,
        scratch_shapes=[pltpu.VMEM((model, width), F32)],
        name="assemble_one",
        vmem_mib=16,
    )


def assemble_kernel(
    rows_total,
    core_ref,
    own_ref,
    other_ref,
    decay_ref,
    input_out,
    recall_out,
    admit_out,
    recall_bias_out,
    admit_bias_out,
    taps_out,
    bias_out,
    decay_out,
    mean_out,
    gain_one_out,
    gain_two_out,
    *rest,
):
    *grads_out, small = rest
    quads, rows, width = other_ref.shape
    piece, hidden = grads_out[0].shape
    parts = hidden // (quads * width)
    for quad in range(quads):
        for part in range(3):
            for i in range(parts):
                start = rows + (part * parts + i) * piece
                first = (quad * parts + i) * width
                grads_out[part][:, first : first + width] = own_ref[
                    quad, start : start + piece
                ].astype(F32)
    model = input_out.shape[0]
    block = model // (2 * quads)
    extra = TABLE // (2 * quads)
    for quad in range(quads):
        for ref, who in ((own_ref, core_ref[0]), (other_ref, 1 - core_ref[0])):
            start = pl.multiple_of((quad * 2 + who) * block, block)
            input_out[pl.ds(start, block), :] = ref[quad, :block].astype(F32)
            start = pl.multiple_of((quad * 2 + who) * extra, extra)
            small[pl.ds(start, extra), :] = ref[quad, block : block + extra].astype(F32)
    heads, head, _ = recall_out.shape
    lines = small[2 * head : 2 * head + 16]
    for h in range(heads):
        cols = slice(h * head, (h + 1) * head)
        recall_out[h] = small[:head, cols]
        admit_out[h] = small[head : 2 * head, cols]
        recall_bias_out[h : h + 1] = lines[5:6, cols]
        admit_bias_out[h : h + 1] = lines[6:7, cols]
    taps_out[...] = lines[:4]
    bias_out[...] = lines[4]
    decay_out[...] = lines[7] * (STRENGTH * jax.nn.sigmoid(-decay_ref[...]))
    mean_out[...] = lines[8] * (1.0 / rows_total)
    gains = None
    for ref in (own_ref, other_ref):
        part = None
        for quad in range(quads):
            value = unpack_gains(ref[quad, block + extra : rows], model)
            part = value if part is None else [a + b for a, b in zip(part, value, strict=True)]
        gains = part if gains is None else [a + b for a, b in zip(gains, part, strict=True)]
    gain_one_out[...] = gains[0].reshape(model)
    gain_two_out[...] = gains[1].reshape(model)


def assemble(core, own, other, decay, model, heads, head, rows_total, piece):
    width = own.shape[2]
    hidden = own.shape[0] * (own.shape[1] - other.shape[1]) * width // (3 * piece)
    shapes = [
        (model, width),
        (heads, head, head),
        (heads, head, head),
        (heads, head),
        (heads, head),
        (4, width),
        (width,),
        (width,),
        (width,),
        (model,),
        (model,),
        (piece, hidden),
        (piece, hidden),
        (piece, hidden),
    ]
    return launch(
        functools.partial(assemble_kernel, rows_total),
        [core, own, other, decay],
        [smem(), vmem(), vmem(), vmem()],
        0.1,
        out_shape=[jax.ShapeDtypeStruct(shape, F32) for shape in shapes],
        out_specs=[vmem()] * len(shapes),
        scratch_shapes=[pltpu.VMEM((TABLE, width), F32)],
        name="assemble",
        vmem_mib=16,
    )


def on_device(
    tokens,
    doc_ids,
    cotangent,
    norm_gain,
    gate_proj,
    input_proj,
    conv_weight,
    conv_bias,
    recall_weight,
    recall_bias,
    admit_weight,
    admit_bias,
    decay_param,
    out_proj,
    mlp_gain,
    mlp_gate,
    mlp_up,
    mlp_down,
):
    count, model = tokens.shape
    width = gate_proj.shape[1]
    heads, head, _ = recall_weight.shape
    hidden_width = mlp_gate.shape[1]
    piece = mlp_gate.shape[0]
    quads = lax.axis_size("quad")
    shards = lax.axis_size("chan")
    group = 2 * quads
    quad = lax.axis_index("quad").astype(jnp.int32)
    core = lax.axis_index("core").astype(jnp.int32)
    place = lax.axis_index("chan").astype(jnp.int32)
    quad_one, core_one = quad.reshape(1), core.reshape(1)

    def hop(values, rel):
        return lax.ppermute(values, "quad", [(i, i ^ rel) for i in range(quads)])

    def swap(values):
        return lax.ppermute(values, "core", [(0, 1), (1, 0)])

    def along(values, shift):
        return lax.ppermute(values, "chan", [(i, (i + shift) % shards) for i in range(shards)])

    def share(values):
        every = jnp.broadcast_to(values[None], (quads,) + values.shape)
        return lax.all_to_all(every, "quad", 0, 0, tiled=True)

    slots = (quad * 2 + core).reshape(1)
    arriving = jnp.stack([(quad ^ rel) * 2 for rel in range(quads)])
    arriving = jnp.concatenate([arriving + core, arriving + 1 - core])

    def halves(values, made):
        if made:
            return made
        rows = values.shape[0]
        split = values.reshape(rows, quads, 2, model // group)
        return [
            lax.dynamic_index_in_dim(split, who, 2, False).reshape(rows, model // 2)
            for who in (core, 1 - core)
        ]

    ends = along(tokens[count - HALO :], 1)
    own_weights, own_table, pieces = prepare(
        slots,
        gate_proj,
        input_proj,
        out_proj,
        recall_weight,
        recall_bias,
        admit_weight,
        admit_bias,
        conv_weight,
        conv_bias,
        decay_param,
        group,
    )
    arrived = along(pieces, 1)
    normed, *made = norm(core_one, ends, tokens, norm_gain, group)

    offset = place * count
    spots = (offset + jnp.arange(count)) % LENGTH
    padded = jnp.concatenate([jnp.full((HALO,), -1, jnp.int32), doc_ids])
    here = lax.dynamic_slice_in_dim(padded, offset + HALO, count)
    columns = [jnp.ones((count,), F32)]
    for shift in range(1, 4):
        moved = lax.dynamic_slice_in_dim(padded, offset + HALO - shift, count)
        columns.append(((spots >= shift) & (here == moved)).astype(F32))
    columns += [jnp.zeros((count,), F32)] * 4
    mask = jnp.stack(columns, axis=1)

    own_width = hidden_width // quads
    slices = jnp.stack([mlp_gate, mlp_up, mlp_down])
    slices = slices.reshape(3, piece, quads, own_width).transpose(2, 0, 1, 3)
    def local(shard, weight_pieces, stacks, after=()):
        return mix_local(
            shard, shards, head, arriving, normed, mask, weight_pieces, stacks, after
        )

    normed_own, normed_other = halves(normed, made)
    normed_other = swap(normed_other)
    stacks, _ = local(0, [own_weights, own_table], None)
    (slices,) = fence([slices], [pieces])
    slices = lax.all_to_all(slices, "quad", 0, 0, tiled=True)
    near = quads // 2 + 1
    cots = [cotangent] + [hop(cotangent, rel) for rel in range(1, near)]
    gathered, waits, edges, shard_pieces = None, [normed_other, *cots[1:]], [stacks[5]], []
    for s in range(1, shards + 1):
        onward = [arrived] if s < shards else [cotangent]
        if s == min(2, shards - 1):
            onward.append(slices)
        if s == 1:
            arrived, *onward = fence(onward, waits)
        else:
            packed, arrived, *onward = pack(held, onward, [edges[s - 2]])
            stacks, _ = local(s - 1, [packed, swap(packed)], stacks)
            edges.append(stacks[5])
        if onward:
            gathered = lax.all_gather(onward[0], "chan", axis=0)
        if s == shards:
            cots += [hop(arrived, rel) for rel in range(near, quads)]
            break
        held = [arrived] + [hop(arrived, rel) for rel in range(1, quads)]
        if s < shards - 1:
            arrived = along(arrived, 1)
    weights, inputs, gated, kept, scan, edge, gates, vec = stacks
    (edge,) = fence([edge], cots[near:])
    depth = LENGTH // count - 1
    behind = [along(edge, i + 1) for i in range(depth)]
    (gathered,) = fence([gathered], behind)
    carry, branch_in, middle, second, again = branch(
        scan, gated, weights, tokens, mlp_gain.reshape(1, model), behind, []
    )
    mlp_weights = arrange(core_one, gathered, swap(gathered), [second])
    ahead = [along(edge, -(i + 1)) for i in range(depth - 1)]
    branch_in_other = swap(branch_in)

    gate_grads, up_grads, hiddens, backs, seconds = [], [], [], [], []
    for rel in range(quads):
        if rel == 0:
            seconds.append(second)
        else:
            seconds.append(hop(second if rel < near else again, rel))
        gate_grad, up_grad, hidden, back, *carry_on = mlp_block(
            seconds[rel], cots[rel], mlp_weights,
            backs[-1:] if rel else [*ahead, branch_in_other], [] if rel else [again],
        )
        if rel == 0:
            (again,) = carry_on
        gate_grads.append(gate_grad)
        up_grads.append(up_grad)
        hiddens.append(hidden)
        backs.append(back)
    backs = [hop(back, rel) if rel else back for rel, back in enumerate(backs)]
    own_grads, other_grads, results = mlp_grads(
        quad_one, core_one, mlp_weights, cots, seconds, gate_grads, up_grads, hiddens, shards
    )
    results = lax.all_to_all(results, "quad", 0, 0, tiled=True)
    block_out = (middle + jnp.sum(results.astype(F32), axis=0)).astype(BF16)
    middle_grad, branch_grad, gain_two, *made, own_grads, other_grads = middle_back(
        backs, middle, cotangent, mlp_gain, core_one, group, [], [own_grads, other_grads]
    )

    def spread(chip):
        return lax.all_to_all(chip, "quad", 0, 0, tiled=True)

    def add_up(arrived):
        return jnp.sum(arrived.astype(F32), axis=0)

    grad_own, grad_other = halves(branch_grad, made)
    gate_back, adj, edge_back = adjoint(
        branch_grad, weights, gated, scan, kept, carry, mask, vec, []
    )
    edges_back = [along(edge_back, -(i + 1)) for i in range(depth)]
    (chip_one,) = outer(
        core_one,
        quads,
        [
            normed_own,
            normed_other,
            gate_back,
            swap(gate_back),
            grad_own,
            swap(grad_other),
            branch_in,
            branch_in_other,
        ],
    )
    (chip_one,) = fence([chip_one], [*edges_back, results])
    grads = add_pair(own_grads, swap(other_grads), edges_back)
    grads = lax.psum_scatter(grads, "chan", scatter_dimension=0)

    def home(totals):
        return [totals[0]] + [along(totals[s].astype(BF16), -s) for s in range(1, shards)]

    arrived_one = spread(chip_one)
    input_back, small, normed_grad = mix_back(
        weights, inputs, gate_back, kept, scan, adj, carry, mask, gates, vec, edge, edges_back, ahead,
        [chip_one],
    )

    halo_grad = along(normed_grad[:HALO].astype(BF16), -1)
    inside = ((place + 1) * count % LENGTH != 0).astype(jnp.int32).reshape(1)
    grad_tokens, lines = tokens_back(
        inside, normed_grad, halo_grad, tokens, norm_gain, middle_grad, gain_two, width
    )
    (chip_two,) = outer(
        core_one,
        quads,
        [normed_own, normed_other, input_back, swap(input_back)],
        [small, swap(small)],
    )
    (chip_two,) = fence([chip_two], [arrived_one])
    extra = lines.shape[0]
    totals = add_up(spread(chip_two))
    one = home_sum(place.reshape(1), [home(add_up(arrived_one))], 0)
    (one,) = fence([one], [totals, lines])
    own_one = share(one)
    totals = jnp.concatenate(
        [totals, jnp.broadcast_to(lines.astype(F32)[None], (shards, extra, width))], axis=1
    )
    parts = own_width // width
    grads = grads.reshape(quads, 3, piece, parts, width).transpose(0, 1, 3, 2, 4)
    grads = grads.reshape(quads, 3 * parts * piece, width)
    two = home_sum(place.reshape(1), [home(totals)], extra, grads, [own_one, block_out])
    own_two = lax.all_to_all(two, "quad", 0, 0, tiled=True)
    size = totals.shape[1]
    grad_gate, grad_out = assemble_one(core_one, own_one, swap(own_one))
    (own_two,) = fence([own_two], [grad_gate])
    (
        grad_input,
        grad_recall,
        grad_admit,
        grad_recall_bias,
        grad_admit_bias,
        grad_taps,
        grad_bias,
        grad_decay,
        gate_mean,
        gain_one,
        gain_two,
        *grads,
    ) = assemble(
        core_one,
        own_two,
        swap(own_two[:, :size]),
        decay_param,
        model,
        heads,
        head,
        count * group * shards,
        piece,
    )
    return (
        block_out,
        grad_tokens,
        gain_one,
        grad_gate,
        grad_input,
        grad_taps,
        grad_bias,
        grad_recall,
        grad_recall_bias,
        grad_admit,
        grad_admit_bias,
        grad_decay,
        grad_out,
        gain_two,
        grads[0],
        grads[1],
        grads[2],
        gate_mean,
    )


def solution(mesh):
    in_specs = (
        P(("quad", "core", "chan"), None),
        P(("quad", "core")),
        P(("quad", "core", "chan"), None),
        P(),
        P(None, "chan"),
        P(None, "chan"),
        P(None, "chan"),
        P("chan"),
        P("chan", None, None),
        P("chan", None),
        P("chan", None, None),
        P("chan", None),
        P("chan"),
        P("chan", None),
        P(),
        P(("quad", "core", "chan"), None),
        P(("quad", "core", "chan"), None),
        P(("quad", "core", "chan"), None),
    )
    out_specs = (
        P(("quad", "core", "chan"), None),
        P(("quad", "core", "chan"), None),
        P(),
        P(None, "chan"),
        P(None, "chan"),
        P(None, "chan"),
        P("chan"),
        P("chan", None, None),
        P("chan", None),
        P("chan", None, None),
        P("chan", None),
        P("chan"),
        P("chan", None),
        P(),
        P(("quad", "core", "chan"), None),
        P(("quad", "core", "chan"), None),
        P(("quad", "core", "chan"), None),
        P("chan"),
    )
    devices = mesh.devices
    quads, shards = devices.shape[0] // 2, devices.shape[1]
    split = jax.sharding.Mesh(devices.reshape(quads, 2, shards), ("quad", "core", "chan"))
    return jax.shard_map(
        on_device, mesh=split, in_specs=in_specs, out_specs=out_specs, check_vma=False
    )
```

```python
import functools

import jax
import jax.numpy as jnp
from jax import lax
from jax.experimental import pallas as pl
from jax.experimental.pallas import tpu as pltpu
from jax.sharding import PartitionSpec as P

LENGTH = 1024
EPS = 1e-06
STRENGTH = 8.0
HALO = 16
TABLE = 256
COST = 0.3
GELU_A = 0.7978845608028654
GELU_B = 0.044715
BF16 = jnp.bfloat16
F32 = jnp.float32
MIB = 1024 * 1024


def mm(left, right, left_dim, right_dim):
    return lax.dot_general(
        left, right, (((left_dim,), (right_dim,)), ((), ())), preferred_element_type=F32
    )


def gelu_parts(value):
    square = value * value
    th = jnp.tanh(GELU_A * value * (1.0 + GELU_B * square))
    half = 0.5 * (1.0 + th)
    slope = half + 0.5 * value * (1.0 - th * th) * (GELU_A * (1.0 + 3.0 * GELU_B * square))
    return value * half, slope


def gelu(value):
    th = jnp.tanh(GELU_A * value * (1.0 + GELU_B * value * value))
    return 0.5 * value * (1.0 + th)


def one_minus_exp(v):
    series = v * (
        1.0
        - v
        * (1 / 2)
        * (
            1.0
            - v
            * (1 / 3)
            * (1.0 - v * (1 / 4) * (1.0 - v * (1 / 5) * (1.0 - v * (1 / 6) * (1.0 - v * (1 / 7)))))
        )
    )
    return jnp.where(v < 0.4, series, 1.0 - jnp.exp(-v))


def rows_index(shape):
    return lax.broadcasted_iota(jnp.int32, shape, 0)


def scan_down(a, b):
    count = a.shape[0]
    index = rows_index(a.shape)
    step = 1
    while step < count:
        if step < 8:
            inside = index >= step
            a_prev = jnp.where(inside, pltpu.roll(a, step, 0), 1.0)
            b_prev = jnp.where(inside, pltpu.roll(b, step, 0), 0.0)
        else:
            a_prev = jnp.concatenate([jnp.ones_like(a[:step]), a[: count - step]], axis=0)
            b_prev = jnp.concatenate([jnp.zeros_like(b[:step]), b[: count - step]], axis=0)
        b = b + a * b_prev
        a = a * a_prev
        step *= 2
    return a, b


def scan_up(a, b):
    count = a.shape[0]
    index = rows_index(a.shape)
    step = 1
    while step < count:
        if step < 8:
            inside = index < count - step
            a_next = jnp.where(inside, pltpu.roll(a, count - step, 0), 1.0)
            b_next = jnp.where(inside, pltpu.roll(b, count - step, 0), 0.0)
        else:
            a_next = jnp.concatenate([a[step:], jnp.ones_like(a[:step])], axis=0)
            b_next = jnp.concatenate([b[step:], jnp.zeros_like(b[:step])], axis=0)
        b = b + a * b_next
        a = a * a_next
        step *= 2
    return a, b


def same_block(width, head):
    row = lax.broadcasted_iota(jnp.int32, (width, 1), 0) // head
    col = lax.broadcasted_iota(jnp.int32, (1, width), 1) // head
    return row == col


def block_diagonal(flat, head, dtype):
    width = flat.shape[1]
    tall = jnp.concatenate([flat] * (width // head), axis=0)
    shape = (width, width)
    del shape
    return jnp.where(same_block(width, head), tall, 0.0).astype(dtype)


def fold_diagonal(square, head):
    width = square.shape[0]
    kept = jnp.where(same_block(width, head), square, 0.0)
    total = kept[:head]
    for start in range(head, width, head):
        total = total + kept[start : start + head]
    return total


def vmem():
    return pl.BlockSpec(memory_space=pltpu.VMEM)


def smem():
    return pl.BlockSpec(memory_space=pltpu.SMEM)


def launch(
    kernel,
    inputs,
    in_specs,
    micros,
    after=(),
    carry=(),
    prefetch=0,
    grid=(),
    out_shape=(),
    out_specs=(),
    scratch_shapes=(),
    aliases=None,
    name=None,
    vmem_mib=60,
):
    count, extra, through = len(inputs), len(after), len(carry)
    made = len(out_shape)
    aliases = dict(aliases or {})
    for i in range(through):
        aliases[count + extra + i] = made + i

    def body(*refs):
        first = count + extra + through
        kernel(*refs[:count], *refs[first : first + made], *refs[first + made + through :])

    anywhere = pl.BlockSpec(memory_space=pl.ANY)
    return pl.pallas_call(
        body,
        out_shape=list(out_shape) + [jax.ShapeDtypeStruct(c.shape, c.dtype) for c in carry],
        grid_spec=pltpu.PrefetchScalarGridSpec(
            num_scalar_prefetch=prefetch,
            grid=grid,
            in_specs=list(in_specs) + [anywhere] * (extra + through),
            out_specs=list(out_specs) + [anywhere] * through,
            scratch_shapes=scratch_shapes,
        ),
        input_output_aliases=aliases,
        compiler_params=pltpu.CompilerParams(vmem_limit_bytes=vmem_mib * MIB),
        cost_estimate=pl.CostEstimate(
            flops=int(micros * 1.1e9 * COST), bytes_accessed=int(micros * 3.5e6 * COST), transcendentals=0
        ),
        name=name,
    )(*inputs, *after, *carry)


def split_features(core, source, own_out, other_out):
    half = own_out.shape[1]
    block = 128
    quads = half // block
    for quad in range(quads):
        for out, who in ((own_out, core), (other_out, 1 - core)):
            start = pl.multiple_of((quad * 2 + who) * block, block)
            out[:, quad * block : (quad + 1) * block] = source[:, pl.ds(start, block)]


def pack_kernel(*refs):
    *pieces, out = refs
    for i, ref in enumerate(pieces):
        out[i] = ref[0]


def pack(pieces, carry, after):
    return launch(
        pack_kernel,
        pieces,
        [vmem()] * len(pieces),
        0.1,
        after,
        carry,
        out_shape=[jax.ShapeDtypeStruct((len(pieces),) + pieces[0].shape[1:], pieces[0].dtype)],
        out_specs=[vmem()],
        name="pack",
        vmem_mib=8,
    )


def fence(carry, after=()):
    return launch(lambda *refs: None, [], [], 0.01, after, carry, name="fence", vmem_mib=60)


def prepare_kernel(
    slots_ref,
    gate_ref,
    input_ref,
    out_ref,
    recall_ref,
    recall_bias_ref,
    admit_ref,
    admit_bias_ref,
    taps_ref,
    bias_ref,
    decay_ref,
    weights,
    table_out,
    pieces_out,
    table,
):
    weights[0] = gate_ref[...]
    weights[1] = input_ref[...]
    weights[2] = out_ref[...].T
    heads, head, _ = recall_ref.shape
    for h in range(heads):
        cols = slice(h * head, (h + 1) * head)
        table[:head, cols] = recall_ref[h]
        table[head : 2 * head, cols] = admit_ref[h]
    side = jnp.concatenate
    lines = side(
        [
            taps_ref[...],
            bias_ref[...].reshape(1, -1),
            side([recall_bias_ref[h : h + 1] for h in range(heads)], axis=1),
            side([admit_bias_ref[h : h + 1] for h in range(heads)], axis=1),
            jax.nn.softplus(-decay_ref[...].reshape(1, -1)),
        ],
        axis=0,
    )
    high = lines.astype(BF16).astype(F32)
    rest = lines - high
    mid = rest.astype(BF16).astype(F32)
    table[2 * head : 2 * head + 8] = high
    table[2 * head + 8 : 2 * head + 16] = mid
    table[2 * head + 16 : 2 * head + 24] = rest - mid
    table[2 * head + 24 :] = jnp.zeros((table.shape[0] - 2 * head - 24, table.shape[1]), F32)
    table_out[...] = table[...].astype(BF16)
    count, rows, _ = pieces_out.shape
    block = pieces_block(weights.shape[1], rows)
    extra = rows - 3 * block
    for k in range(count):
        start = pl.multiple_of(slots_ref[k] * block, block)
        for part in range(3):
            pieces_out[k, part * block : (part + 1) * block] = weights[part, pl.ds(start, block), :]
        start = pl.multiple_of(slots_ref[k] * extra, extra)
        pieces_out[k, 3 * block :] = table_out[pl.ds(start, extra), :]

def norm_kernel(core_ref, ends_ref, tokens_ref, gain_ref, normed_out, *halves_out):
    for ref, rows in ((ends_ref, slice(0, HALO)), (tokens_ref, slice(HALO, None))):
        values = ref[...].astype(F32)
        scale = lax.rsqrt(jnp.mean(values * values, axis=1, keepdims=True) + EPS)
        normed_out[rows] = (values * scale * gain_ref[...]).astype(BF16)
    if halves_out:
        split_features(core_ref[0], normed_out, *halves_out)


def norm(core, ends, tokens, gain, group):
    count, model = tokens.shape
    halves = half_shapes(HALO + count, model, group)
    return launch(
        norm_kernel,
        [core, ends, tokens, gain.reshape(1, model)],
        [smem()] + [vmem()] * 3,
        0.1,
        out_shape=[jax.ShapeDtypeStruct((HALO + count, model), BF16)] + halves,
        out_specs=[vmem()] * (1 + len(halves)),
        name="norm",
        vmem_mib=16,
    )


def pieces_block(model, rows):
    return rows * model // (3 * model + TABLE)


def half_shapes(rows, model, group):
    return [jax.ShapeDtypeStruct((rows, model // 2), BF16)] * (2 if model // group == 128 else 0)


def prepare(slots, gate, inputs, out, recall, recall_bias, admit, admit_bias, taps, bias, decay, group):
    model, width = gate.shape
    rows = (3 * model + TABLE) // group
    return launch(
        prepare_kernel,
        [slots, gate, inputs, out, recall, recall_bias, admit, admit_bias, taps, bias, decay],
        [smem()] + [vmem()] * 10,
        0.1,
        out_shape=[
            jax.ShapeDtypeStruct((3, model, width), BF16),
            jax.ShapeDtypeStruct((TABLE, width), BF16),
            jax.ShapeDtypeStruct((slots.shape[0], rows, width), BF16),
        ],
        out_specs=[vmem()] * 3,
        scratch_shapes=[pltpu.VMEM((TABLE, width), F32)],
        name="prepare",
    )


def mix_local_kernel(own, head, counts, stacked, slots_ref, normed_ref, mask_ref, *rest):
    piece_refs, rest = rest[: len(counts)], rest[len(counts) :]
    weights, inputs_out, gated_out, kept_out, scan_out, edge_out, gates_out, vec_out = rest[
        stacked : stacked + 8
    ]
    (table,) = rest[stacked + 8 :]
    model = normed_ref.shape[1]
    if own:
        weights[0] = piece_refs[0][...]
        table[...] = piece_refs[1][...].astype(F32)
    else:
        number = 0
        for ref, many in zip(piece_refs, counts, strict=True):
            rows = ref.shape[1]
            block = pieces_block(model, rows)
            extra = rows - 3 * block
            for k in range(many):
                slot = slots_ref[number]
                number += 1
                start = pl.multiple_of(slot * block, block)
                for part in range(3):
                    weights[0, part, pl.ds(start, block), :] = ref[
                        k, part * block : (part + 1) * block
                    ]
                start = pl.multiple_of(slot * extra, extra)
                table[pl.ds(start, extra), :] = ref[k, 3 * block :].astype(F32)
    count = mask_ref.shape[0]
    vec = table[2 * head : 2 * head + 8] + (
        table[2 * head + 8 : 2 * head + 16] + table[2 * head + 16 : 2 * head + 24]
    )
    vec_out[0] = vec
    gates_out[0] = table[: 2 * head].astype(BF16)
    gated = mm(normed_ref[HALO:], weights[0, 0], 1, 0).astype(BF16)
    gated_out[0] = gated
    inputs = mm(normed_ref[...], weights[0, 1], 1, 0).astype(BF16)
    inputs_out[0] = inputs
    wide = inputs.astype(F32)
    conv = vec[4:5] + vec[0:1] * wide[HALO:]
    for shift in range(1, 4):
        moved = pltpu.roll(wide, shift, 0)[HALO:]
        conv = conv + vec[shift : shift + 1] * (moved * mask_ref[:, shift : shift + 1])
    low = conv.astype(BF16)
    recall_weight = block_diagonal(table[:head], head, BF16)
    admit_weight = block_diagonal(table[head : 2 * head], head, BF16)
    recall = jax.nn.sigmoid(mm(low, recall_weight, 1, 0) + vec[5:6])
    admit = jax.nn.sigmoid(mm(low, admit_weight, 1, 0) + vec[6:7])
    rate = STRENGTH * recall * vec[7:8]
    decay = jnp.exp(-rate)
    inject = jnp.sqrt(one_minus_exp(2.0 * rate)) * admit * conv
    product, state = scan_down(decay * mask_ref[:, 1:2], inject)
    kept_out[0, 0] = conv
    kept_out[0, 1] = recall
    kept_out[0, 2] = admit
    scan_out[0, 0] = product
    scan_out[0, 1] = state
    edge_out[0, 0:1] = product[count - 1 :]
    edge_out[0, 1:2] = state[count - 1 :]
    edge_out[0, 2:3] = jnp.sum(decay, axis=0, keepdims=True)


def mix_local(shard, shards, head, slots, normed, mask, pieces, stacks, after=(), carry=()):
    count = mask.shape[0]
    model = normed.shape[1]
    width = pieces[0].shape[-1]
    own = shard == 0
    counts = [p.shape[0] for p in pieces]
    shapes = [
        ((shards, 3, model, width), BF16),
        ((shards, count + HALO, width), BF16),
        ((shards, count, width), BF16),
        ((shards, 3, count, width), F32),
        ((shards, 2, count, width), F32),
        ((shards, 8, width), F32),
        ((shards, 2 * head, width), BF16),
        ((shards, 8, width), F32),
    ]

    def at(shape):
        tail = (0,) * (len(shape) - 1)
        return pl.BlockSpec((1,) + shape[1:], lambda i: (shard,) + tail)

    first = [slots, normed, mask, *pieces]
    in_specs = [smem()] + [vmem()] * (len(first) - 1)
    aliases = {}
    if stacks is not None:
        aliases = {len(first) + i: i for i in range(len(stacks))}
        in_specs += [pl.BlockSpec(memory_space=pl.ANY)] * len(stacks)
        first += list(stacks)
    outs = launch(
        functools.partial(mix_local_kernel, own, head, counts, len(aliases)),
        first,
        in_specs,
        5.7,
        after=after,
        carry=carry,
        grid=(1,),
        out_shape=[jax.ShapeDtypeStruct(shape, dtype) for shape, dtype in shapes],
        out_specs=[at(shape) for shape, _ in shapes],
        scratch_shapes=[pltpu.VMEM((TABLE, width), F32)],
        aliases=aliases,
        name="mix_local",
    )
    return outs[:8], outs[8:]


def carried(edges):
    total = edges[-1][0, 1:2]
    for edge in edges[-2::-1]:
        total = edge[0, 1:2] + edge[0, 0:1] * total
    return total


def branch_kernel(
    depth, scan_ref, gated_ref, weight_ref, resid_ref, gain_ref, *rest
):
    edges = rest[:depth]
    carry_out, branch_in_out, middle_out, second_out, again_out, acc = rest[depth:]
    step = pl.program_id(0)

    @pl.when(step == 0)
    def _():
        acc[...] = resid_ref[...].astype(F32)

    carry = carried(edges)
    carry_out[0] = jnp.broadcast_to(carry, carry_out.shape[1:])
    state = scan_ref[0, 1] + scan_ref[0, 0] * carry
    mixed = (gelu(gated_ref[0].astype(F32)) * state).astype(BF16)
    branch_in_out[0] = mixed
    acc[...] += mm(mixed, weight_ref[0, 0], 1, 1)

    @pl.when(step == pl.num_programs(0) - 1)
    def _():
        middle = acc[...]
        middle_out[...] = middle
        scale = lax.rsqrt(jnp.mean(middle * middle, axis=1, keepdims=True) + EPS)
        second = (middle * scale * gain_ref[...]).astype(BF16)
        second_out[...] = second
        again_out[...] = second


def branch(scan, gated, weights, tokens, gain, edges, after):
    shards, _, count, width = scan.shape
    model = tokens.shape[1]

    def edge_spec(shift):
        return pl.BlockSpec((1, 8, width), lambda s: ((s + shards - shift % shards) % shards, 0, 0))

    return launch(
        functools.partial(branch_kernel, len(edges)),
        [scan, gated, weights, tokens, gain, *edges],
        [
            pl.BlockSpec((1, 2, count, width), lambda s: (s, 0, 0, 0)),
            pl.BlockSpec((1, count, width), lambda s: (s, 0, 0)),
            pl.BlockSpec((1, 1, model, width), lambda s: (s, 2, 0, 0)),
            pl.BlockSpec((count, model), lambda s: (0, 0)),
            pl.BlockSpec((1, model), lambda s: (0, 0)),
        ]
        + [edge_spec(i + 1) for i in range(len(edges))],
        0.1,
        after,
        grid=(shards,),
        out_shape=[
            jax.ShapeDtypeStruct((shards, 8, width), F32),
            jax.ShapeDtypeStruct((shards, count, width), BF16),
            jax.ShapeDtypeStruct((count, model), F32),
            jax.ShapeDtypeStruct((count, model), BF16),
            jax.ShapeDtypeStruct((count, model), BF16),
        ],
        out_specs=[
            pl.BlockSpec((1, 8, width), lambda s: (s, 0, 0)),
            pl.BlockSpec((1, count, width), lambda s: (s, 0, 0)),
            pl.BlockSpec((count, model), lambda s: (0, 0)),
            pl.BlockSpec((count, model), lambda s: (0, 0)),
            pl.BlockSpec((count, model), lambda s: (0, 0)),
        ],
        scratch_shapes=[pltpu.VMEM((count, model), F32)],
        name="mix_branch",
    )


def arrange_kernel(core_ref, own_ref, other_ref, out_ref):
    shards, quads, _, piece, _ = own_ref.shape
    for ref, core in ((own_ref, core_ref[0]), (other_ref, 1 - core_ref[0])):
        for shard in range(shards):
            for quad in range(quads):
                start = pl.multiple_of(((quad * 2 + core) * shards + shard) * piece, piece)
                for part in range(3):
                    out_ref[part, pl.ds(start, piece), :] = ref[shard, quad, part]


def arrange(core, own, other, after):
    shards, quads, _, piece, width = own.shape
    if piece % 16:
        both = jnp.where(core[0] == 0, jnp.stack([own, other]), jnp.stack([other, own]))
        return both.transpose(3, 2, 0, 1, 4, 5).reshape(3, 2 * shards * quads * piece, width)
    return launch(
        arrange_kernel,
        [core, own, other],
        [smem(), vmem(), vmem()],
        0.1,
        after,
        out_shape=[jax.ShapeDtypeStruct((3, 2 * shards * quads * piece, width), BF16)],
        out_specs=[vmem()],
        name="mlp_arrange",
        vmem_mib=16,
    )[0]


def mlp_tiles(width):
    tile = 256 if width % 256 == 0 else width
    return [slice(start, start + tile) for start in range(0, width, tile)]


def mlp_kernel(
    second_ref,
    cot_ref,
    weight_ref,
    gate_grad_out,
    up_grad_out,
    hidden_out,
    back_out,
):
    second = second_ref[...]
    cot = cot_ref[...]
    total = None
    for cols in mlp_tiles(weight_ref.shape[2]):
        gate_weight, up_weight = weight_ref[0, :, cols], weight_ref[1, :, cols]
        gate = mm(second, gate_weight, 1, 0)
        upward = mm(second, up_weight, 1, 0)
        hidden_grad = mm(cot, weight_ref[2, :, cols], 1, 0)
        act, slope = gelu_parts(gate)
        hidden_out[:, cols] = (act * upward).astype(BF16)
        gate_grad = (hidden_grad * upward * slope).astype(BF16)
        up_grad = (hidden_grad * act).astype(BF16)
        gate_grad_out[:, cols] = gate_grad
        up_grad_out[:, cols] = up_grad
        back = mm(gate_grad, gate_weight, 1, 1) + mm(up_grad, up_weight, 1, 1)
        total = back if total is None else total + back
    back_out[...] = total.astype(BF16)


def mlp_block(second, cot, weights, after, carry):
    count, model = second.shape
    width = weights.shape[-1]
    wide = jax.ShapeDtypeStruct((count, width), BF16)
    return launch(
        mlp_kernel,
        [second, cot, weights],
        [vmem()] * 3,
        7.4,
        after,
        carry,
        out_shape=[wide, wide, wide, jax.ShapeDtypeStruct((count, model), BF16)],
        out_specs=[vmem()] * 4,
        name="mlp_block",
        vmem_mib=16,
    )


def mlp_grads_kernel(quads, quad_ref, core_ref, weight_ref, *rest):
    cots, rest = rest[:quads], rest[quads:]
    seconds, rest = rest[:quads], rest[quads:]
    gate_grads, rest = rest[:quads], rest[quads:]
    up_grads, rest = rest[:quads], rest[quads:]
    hiddens, rest = rest[:quads], rest[quads:]
    *grads_out, results_out, second, cot, left, whole_ref = rest
    count = seconds[0].shape[0]
    rows = [slice(rel * count, (rel + 1) * count) for rel in range(quads)]
    for rel in range(quads):
        second[rows[rel]] = seconds[rel][...]
        cot[rows[rel]] = cots[rel][...]
    total = None
    for cols in mlp_tiles(weight_ref.shape[2]):
        for part, (base, group) in enumerate(
            ((second, gate_grads), (second, up_grads), (cot, hiddens))
        ):
            for rel in range(quads):
                left[rows[rel]] = group[rel][:, cols]
            whole = mm(base[...], left[...], 0, 0).astype(BF16)
            if len(grads_out) == 1:
                grads_out[0][part, :, cols] = whole
                continue
            whole_ref[...] = whole
            shards, _, _, piece, _ = grads_out[0].shape
            for out, core in zip(grads_out, (core_ref[0], 1 - core_ref[0]), strict=True):
                for shard in range(shards):
                    for quad in range(quads):
                        start = pl.multiple_of(((quad * 2 + core) * shards + shard) * piece, piece)
                        out[shard, quad, part, :, cols] = whole_ref[pl.ds(start, piece), :]
        result = mm(left[...], weight_ref[2, :, cols], 1, 1)
        total = result if total is None else total + result
    for rel in range(quads):
        results_out[quad_ref[0] ^ rel] = total[rows[rel]].astype(BF16)


def mlp_grads(quad, core, weights, cots, seconds, gate_grads, up_grads, hiddens, shards):
    quads = len(seconds)
    count, model = seconds[0].shape
    width = weights.shape[2]
    tile = mlp_tiles(width)[0].stop
    piece = model // (quads * 2 * shards)
    shapes = [(shards, quads, 3, piece, width)] * 2 if piece % 16 == 0 else [(3, model, width)]
    *grads, results = launch(
        functools.partial(mlp_grads_kernel, quads),
        [quad, core, weights, *cots, *seconds, *gate_grads, *up_grads, *hiddens],
        [smem()] * 2 + [vmem()] * (1 + 5 * quads),
        15.0,
        out_shape=[jax.ShapeDtypeStruct(shape, BF16) for shape in shapes]
        + [jax.ShapeDtypeStruct((quads, count, model), BF16)],
        out_specs=[vmem()] * (1 + len(shapes)),
        scratch_shapes=[
            pltpu.VMEM((quads * count, model), BF16),
            pltpu.VMEM((quads * count, model), BF16),
            pltpu.VMEM((quads * count, tile), BF16),
            pltpu.VMEM((model, tile), BF16),
        ],
        name="mlp_grads",
        vmem_mib=32,
    )
    if piece % 16:
        both = grads[0].reshape(3, quads, 2, shards, piece, width).transpose(2, 3, 1, 0, 4, 5)
        grads = [lax.dynamic_index_in_dim(both, who, 0, False) for who in (core[0], 1 - core[0])]
    return *grads, results


def add_kernel(a_ref, b_ref, out_ref):
    out_ref[...] = (a_ref[...].astype(F32) + b_ref[...].astype(F32)).astype(BF16)


def add_pair(a, b, after=()):
    return launch(
        add_kernel,
        [a, b],
        [vmem()] * 2,
        0.1,
        after,
        out_shape=[jax.ShapeDtypeStruct(a.shape, BF16)],
        out_specs=[vmem()],
        name="add_pair",
        vmem_mib=16,
    )[0]


def middle_kernel(blocks, back_ref, *rest):
    (*backs, values_ref, cot_ref, gain_ref, core_ref), outs = rest[: blocks + 3], rest[blocks + 3 :]
    middle_grad_out, low_out, gain_out, *halves_out = outs
    grad = back_ref[...].astype(F32)
    for ref in backs:
        grad = grad + ref[...].astype(F32)
    values = values_ref[...]
    scale = lax.rsqrt(jnp.mean(values * values, axis=1, keepdims=True) + EPS)
    scaled = grad * gain_ref[...]
    inner = jnp.mean(scaled * values, axis=1, keepdims=True)
    total = cot_ref[...].astype(F32) + scale * scaled - values * (scale * scale * scale * inner)
    middle_grad_out[...] = total
    low_out[...] = total.astype(BF16)
    if halves_out:
        split_features(core_ref[0], low_out, *halves_out)
    gain_out[...] = jnp.sum(grad * values * scale, axis=0, keepdims=True)


def middle_back(backs, values, cot, gain, core, group, after, carry):
    count, model = values.shape
    halves = half_shapes(count, model, group)
    return launch(
        functools.partial(middle_kernel, len(backs)),
        [*backs, values, cot, gain.reshape(1, model), core],
        [vmem()] * (len(backs) + 3) + [smem()],
        0.1,
        after,
        carry,
        out_shape=[
            jax.ShapeDtypeStruct((count, model), F32),
            jax.ShapeDtypeStruct((count, model), BF16),
            jax.ShapeDtypeStruct((1, model), F32),
        ]
        + halves,
        out_specs=[vmem()] * (3 + len(halves)),
        name="middle_back",
        vmem_mib=16,
    )


def tokens_kernel(
    inside_ref, grad_ref, halo_ref, tokens_ref, gain_ref, middle_grad_ref, gain_two_ref, out, lines_out
):
    grad = grad_ref[HALO:]
    count = grad.shape[0]
    last = jnp.where(inside_ref[0] > 0, halo_ref[...].astype(F32), 0.0)
    grad = jnp.concatenate([grad[: count - HALO], grad[count - HALO :] + last], axis=0)
    values = tokens_ref[...].astype(F32)
    scale = lax.rsqrt(jnp.mean(values * values, axis=1, keepdims=True) + EPS)
    scaled = grad * gain_ref[...]
    inner = jnp.mean(scaled * values, axis=1, keepdims=True)
    out[...] = middle_grad_ref[...] + scale * scaled - values * (scale * scale * scale * inner)
    both = (jnp.sum(grad * values * scale, axis=0, keepdims=True), gain_two_ref[...])
    lines_out[...] = pack_gains(both, lines_out.shape[1])


def gain_chunk(model, width):
    chunk = 128
    while chunk * 2 <= width:
        chunk *= 2
    while chunk > width:
        chunk //= 2
    return chunk


def gain_lines(model, width):
    return 4 * (model // gain_chunk(model, width))


def pack_gains(both, width):
    chunk = gain_chunk(both[0].shape[1], width)
    lines = []
    for value in both:
        high = value.astype(BF16).astype(F32)
        for term in (high, value - high):
            lines += [term[:, i : i + chunk] for i in range(0, term.shape[1], chunk)]
    lines = jnp.concatenate(lines, axis=0)
    if chunk < width:
        blank = jnp.zeros((lines.shape[0], width - chunk), F32)
        lines = jnp.concatenate([lines, blank], axis=1)
    return lines.astype(BF16)


def unpack_gains(lines, model):
    chunk = gain_chunk(model, lines.shape[1])
    many = model // chunk
    lines = lines.astype(F32)
    both = []
    for i in range(2):
        value = lines[2 * i * many : (2 * i + 1) * many] + lines[
            (2 * i + 1) * many : (2 * i + 2) * many
        ]
        both.append(
            jnp.concatenate([value[j : j + 1, :chunk] for j in range(many)], axis=1)
        )
    return both


def tokens_back(inside, grad, halo, tokens, gain, middle_grad, gain_two, width, after):
    count, model = tokens.shape
    return launch(
        tokens_kernel,
        [inside, grad, halo, tokens, gain.reshape(1, model), middle_grad, gain_two],
        [smem()] + [vmem()] * 6,
        0.1,
        after,
        out_shape=[
            jax.ShapeDtypeStruct((count, model), F32),
            jax.ShapeDtypeStruct((gain_lines(model, width), width), BF16),
        ],
        out_specs=[vmem()] * 2,
        name="tokens_back",
        vmem_mib=16,
    )


def adjoint_kernel(
    grad_ref,
    weight_ref,
    gated_ref,
    scan_ref,
    kept_ref,
    carry_ref,
    mask_ref,
    vec_ref,
    gate_back_out,
    adjoint_out,
    edge_out,
):
    into = mm(grad_ref[...], weight_ref[0, 0], 1, 0).astype(BF16).astype(F32)
    act, slope = gelu_parts(gated_ref[0].astype(F32))
    state = scan_ref[0, 1] + scan_ref[0, 0] * carry_ref[0, 0:1]
    gate_back_out[0] = (into * state * slope).astype(BF16)
    decay = jnp.exp(-STRENGTH * kept_ref[0, 0] * vec_ref[0, 7:8]) * mask_ref[:, 1:2]
    count = decay.shape[0]
    shifted = jnp.where(
        rows_index(decay.shape) < count - 1, pltpu.roll(decay, count - 1, 0), 1.0
    )
    product, value = scan_up(shifted, into * act)
    adjoint_out[0, 0] = product
    adjoint_out[0, 1] = value
    edge_out[0] = jnp.broadcast_to(decay[0:1] * value[0:1], edge_out.shape[1:])


def adjoint(grad, weights, gated, scan, kept, carry, mask, vec, through):
    shards, _, count, width = scan.shape
    model = grad.shape[1]

    def flat(*shape):
        return pl.BlockSpec(shape, lambda s: (0,) * len(shape))

    def at(*shape):
        return pl.BlockSpec((1,) + shape, lambda s: (s,) + (0,) * len(shape))

    return launch(
        adjoint_kernel,
        [grad, weights, gated, scan, kept, carry, mask, vec],
        [
            flat(count, model),
            pl.BlockSpec((1, 1, model, width), lambda s: (s, 2, 0, 0)),
            at(count, width),
            at(2, count, width),
            pl.BlockSpec((1, 1, count, width), lambda s: (s, 1, 0, 0)),
            at(8, width),
            flat(*mask.shape),
            at(8, width),
        ],
        0.1,
        carry=through,
        grid=(shards,),
        out_shape=[
            jax.ShapeDtypeStruct((shards, count, width), BF16),
            jax.ShapeDtypeStruct((shards, 2, count, width), F32),
            jax.ShapeDtypeStruct((shards, 8, width), F32),
        ],
        out_specs=[at(count, width), at(2, count, width), at(8, width)],
        name="mix_adjoint",
    )


def outer_kernel(groups, core_ref, *rest):
    pairs, rest = rest[: 4 * groups], rest[4 * groups :]
    *smalls, out, left, right, small = rest
    count = pairs[2].shape[1]
    quads, shards = out.shape[:2]
    block = left.shape[1] // quads
    for group in range(groups):
        left_ref, left_other, right_ref, right_other = pairs[4 * group : 4 * group + 4]
        left[:count] = left_ref[left_ref.shape[0] - count :]
        left[count:] = left_other[left_ref.shape[0] - count :]
        for s in range(shards):
            right[:count] = right_ref[s]
            right[count:] = right_other[s]
            total = mm(left[...], right[...], 0, 0).astype(BF16)
            for quad in range(quads):
                out[quad, s, group * block : (group + 1) * block] = total[
                    quad * block : (quad + 1) * block
                ]
    if smalls:
        extra = out.shape[2] - groups * block
        for s in range(shards):
            small[...] = (smalls[0][s].astype(F32) + smalls[1][s].astype(F32)).astype(BF16)
            for quad in range(quads):
                start = pl.multiple_of((quad * 2 + core_ref[0]) * extra, extra)
                out[quad, s, groups * block :] = small[pl.ds(start, extra), :]


def outer(core, quads, pairs, smalls=(), after=(), carry=()):
    shards, count, width = pairs[2].shape
    model = pairs[0].shape[1]
    groups = len(pairs) // 4
    rows = groups * model // quads + (TABLE // (2 * quads) if smalls else 0)
    return launch(
        functools.partial(outer_kernel, groups),
        [core, *pairs, *smalls],
        [smem()] + [vmem()] * (len(pairs) + len(smalls)),
        0.1,
        after,
        carry,
        out_shape=[jax.ShapeDtypeStruct((quads, shards, rows, width), BF16)],
        out_specs=[vmem()],
        scratch_shapes=[
            pltpu.VMEM((2 * count, model), BF16),
            pltpu.VMEM((2 * count, width), BF16),
            pltpu.VMEM((TABLE, width), BF16),
        ],
        name="mix_outer",
    )


def mix_back_kernel(
    head,
    depth,
    gate_weight_ref,
    input_weight_ref,
    inputs_ref,
    gate_back_ref,
    kept_ref,
    scan_ref,
    adjoint_ref,
    carry_ref,
    mask_ref,
    gates_ref,
    vec_ref,
    edge_ref,
    *rest,
):
    backs, decays = rest[:depth], rest[depth : 2 * depth - 1]
    input_back_out, small_out, normed_grad_out, acc = rest[2 * depth - 1 :]
    step = pl.program_id(0)
    count = mask_ref.shape[0]
    width = vec_ref.shape[2]
    vec = vec_ref[0]
    incoming = backs[-1][0, 0:1]
    for back, edge in zip(backs[-2::-1], decays[::-1], strict=True):
        incoming = back[0, 0:1] + edge[0, 0:1] * incoming
    adj = adjoint_ref[0, 1] + adjoint_ref[0, 0] * incoming
    carry = carry_ref[0, 0:1]
    state = scan_ref[0, 1] + scan_ref[0, 0] * carry
    before = jnp.where(rows_index(state.shape) == 0, carry, pltpu.roll(state, 1, 0))
    conv, recall, admit = kept_ref[0, 0], kept_ref[0, 1], kept_ref[0, 2]
    speed = STRENGTH * vec[7:8]
    rate = recall * speed
    decay = jnp.exp(-rate)
    square = one_minus_exp(2.0 * rate)
    inverse = lax.rsqrt(square)
    sized = adj * (square * inverse)
    pulled = adj * admit
    log_grad = decay * (adj * before * mask_ref[:, 1:2] - pulled * conv * decay * inverse)
    recall_grad = -speed * log_grad * recall * (1.0 - recall)
    admit_grad = sized * conv * admit * (1.0 - admit)
    conv_grad = sized * admit
    recall_low = recall_grad.astype(BF16)
    admit_low = admit_grad.astype(BF16)
    gates = gates_ref[0].astype(F32)
    recall_weight = block_diagonal(gates[:head], head, BF16)
    admit_weight = block_diagonal(gates[head:], head, BF16)
    conv_grad = conv_grad + mm(recall_low, recall_weight, 1, 1) + mm(admit_low, admit_weight, 1, 1)
    wide = inputs_ref[0].astype(F32)
    blank = jnp.zeros((HALO, width), F32)
    reach = jnp.concatenate([blank, vec[0:1] * conv_grad], axis=0)
    tap_grads = [jnp.sum(conv_grad * wide[HALO:], axis=0, keepdims=True)]
    for shift in range(1, 4):
        masked = conv_grad * mask_ref[:, shift : shift + 1]
        moved = pltpu.roll(wide, shift, 0)[HALO:]
        tap_grads.append(jnp.sum(masked * moved, axis=0, keepdims=True))
        back = jnp.concatenate([blank, vec[shift : shift + 1] * masked], axis=0)
        reach = reach + pltpu.roll(back, count + HALO - shift, 0)
    input_back = reach.astype(BF16)
    conv_low = conv.astype(BF16)
    input_back_out[0] = input_back
    small_out[0, :head] = fold_diagonal(mm(conv_low, recall_low, 0, 0), head).astype(BF16)
    small_out[0, head : 2 * head] = fold_diagonal(mm(conv_low, admit_low, 0, 0), head).astype(BF16)
    rows = tap_grads + [
        jnp.sum(conv_grad, axis=0, keepdims=True),
        jnp.sum(recall_grad, axis=0, keepdims=True),
        jnp.sum(admit_grad, axis=0, keepdims=True),
        jnp.sum(recall * log_grad, axis=0, keepdims=True),
        edge_ref[0, 2:3],
    ]
    rows.append(jnp.zeros((TABLE - 2 * head - len(rows), width), F32))
    small_out[0, 2 * head :] = jnp.concatenate(rows, axis=0).astype(BF16)
    through_gate = mm(gate_back_ref[0], gate_weight_ref[0, 0], 1, 1)
    through_input = mm(input_back, input_weight_ref[0, 0], 1, 1)

    @pl.when(step == 0)
    def _():
        acc[...] = through_input

    @pl.when(step > 0)
    def _():
        acc[...] += through_input

    acc[HALO:] += through_gate

    @pl.when(step == pl.num_programs(0) - 1)
    def _():
        normed_grad_out[...] = acc[...]


def mix_back(
    weights, inputs, gate_back, kept, scan, adj, carry, mask, gates, vec, edge, backs, ahead, after
):
    shards, _, count, width = scan.shape
    model = weights.shape[2]
    head = gates.shape[1] // 2
    depth = len(backs)

    def flat(*shape):
        return pl.BlockSpec(shape, lambda s: (0,) * len(shape))

    def at(*shape):
        return pl.BlockSpec((1,) + shape, lambda s: (s,) + (0,) * len(shape))

    def ahead_spec(shift):
        return pl.BlockSpec((1, 8, width), lambda s: ((s + shift) % shards, 0, 0))

    return launch(
        functools.partial(mix_back_kernel, head, depth),
        [
            weights, weights, inputs, gate_back, kept, scan, adj, carry, mask, gates, vec,
            edge, *backs, *ahead,
        ],
        [
            pl.BlockSpec((1, 1, model, width), lambda s: (s, 0, 0, 0)),
            pl.BlockSpec((1, 1, model, width), lambda s: (s, 1, 0, 0)),
            at(count + HALO, width),
            at(count, width),
            at(3, count, width),
            at(2, count, width),
            at(2, count, width),
            at(8, width),
            flat(*mask.shape),
            at(2 * head, width),
            at(8, width),
            at(8, width),
        ]
        + [ahead_spec(i + 1) for i in range(depth)]
        + [ahead_spec(i + 1) for i in range(depth - 1)],
        0.1,
        after,
        grid=(shards,),
        out_shape=[
            jax.ShapeDtypeStruct((shards, count + HALO, width), BF16),
            jax.ShapeDtypeStruct((shards, TABLE, width), BF16),
            jax.ShapeDtypeStruct((count + HALO, model), F32),
        ],
        out_specs=[at(count + HALO, width), at(TABLE, width), flat(count + HALO, model)],
        scratch_shapes=[pltpu.VMEM((count + HALO, model), F32)],
        name="mix_back",
    )


def home_kernel(groups, shards, place_ref, *rest):
    parts, rest = rest[: groups * shards], rest[groups * shards :]
    if len(rest) == 1:
        (out,) = rest
        start = 0
        for group in range(groups):
            refs = parts[group * shards : (group + 1) * shards]
            size = refs[0].shape[0]
            total = refs[0][...].astype(F32)
            for ref in refs[1:]:
                total = total + ref[...].astype(F32)
            for quad in range(out.shape[0]):
                out[quad, start : start + size] = total.astype(BF16)
            start += size
        return
    grads_ref, out, lines = rest
    rows = parts[0].shape[0]
    size = rows - lines.shape[1]
    total = parts[0][:size].astype(F32)
    for ref in parts[1:]:
        total = total + ref[:size].astype(F32)
    total = total.astype(BF16)
    for s in range(shards):
        lines[s] = parts[s][size:].astype(F32)
    model = lines.shape[1] // 4 * gain_chunk(0, lines.shape[2])
    gains = None
    for owner in range(shards):
        which = lax.rem(owner - place_ref[0] + shards, shards)
        value = unpack_gains(lines[which], model)
        gains = value if gains is None else [a + b for a, b in zip(gains, value, strict=True)]
    gains = pack_gains(gains, lines.shape[2])
    for quad in range(out.shape[0]):
        out[quad, :size] = total
        out[quad, size:rows] = gains
        out[quad, rows:] = grads_ref[quad]


def home_sum(place, groups, extra, grads=None, after=(), quads=1):
    shards = len(groups[0])
    rows = sum(group[0].shape[0] for group in groups)
    width = groups[0][0].shape[1]
    inputs = [place, *[part for group in groups for part in group]]
    shape = (quads, rows, width)
    if grads is not None:
        inputs.append(grads)
        shape = (grads.shape[0], rows + grads.shape[1], width)
    return launch(
        functools.partial(home_kernel, len(groups), shards),
        inputs,
        [smem()] + [vmem()] * (len(inputs) - 1),
        0.1,
        after,
        out_shape=[jax.ShapeDtypeStruct(shape, BF16)],
        out_specs=[vmem()],
        scratch_shapes=[pltpu.VMEM((shards, extra, width), F32)] if extra else [],
        name="home_sum",
        vmem_mib=16,
    )[0]


def assemble_one_kernel(core_ref, own_ref, other_ref, gate_out, out_out, whole):
    quads, rows, _ = own_ref.shape
    block = rows // 2
    for quad in range(quads):
        for ref, who in ((own_ref, core_ref[0]), (other_ref, 1 - core_ref[0])):
            start = pl.multiple_of((quad * 2 + who) * block, block)
            gate_out[pl.ds(start, block), :] = ref[quad, :block].astype(F32)
            whole[pl.ds(start, block), :] = ref[quad, block:].astype(F32)
    out_out[...] = whole[...].T


def assemble_one(core, own, other):
    quads, rows, width = own.shape
    model = quads * rows
    return launch(
        assemble_one_kernel,
        [core, own, other],
        [smem(), vmem(), vmem()],
        0.1,
        out_shape=[
            jax.ShapeDtypeStruct((model, width), F32),
            jax.ShapeDtypeStruct((width, model), F32),
        ],
        out_specs=[vmem()] * 2,
        scratch_shapes=[pltpu.VMEM((model, width), F32)],
        name="assemble_one",
        vmem_mib=16,
    )


def assemble_kernel(
    rows_total,
    core_ref,
    own_ref,
    other_ref,
    decay_ref,
    input_out,
    recall_out,
    admit_out,
    recall_bias_out,
    admit_bias_out,
    taps_out,
    bias_out,
    decay_out,
    mean_out,
    gain_one_out,
    gain_two_out,
    *rest,
):
    *grads_out, small = rest
    quads, rows, width = other_ref.shape
    piece, hidden = grads_out[0].shape
    parts = hidden // (quads * width)
    for quad in range(quads):
        for part in range(3):
            for i in range(parts):
                start = rows + (part * parts + i) * piece
                first = (quad * parts + i) * width
                grads_out[part][:, first : first + width] = own_ref[
                    quad, start : start + piece
                ].astype(F32)
    model = input_out.shape[0]
    block = model // (2 * quads)
    extra = TABLE // (2 * quads)
    for quad in range(quads):
        for ref, who in ((own_ref, core_ref[0]), (other_ref, 1 - core_ref[0])):
            start = pl.multiple_of((quad * 2 + who) * block, block)
            input_out[pl.ds(start, block), :] = ref[quad, :block].astype(F32)
            start = pl.multiple_of((quad * 2 + who) * extra, extra)
            small[pl.ds(start, extra), :] = ref[quad, block : block + extra].astype(F32)
    heads, head, _ = recall_out.shape
    lines = small[2 * head : 2 * head + 16]
    for h in range(heads):
        cols = slice(h * head, (h + 1) * head)
        recall_out[h] = small[:head, cols]
        admit_out[h] = small[head : 2 * head, cols]
        recall_bias_out[h : h + 1] = lines[5:6, cols]
        admit_bias_out[h : h + 1] = lines[6:7, cols]
    taps_out[...] = lines[:4]
    bias_out[...] = lines[4]
    decay_out[...] = lines[7] * (STRENGTH * jax.nn.sigmoid(-decay_ref[...]))
    mean_out[...] = lines[8] * (1.0 / rows_total)
    gains = None
    for ref in (own_ref, other_ref):
        part = None
        for quad in range(quads):
            value = unpack_gains(ref[quad, block + extra : rows], model)
            part = value if part is None else [a + b for a, b in zip(part, value, strict=True)]
        gains = part if gains is None else [a + b for a, b in zip(gains, part, strict=True)]
    gain_one_out[...] = gains[0].reshape(model)
    gain_two_out[...] = gains[1].reshape(model)


def assemble(core, own, other, decay, model, heads, head, rows_total, piece):
    width = own.shape[2]
    hidden = own.shape[0] * (own.shape[1] - other.shape[1]) * width // (3 * piece)
    shapes = [
        (model, width),
        (heads, head, head),
        (heads, head, head),
        (heads, head),
        (heads, head),
        (4, width),
        (width,),
        (width,),
        (width,),
        (model,),
        (model,),
        (piece, hidden),
        (piece, hidden),
        (piece, hidden),
    ]
    return launch(
        functools.partial(assemble_kernel, rows_total),
        [core, own, other, decay],
        [smem(), vmem(), vmem(), vmem()],
        0.1,
        out_shape=[jax.ShapeDtypeStruct(shape, F32) for shape in shapes],
        out_specs=[vmem()] * len(shapes),
        scratch_shapes=[pltpu.VMEM((TABLE, width), F32)],
        name="assemble",
        vmem_mib=16,
    )


def on_device(
    tokens,
    doc_ids,
    cotangent,
    norm_gain,
    gate_proj,
    input_proj,
    conv_weight,
    conv_bias,
    recall_weight,
    recall_bias,
    admit_weight,
    admit_bias,
    decay_param,
    out_proj,
    mlp_gain,
    mlp_gate,
    mlp_up,
    mlp_down,
):
    count, model = tokens.shape
    width = gate_proj.shape[1]
    heads, head, _ = recall_weight.shape
    hidden_width = mlp_gate.shape[1]
    piece = mlp_gate.shape[0]
    quads = lax.axis_size("quad")
    shards = lax.axis_size("chan")
    group = 2 * quads
    quad = lax.axis_index("quad").astype(jnp.int32)
    core = lax.axis_index("core").astype(jnp.int32)
    place = lax.axis_index("chan").astype(jnp.int32)
    quad_one, core_one = quad.reshape(1), core.reshape(1)

    def hop(values, rel):
        return lax.ppermute(values, "quad", [(i, i ^ rel) for i in range(quads)])

    def swap(values):
        return lax.ppermute(values, "core", [(0, 1), (1, 0)])

    def along(values, shift):
        return lax.ppermute(values, "chan", [(i, (i + shift) % shards) for i in range(shards)])

    def share(values):
        every = jnp.broadcast_to(values[None], (quads,) + values.shape)
        return lax.all_to_all(every, "quad", 0, 0, tiled=True)

    slots = (quad * 2 + core).reshape(1)
    arriving = jnp.stack([(quad ^ rel) * 2 for rel in range(quads)])
    arriving = jnp.concatenate([arriving + core, arriving + 1 - core])

    def halves(values, made):
        if made:
            return made
        rows = values.shape[0]
        split = values.reshape(rows, quads, 2, model // group)
        return [
            lax.dynamic_index_in_dim(split, who, 2, False).reshape(rows, model // 2)
            for who in (core, 1 - core)
        ]

    ends = along(tokens[count - HALO :], 1)
    own_weights, own_table, pieces = prepare(
        slots,
        gate_proj,
        input_proj,
        out_proj,
        recall_weight,
        recall_bias,
        admit_weight,
        admit_bias,
        conv_weight,
        conv_bias,
        decay_param,
        group,
    )
    arrived = along(pieces, 1)
    normed, *made = norm(core_one, ends, tokens, norm_gain, group)

    offset = place * count
    spots = (offset + jnp.arange(count)) % LENGTH
    padded = jnp.concatenate([jnp.full((HALO,), -1, jnp.int32), doc_ids])
    here = lax.dynamic_slice_in_dim(padded, offset + HALO, count)
    columns = [jnp.ones((count,), F32)]
    for shift in range(1, 4):
        moved = lax.dynamic_slice_in_dim(padded, offset + HALO - shift, count)
        columns.append(((spots >= shift) & (here == moved)).astype(F32))
    columns += [jnp.zeros((count,), F32)] * 4
    mask = jnp.stack(columns, axis=1)

    own_width = hidden_width // quads
    slices = jnp.stack([mlp_gate, mlp_up, mlp_down])
    slices = slices.reshape(3, piece, quads, own_width).transpose(2, 0, 1, 3)
    def local(shard, weight_pieces, stacks, after=()):
        return mix_local(
            shard, shards, head, arriving, normed, mask, weight_pieces, stacks, after
        )

    normed_own, normed_other = halves(normed, made)
    normed_other = swap(normed_other)
    stacks, _ = local(0, [own_weights, own_table], None)
    (slices,) = fence([slices], [pieces])
    slices = lax.all_to_all(slices, "quad", 0, 0, tiled=True)
    near = quads // 2 + 1
    cots = [cotangent] + [hop(cotangent, rel) for rel in range(1, near)]
    gathered, waits, edges, shard_pieces = None, [normed_other, *cots[1:]], [stacks[5]], []
    for s in range(1, shards + 1):
        onward = [arrived] if s < shards else [cotangent]
        if s == min(2, shards - 1):
            onward.append(slices)
        if s == 1:
            arrived, *onward = fence(onward, waits)
        else:
            packed, arrived, *onward = pack(held, onward, [edges[s - 2]])
            stacks, _ = local(s - 1, [packed, swap(packed)], stacks)
            edges.append(stacks[5])
        if onward:
            gathered = lax.all_gather(onward[0], "chan", axis=0)
        if s == shards:
            cots += [hop(arrived, rel) for rel in range(near, quads)]
            break
        held = [arrived] + [hop(arrived, rel) for rel in range(1, quads)]
        if s < shards - 1:
            arrived = along(arrived, 1)
    weights, inputs, gated, kept, scan, edge, gates, vec = stacks
    edge, gathered = fence([edge, gathered], cots[near:])
    other_gathered = swap(gathered)
    depth = LENGTH // count - 1
    behind = [along(edge, i + 1) for i in range(depth)]
    carry, branch_in, middle, second, again = branch(
        scan, gated, weights, tokens, mlp_gain.reshape(1, model), behind, []
    )
    mlp_weights = arrange(core_one, gathered, other_gathered, [second])
    ahead = [along(edge, -(i + 1)) for i in range(depth - 1)]

    gate_grads, up_grads, hiddens, backs, seconds = [], [], [], [], []
    for rel in range(quads):
        if rel == 0:
            seconds.append(second)
        else:
            seconds.append(hop(second if rel < near else again, rel))
        gate_grad, up_grad, hidden, back, *carry_on = mlp_block(
            seconds[rel], cots[rel], mlp_weights,
            backs[-1:] if rel else [*ahead], [] if rel else [again],
        )
        if rel == 0:
            (again,) = carry_on
        gate_grads.append(gate_grad)
        up_grads.append(up_grad)
        hiddens.append(hidden)
        backs.append(back)
    backs = [hop(back, rel) if rel else back for rel, back in enumerate(backs)]
    own_grads, other_grads, results = mlp_grads(
        quad_one, core_one, mlp_weights, cots, seconds, gate_grads, up_grads, hiddens, shards
    )
    results = lax.all_to_all(results, "quad", 0, 0, tiled=True)
    block_out = (middle + jnp.sum(results.astype(F32), axis=0)).astype(BF16)
    middle_grad, branch_grad, gain_two, *made, own_grads, other_grads = middle_back(
        backs, middle, cotangent, mlp_gain, core_one, group, [], [own_grads, other_grads]
    )

    def spread(chip):
        return lax.all_to_all(chip, "quad", 0, 0, tiled=True)

    def add_up(arrived):
        return jnp.sum(arrived.astype(F32), axis=0)

    grad_own, grad_other = halves(branch_grad, made)
    gate_back, adj, edge_back, branch_in = adjoint(
        branch_grad, weights, gated, scan, kept, carry, mask, vec, [branch_in]
    )
    edges_back = [along(edge_back, -(i + 1)) for i in range(depth)]
    (chip_one,) = outer(
        core_one,
        quads,
        [
            normed_own,
            normed_other,
            gate_back,
            swap(gate_back),
            grad_own,
            swap(grad_other),
            branch_in,
            swap(branch_in),
        ],
    )
    grads = add_pair(own_grads, swap(other_grads), [*edges_back, chip_one])
    (chip_one,) = fence([chip_one], [*edges_back, results, grads])
    grads = lax.psum_scatter(grads, "chan", scatter_dimension=0)

    def home(totals):
        return [totals[0]] + [along(totals[s].astype(BF16), -s) for s in range(1, shards)]

    arrived_one = spread(chip_one)
    input_back, small, normed_grad = mix_back(
        weights, inputs, gate_back, kept, scan, adj, carry, mask, gates, vec, edge, edges_back, ahead,
        [chip_one],
    )

    sum_one = add_up(arrived_one)
    halo_grad = along(normed_grad[:HALO].astype(BF16), -1)
    inside = ((place + 1) * count % LENGTH != 0).astype(jnp.int32).reshape(1)
    grad_tokens, lines = tokens_back(
        inside, normed_grad, halo_grad, tokens, norm_gain, middle_grad, gain_two, width, [sum_one]
    )
    (chip_two,) = outer(
        core_one,
        quads,
        [normed_own, normed_other, input_back, swap(input_back)],
        [small, swap(small)],
    )
    (chip_two,) = fence([chip_two], [arrived_one])
    extra = lines.shape[0]
    totals = add_up(spread(chip_two))
    one = home_sum(place.reshape(1), [home(sum_one)], 0, quads=quads)
    (one,) = fence([one], [totals, lines])
    own_one = spread(one)
    totals = jnp.concatenate(
        [totals, jnp.broadcast_to(lines.astype(F32)[None], (shards, extra, width))], axis=1
    )
    parts = own_width // width
    grads = grads.reshape(quads, 3, piece, parts, width).transpose(0, 1, 3, 2, 4)
    grads = grads.reshape(quads, 3 * parts * piece, width)
    two = home_sum(place.reshape(1), [home(totals)], extra, grads, [own_one])
    own_two = lax.all_to_all(two, "quad", 0, 0, tiled=True)
    size = totals.shape[1]
    grad_gate, grad_out = assemble_one(core_one, own_one, swap(own_one))
    (own_two,) = fence([own_two], [grad_gate, block_out])
    (
        grad_input,
        grad_recall,
        grad_admit,
        grad_recall_bias,
        grad_admit_bias,
        grad_taps,
        grad_bias,
        grad_decay,
        gate_mean,
        gain_one,
        gain_two,
        *grads,
    ) = assemble(
        core_one,
        own_two,
        swap(own_two[:, :size]),
        decay_param,
        model,
        heads,
        head,
        count * group * shards,
        piece,
    )
    return (
        block_out,
        grad_tokens,
        gain_one,
        grad_gate,
        grad_input,
        grad_taps,
        grad_bias,
        grad_recall,
        grad_recall_bias,
        grad_admit,
        grad_admit_bias,
        grad_decay,
        grad_out,
        gain_two,
        grads[0],
        grads[1],
        grads[2],
        gate_mean,
    )


def solution(mesh):
    in_specs = (
        P(("quad", "core", "chan"), None),
        P(("quad", "core")),
        P(("quad", "core", "chan"), None),
        P(),
        P(None, "chan"),
        P(None, "chan"),
        P(None, "chan"),
        P("chan"),
        P("chan", None, None),
        P("chan", None),
        P("chan", None, None),
        P("chan", None),
        P("chan"),
        P("chan", None),
        P(),
        P(("quad", "core", "chan"), None),
        P(("quad", "core", "chan"), None),
        P(("quad", "core", "chan"), None),
    )
    out_specs = (
        P(("quad", "core", "chan"), None),
        P(("quad", "core", "chan"), None),
        P(),
        P(None, "chan"),
        P(None, "chan"),
        P(None, "chan"),
        P("chan"),
        P("chan", None, None),
        P("chan", None),
        P("chan", None, None),
        P("chan", None),
        P("chan"),
        P("chan", None),
        P(),
        P(("quad", "core", "chan"), None),
        P(("quad", "core", "chan"), None),
        P(("quad", "core", "chan"), None),
        P("chan"),
    )
    devices = mesh.devices
    quads, shards = devices.shape[0] // 2, devices.shape[1]
    split = jax.sharding.Mesh(devices.reshape(quads, 2, shards), ("quad", "core", "chan"))
    return jax.shard_map(
        on_device, mesh=split, in_specs=in_specs, out_specs=out_specs, check_vma=False
    )
```

```python
import functools

import jax
import jax.numpy as jnp
from jax import lax
from jax.experimental import pallas as pl
from jax.experimental.pallas import tpu as pltpu
from jax.sharding import PartitionSpec as P

LENGTH = 1024
EPS = 1e-06
STRENGTH = 8.0
HALO = 16
TABLE = 256
COST = 0.3
GELU_A = 0.7978845608028654
GELU_B = 0.044715
BF16 = jnp.bfloat16
F32 = jnp.float32
MIB = 1024 * 1024


def mm(left, right, left_dim, right_dim):
    return lax.dot_general(
        left, right, (((left_dim,), (right_dim,)), ((), ())), preferred_element_type=F32
    )


def gelu_parts(value):
    square = value * value
    th = jnp.tanh(GELU_A * value * (1.0 + GELU_B * square))
    half = 0.5 * (1.0 + th)
    slope = half + 0.5 * value * (1.0 - th * th) * (GELU_A * (1.0 + 3.0 * GELU_B * square))
    return value * half, slope


def gelu(value):
    th = jnp.tanh(GELU_A * value * (1.0 + GELU_B * value * value))
    return 0.5 * value * (1.0 + th)


def one_minus_exp(v):
    series = v * (
        1.0
        - v
        * (1 / 2)
        * (
            1.0
            - v
            * (1 / 3)
            * (1.0 - v * (1 / 4) * (1.0 - v * (1 / 5) * (1.0 - v * (1 / 6) * (1.0 - v * (1 / 7)))))
        )
    )
    return jnp.where(v < 0.4, series, 1.0 - jnp.exp(-v))


def rows_index(shape):
    return lax.broadcasted_iota(jnp.int32, shape, 0)


def scan_down(a, b):
    count = a.shape[0]
    index = rows_index(a.shape)
    step = 1
    while step < count:
        if step < 8:
            inside = index >= step
            a_prev = jnp.where(inside, pltpu.roll(a, step, 0), 1.0)
            b_prev = jnp.where(inside, pltpu.roll(b, step, 0), 0.0)
        else:
            a_prev = jnp.concatenate([jnp.ones_like(a[:step]), a[: count - step]], axis=0)
            b_prev = jnp.concatenate([jnp.zeros_like(b[:step]), b[: count - step]], axis=0)
        b = b + a * b_prev
        a = a * a_prev
        step *= 2
    return a, b


def scan_up(a, b):
    count = a.shape[0]
    index = rows_index(a.shape)
    step = 1
    while step < count:
        if step < 8:
            inside = index < count - step
            a_next = jnp.where(inside, pltpu.roll(a, count - step, 0), 1.0)
            b_next = jnp.where(inside, pltpu.roll(b, count - step, 0), 0.0)
        else:
            a_next = jnp.concatenate([a[step:], jnp.ones_like(a[:step])], axis=0)
            b_next = jnp.concatenate([b[step:], jnp.zeros_like(b[:step])], axis=0)
        b = b + a * b_next
        a = a * a_next
        step *= 2
    return a, b


def same_block(width, head):
    row = lax.broadcasted_iota(jnp.int32, (width, 1), 0) // head
    col = lax.broadcasted_iota(jnp.int32, (1, width), 1) // head
    return row == col


def block_diagonal(flat, head, dtype):
    width = flat.shape[1]
    tall = jnp.concatenate([flat] * (width // head), axis=0)
    shape = (width, width)
    del shape
    return jnp.where(same_block(width, head), tall, 0.0).astype(dtype)


def fold_diagonal(square, head):
    width = square.shape[0]
    kept = jnp.where(same_block(width, head), square, 0.0)
    total = kept[:head]
    for start in range(head, width, head):
        total = total + kept[start : start + head]
    return total


def vmem():
    return pl.BlockSpec(memory_space=pltpu.VMEM)


def smem():
    return pl.BlockSpec(memory_space=pltpu.SMEM)


def launch(
    kernel,
    inputs,
    in_specs,
    micros,
    after=(),
    carry=(),
    prefetch=0,
    grid=(),
    out_shape=(),
    out_specs=(),
    scratch_shapes=(),
    aliases=None,
    name=None,
    vmem_mib=60,
):
    count, extra, through = len(inputs), len(after), len(carry)
    made = len(out_shape)
    aliases = dict(aliases or {})
    for i in range(through):
        aliases[count + extra + i] = made + i

    def body(*refs):
        first = count + extra + through
        kernel(*refs[:count], *refs[first : first + made], *refs[first + made + through :])

    anywhere = pl.BlockSpec(memory_space=pl.ANY)
    return pl.pallas_call(
        body,
        out_shape=list(out_shape) + [jax.ShapeDtypeStruct(c.shape, c.dtype) for c in carry],
        grid_spec=pltpu.PrefetchScalarGridSpec(
            num_scalar_prefetch=prefetch,
            grid=grid,
            in_specs=list(in_specs) + [anywhere] * (extra + through),
            out_specs=list(out_specs) + [anywhere] * through,
            scratch_shapes=scratch_shapes,
        ),
        input_output_aliases=aliases,
        compiler_params=pltpu.CompilerParams(vmem_limit_bytes=vmem_mib * MIB),
        cost_estimate=pl.CostEstimate(
            flops=int(micros * 1.1e9 * COST), bytes_accessed=int(micros * 3.5e6 * COST), transcendentals=0
        ),
        name=name,
    )(*inputs, *after, *carry)


def split_features(core, source, own_out, other_out):
    half = own_out.shape[1]
    block = 128
    quads = half // block
    for quad in range(quads):
        for out, who in ((own_out, core), (other_out, 1 - core)):
            start = pl.multiple_of((quad * 2 + who) * block, block)
            out[:, quad * block : (quad + 1) * block] = source[:, pl.ds(start, block)]


def pack_kernel(*refs):
    *pieces, out = refs
    for i, ref in enumerate(pieces):
        out[i] = ref[0]


def pack(pieces, carry, after):
    return launch(
        pack_kernel,
        pieces,
        [vmem()] * len(pieces),
        0.1,
        after,
        carry,
        out_shape=[jax.ShapeDtypeStruct((len(pieces),) + pieces[0].shape[1:], pieces[0].dtype)],
        out_specs=[vmem()],
        name="pack",
        vmem_mib=8,
    )


def fence(carry, after=()):
    return launch(lambda *refs: None, [], [], 0.01, after, carry, name="fence", vmem_mib=60)


def prepare_kernel(
    slots_ref,
    gate_ref,
    input_ref,
    out_ref,
    recall_ref,
    recall_bias_ref,
    admit_ref,
    admit_bias_ref,
    taps_ref,
    bias_ref,
    decay_ref,
    weights,
    table_out,
    pieces_out,
    table,
):
    weights[0] = gate_ref[...]
    weights[1] = input_ref[...]
    weights[2] = out_ref[...].T
    heads, head, _ = recall_ref.shape
    for h in range(heads):
        cols = slice(h * head, (h + 1) * head)
        table[:head, cols] = recall_ref[h]
        table[head : 2 * head, cols] = admit_ref[h]
    side = jnp.concatenate
    lines = side(
        [
            taps_ref[...],
            bias_ref[...].reshape(1, -1),
            side([recall_bias_ref[h : h + 1] for h in range(heads)], axis=1),
            side([admit_bias_ref[h : h + 1] for h in range(heads)], axis=1),
            jax.nn.softplus(-decay_ref[...].reshape(1, -1)),
        ],
        axis=0,
    )
    high = lines.astype(BF16).astype(F32)
    rest = lines - high
    mid = rest.astype(BF16).astype(F32)
    table[2 * head : 2 * head + 8] = high
    table[2 * head + 8 : 2 * head + 16] = mid
    table[2 * head + 16 : 2 * head + 24] = rest - mid
    table[2 * head + 24 :] = jnp.zeros((table.shape[0] - 2 * head - 24, table.shape[1]), F32)
    table_out[...] = table[...].astype(BF16)
    count, rows, _ = pieces_out.shape
    block = pieces_block(weights.shape[1], rows)
    extra = rows - 3 * block
    for k in range(count):
        start = pl.multiple_of(slots_ref[k] * block, block)
        for part in range(3):
            pieces_out[k, part * block : (part + 1) * block] = weights[part, pl.ds(start, block), :]
        start = pl.multiple_of(slots_ref[k] * extra, extra)
        pieces_out[k, 3 * block :] = table_out[pl.ds(start, extra), :]

def norm_kernel(core_ref, ends_ref, tokens_ref, gain_ref, normed_out, *halves_out):
    for ref, rows in ((ends_ref, slice(0, HALO)), (tokens_ref, slice(HALO, None))):
        values = ref[...].astype(F32)
        scale = lax.rsqrt(jnp.mean(values * values, axis=1, keepdims=True) + EPS)
        normed_out[rows] = (values * scale * gain_ref[...]).astype(BF16)
    if halves_out:
        split_features(core_ref[0], normed_out, *halves_out)


def norm(core, ends, tokens, gain, group):
    count, model = tokens.shape
    halves = half_shapes(HALO + count, model, group)
    return launch(
        norm_kernel,
        [core, ends, tokens, gain.reshape(1, model)],
        [smem()] + [vmem()] * 3,
        0.1,
        out_shape=[jax.ShapeDtypeStruct((HALO + count, model), BF16)] + halves,
        out_specs=[vmem()] * (1 + len(halves)),
        name="norm",
        vmem_mib=16,
    )


def pieces_block(model, rows):
    return rows * model // (3 * model + TABLE)


def half_shapes(rows, model, group):
    return [jax.ShapeDtypeStruct((rows, model // 2), BF16)] * (2 if model // group == 128 else 0)


def prepare(slots, gate, inputs, out, recall, recall_bias, admit, admit_bias, taps, bias, decay, group):
    model, width = gate.shape
    rows = (3 * model + TABLE) // group
    return launch(
        prepare_kernel,
        [slots, gate, inputs, out, recall, recall_bias, admit, admit_bias, taps, bias, decay],
        [smem()] + [vmem()] * 10,
        0.1,
        out_shape=[
            jax.ShapeDtypeStruct((3, model, width), BF16),
            jax.ShapeDtypeStruct((TABLE, width), BF16),
            jax.ShapeDtypeStruct((slots.shape[0], rows, width), BF16),
        ],
        out_specs=[vmem()] * 3,
        scratch_shapes=[pltpu.VMEM((TABLE, width), F32)],
        name="prepare",
    )


def mix_local_kernel(own, head, counts, stacked, slots_ref, normed_ref, mask_ref, *rest):
    piece_refs, rest = rest[: len(counts)], rest[len(counts) :]
    weights, inputs_out, gated_out, kept_out, scan_out, edge_out, gates_out, vec_out = rest[
        stacked : stacked + 8
    ]
    (table,) = rest[stacked + 8 :]
    model = normed_ref.shape[1]
    if own:
        weights[0] = piece_refs[0][...]
        table[...] = piece_refs[1][...].astype(F32)
    else:
        number = 0
        for ref, many in zip(piece_refs, counts, strict=True):
            rows = ref.shape[1]
            block = pieces_block(model, rows)
            extra = rows - 3 * block
            for k in range(many):
                slot = slots_ref[number]
                number += 1
                start = pl.multiple_of(slot * block, block)
                for part in range(3):
                    weights[0, part, pl.ds(start, block), :] = ref[
                        k, part * block : (part + 1) * block
                    ]
                start = pl.multiple_of(slot * extra, extra)
                table[pl.ds(start, extra), :] = ref[k, 3 * block :].astype(F32)
    count = mask_ref.shape[0]
    vec = table[2 * head : 2 * head + 8] + (
        table[2 * head + 8 : 2 * head + 16] + table[2 * head + 16 : 2 * head + 24]
    )
    vec_out[0] = vec
    gates_out[0] = table[: 2 * head].astype(BF16)
    gated = mm(normed_ref[HALO:], weights[0, 0], 1, 0).astype(BF16)
    gated_out[0] = gated
    inputs = mm(normed_ref[...], weights[0, 1], 1, 0).astype(BF16)
    inputs_out[0] = inputs
    wide = inputs.astype(F32)
    conv = vec[4:5] + vec[0:1] * wide[HALO:]
    for shift in range(1, 4):
        moved = pltpu.roll(wide, shift, 0)[HALO:]
        conv = conv + vec[shift : shift + 1] * (moved * mask_ref[:, shift : shift + 1])
    low = conv.astype(BF16)
    recall_weight = block_diagonal(table[:head], head, BF16)
    admit_weight = block_diagonal(table[head : 2 * head], head, BF16)
    recall = jax.nn.sigmoid(mm(low, recall_weight, 1, 0) + vec[5:6])
    admit = jax.nn.sigmoid(mm(low, admit_weight, 1, 0) + vec[6:7])
    rate = STRENGTH * recall * vec[7:8]
    decay = jnp.exp(-rate)
    inject = jnp.sqrt(one_minus_exp(2.0 * rate)) * admit * conv
    product, state = scan_down(decay * mask_ref[:, 1:2], inject)
    kept_out[0, 0] = conv
    kept_out[0, 1] = recall
    kept_out[0, 2] = admit
    scan_out[0, 0] = product
    scan_out[0, 1] = state
    edge_out[0, 0:1] = product[count - 1 :]
    edge_out[0, 1:2] = state[count - 1 :]
    edge_out[0, 2:3] = jnp.sum(decay, axis=0, keepdims=True)


def mix_local(shard, shards, head, slots, normed, mask, pieces, stacks, after=(), carry=()):
    count = mask.shape[0]
    model = normed.shape[1]
    width = pieces[0].shape[-1]
    own = shard == 0
    counts = [p.shape[0] for p in pieces]
    shapes = [
        ((shards, 3, model, width), BF16),
        ((shards, count + HALO, width), BF16),
        ((shards, count, width), BF16),
        ((shards, 3, count, width), F32),
        ((shards, 2, count, width), F32),
        ((shards, 8, width), F32),
        ((shards, 2 * head, width), BF16),
        ((shards, 8, width), F32),
    ]

    def at(shape):
        tail = (0,) * (len(shape) - 1)
        return pl.BlockSpec((1,) + shape[1:], lambda i: (shard,) + tail)

    first = [slots, normed, mask, *pieces]
    in_specs = [smem()] + [vmem()] * (len(first) - 1)
    aliases = {}
    if stacks is not None:
        aliases = {len(first) + i: i for i in range(len(stacks))}
        in_specs += [pl.BlockSpec(memory_space=pl.ANY)] * len(stacks)
        first += list(stacks)
    outs = launch(
        functools.partial(mix_local_kernel, own, head, counts, len(aliases)),
        first,
        in_specs,
        5.7,
        after=after,
        carry=carry,
        grid=(1,),
        out_shape=[jax.ShapeDtypeStruct(shape, dtype) for shape, dtype in shapes],
        out_specs=[at(shape) for shape, _ in shapes],
        scratch_shapes=[pltpu.VMEM((TABLE, width), F32)],
        aliases=aliases,
        name="mix_local",
    )
    return outs[:8], outs[8:]


def carried(edges):
    total = edges[-1][0, 1:2]
    for edge in edges[-2::-1]:
        total = edge[0, 1:2] + edge[0, 0:1] * total
    return total


def branch_kernel(
    depth, scan_ref, gated_ref, weight_ref, resid_ref, gain_ref, *rest
):
    edges = rest[:depth]
    carry_out, branch_in_out, middle_out, second_out, again_out, acc = rest[depth:]
    step = pl.program_id(0)

    @pl.when(step == 0)
    def _():
        acc[...] = resid_ref[...].astype(F32)

    carry = carried(edges)
    carry_out[0] = jnp.broadcast_to(carry, carry_out.shape[1:])
    state = scan_ref[0, 1] + scan_ref[0, 0] * carry
    mixed = (gelu(gated_ref[0].astype(F32)) * state).astype(BF16)
    branch_in_out[0] = mixed
    acc[...] += mm(mixed, weight_ref[0, 0], 1, 1)

    @pl.when(step == pl.num_programs(0) - 1)
    def _():
        middle = acc[...]
        middle_out[...] = middle
        scale = lax.rsqrt(jnp.mean(middle * middle, axis=1, keepdims=True) + EPS)
        second = (middle * scale * gain_ref[...]).astype(BF16)
        second_out[...] = second
        again_out[...] = second


def branch(scan, gated, weights, tokens, gain, edges, after):
    shards, _, count, width = scan.shape
    model = tokens.shape[1]

    def edge_spec(shift):
        return pl.BlockSpec((1, 8, width), lambda s: ((s + shards - shift % shards) % shards, 0, 0))

    return launch(
        functools.partial(branch_kernel, len(edges)),
        [scan, gated, weights, tokens, gain, *edges],
        [
            pl.BlockSpec((1, 2, count, width), lambda s: (s, 0, 0, 0)),
            pl.BlockSpec((1, count, width), lambda s: (s, 0, 0)),
            pl.BlockSpec((1, 1, model, width), lambda s: (s, 2, 0, 0)),
            pl.BlockSpec((count, model), lambda s: (0, 0)),
            pl.BlockSpec((1, model), lambda s: (0, 0)),
        ]
        + [edge_spec(i + 1) for i in range(len(edges))],
        0.1,
        after,
        grid=(shards,),
        out_shape=[
            jax.ShapeDtypeStruct((shards, 8, width), F32),
            jax.ShapeDtypeStruct((shards, count, width), BF16),
            jax.ShapeDtypeStruct((count, model), F32),
            jax.ShapeDtypeStruct((count, model), BF16),
            jax.ShapeDtypeStruct((count, model), BF16),
        ],
        out_specs=[
            pl.BlockSpec((1, 8, width), lambda s: (s, 0, 0)),
            pl.BlockSpec((1, count, width), lambda s: (s, 0, 0)),
            pl.BlockSpec((count, model), lambda s: (0, 0)),
            pl.BlockSpec((count, model), lambda s: (0, 0)),
            pl.BlockSpec((count, model), lambda s: (0, 0)),
        ],
        scratch_shapes=[pltpu.VMEM((count, model), F32)],
        name="mix_branch",
    )


def arrange_kernel(core_ref, own_ref, other_ref, out_ref):
    shards, quads, _, piece, _ = own_ref.shape
    for ref, core in ((own_ref, core_ref[0]), (other_ref, 1 - core_ref[0])):
        for shard in range(shards):
            for quad in range(quads):
                start = pl.multiple_of(((quad * 2 + core) * shards + shard) * piece, piece)
                for part in range(3):
                    out_ref[part, pl.ds(start, piece), :] = ref[shard, quad, part]


def arrange(core, own, other, after):
    shards, quads, _, piece, width = own.shape
    if piece % 16:
        both = jnp.where(core[0] == 0, jnp.stack([own, other]), jnp.stack([other, own]))
        return both.transpose(3, 2, 0, 1, 4, 5).reshape(3, 2 * shards * quads * piece, width)
    return launch(
        arrange_kernel,
        [core, own, other],
        [smem(), vmem(), vmem()],
        0.1,
        after,
        out_shape=[jax.ShapeDtypeStruct((3, 2 * shards * quads * piece, width), BF16)],
        out_specs=[vmem()],
        name="mlp_arrange",
        vmem_mib=16,
    )[0]


def mlp_tiles(width):
    tile = 256 if width % 256 == 0 else width
    return [slice(start, start + tile) for start in range(0, width, tile)]


def mlp_kernel(
    second_ref,
    cot_ref,
    weight_ref,
    gate_grad_out,
    up_grad_out,
    hidden_out,
    back_out,
):
    second = second_ref[...]
    cot = cot_ref[...]
    total = None
    for cols in mlp_tiles(weight_ref.shape[2]):
        gate_weight, up_weight = weight_ref[0, :, cols], weight_ref[1, :, cols]
        gate = mm(second, gate_weight, 1, 0)
        upward = mm(second, up_weight, 1, 0)
        hidden_grad = mm(cot, weight_ref[2, :, cols], 1, 0)
        act, slope = gelu_parts(gate)
        hidden_out[:, cols] = (act * upward).astype(BF16)
        gate_grad = (hidden_grad * upward * slope).astype(BF16)
        up_grad = (hidden_grad * act).astype(BF16)
        gate_grad_out[:, cols] = gate_grad
        up_grad_out[:, cols] = up_grad
        back = mm(gate_grad, gate_weight, 1, 1) + mm(up_grad, up_weight, 1, 1)
        total = back if total is None else total + back
    back_out[...] = total.astype(BF16)


def mlp_block(second, cot, weights, after, carry):
    count, model = second.shape
    width = weights.shape[-1]
    wide = jax.ShapeDtypeStruct((count, width), BF16)
    return launch(
        mlp_kernel,
        [second, cot, weights],
        [vmem()] * 3,
        7.4,
        after,
        carry,
        out_shape=[wide, wide, wide, jax.ShapeDtypeStruct((count, model), BF16)],
        out_specs=[vmem()] * 4,
        name="mlp_block",
        vmem_mib=16,
    )


def mlp_grads_kernel(quads, quad_ref, core_ref, weight_ref, *rest):
    cots, rest = rest[:quads], rest[quads:]
    seconds, rest = rest[:quads], rest[quads:]
    gate_grads, rest = rest[:quads], rest[quads:]
    up_grads, rest = rest[:quads], rest[quads:]
    hiddens, rest = rest[:quads], rest[quads:]
    *grads_out, results_out, second, cot, left, whole_ref = rest
    count = seconds[0].shape[0]
    rows = [slice(rel * count, (rel + 1) * count) for rel in range(quads)]
    for rel in range(quads):
        second[rows[rel]] = seconds[rel][...]
        cot[rows[rel]] = cots[rel][...]
    total = None
    for cols in mlp_tiles(weight_ref.shape[2]):
        for part, (base, group) in enumerate(
            ((second, gate_grads), (second, up_grads), (cot, hiddens))
        ):
            for rel in range(quads):
                left[rows[rel]] = group[rel][:, cols]
            whole = mm(base[...], left[...], 0, 0).astype(BF16)
            if len(grads_out) == 1:
                grads_out[0][part, :, cols] = whole
                continue
            whole_ref[...] = whole
            shards, _, _, piece, _ = grads_out[0].shape
            for out, core in zip(grads_out, (core_ref[0], 1 - core_ref[0]), strict=True):
                for shard in range(shards):
                    for quad in range(quads):
                        start = pl.multiple_of(((quad * 2 + core) * shards + shard) * piece, piece)
                        out[shard, quad, part, :, cols] = whole_ref[pl.ds(start, piece), :]
        result = mm(left[...], weight_ref[2, :, cols], 1, 1)
        total = result if total is None else total + result
    for rel in range(quads):
        results_out[quad_ref[0] ^ rel] = total[rows[rel]].astype(BF16)


def mlp_grads(quad, core, weights, cots, seconds, gate_grads, up_grads, hiddens, shards):
    quads = len(seconds)
    count, model = seconds[0].shape
    width = weights.shape[2]
    tile = mlp_tiles(width)[0].stop
    piece = model // (quads * 2 * shards)
    shapes = [(shards, quads, 3, piece, width)] * 2 if piece % 16 == 0 else [(3, model, width)]
    *grads, results = launch(
        functools.partial(mlp_grads_kernel, quads),
        [quad, core, weights, *cots, *seconds, *gate_grads, *up_grads, *hiddens],
        [smem()] * 2 + [vmem()] * (1 + 5 * quads),
        15.0,
        out_shape=[jax.ShapeDtypeStruct(shape, BF16) for shape in shapes]
        + [jax.ShapeDtypeStruct((quads, count, model), BF16)],
        out_specs=[vmem()] * (1 + len(shapes)),
        scratch_shapes=[
            pltpu.VMEM((quads * count, model), BF16),
            pltpu.VMEM((quads * count, model), BF16),
            pltpu.VMEM((quads * count, tile), BF16),
            pltpu.VMEM((model, tile), BF16),
        ],
        name="mlp_grads",
        vmem_mib=32,
    )
    if piece % 16:
        both = grads[0].reshape(3, quads, 2, shards, piece, width).transpose(2, 3, 1, 0, 4, 5)
        grads = [lax.dynamic_index_in_dim(both, who, 0, False) for who in (core[0], 1 - core[0])]
    return *grads, results


def add_kernel(a_ref, b_ref, out_ref):
    out_ref[...] = (a_ref[...].astype(F32) + b_ref[...].astype(F32)).astype(BF16)


def add_pair(a, b, after=()):
    return launch(
        add_kernel,
        [a, b],
        [vmem()] * 2,
        0.1,
        after,
        out_shape=[jax.ShapeDtypeStruct(a.shape, BF16)],
        out_specs=[vmem()],
        name="add_pair",
        vmem_mib=16,
    )[0]


def middle_kernel(blocks, back_ref, *rest):
    (*backs, values_ref, cot_ref, gain_ref, core_ref), outs = rest[: blocks + 3], rest[blocks + 3 :]
    middle_grad_out, low_out, gain_out, *halves_out = outs
    grad = back_ref[...].astype(F32)
    for ref in backs:
        grad = grad + ref[...].astype(F32)
    values = values_ref[...]
    scale = lax.rsqrt(jnp.mean(values * values, axis=1, keepdims=True) + EPS)
    scaled = grad * gain_ref[...]
    inner = jnp.mean(scaled * values, axis=1, keepdims=True)
    total = cot_ref[...].astype(F32) + scale * scaled - values * (scale * scale * scale * inner)
    middle_grad_out[...] = total
    low_out[...] = total.astype(BF16)
    if halves_out:
        split_features(core_ref[0], low_out, *halves_out)
    gain_out[...] = jnp.sum(grad * values * scale, axis=0, keepdims=True)


def middle_back(backs, values, cot, gain, core, group, after, carry):
    count, model = values.shape
    halves = half_shapes(count, model, group)
    return launch(
        functools.partial(middle_kernel, len(backs)),
        [*backs, values, cot, gain.reshape(1, model), core],
        [vmem()] * (len(backs) + 3) + [smem()],
        0.1,
        after,
        carry,
        out_shape=[
            jax.ShapeDtypeStruct((count, model), F32),
            jax.ShapeDtypeStruct((count, model), BF16),
            jax.ShapeDtypeStruct((1, model), F32),
        ]
        + halves,
        out_specs=[vmem()] * (3 + len(halves)),
        name="middle_back",
        vmem_mib=16,
    )


def tokens_kernel(
    inside_ref, grad_ref, halo_ref, tokens_ref, gain_ref, middle_grad_ref, gain_two_ref, out, lines_out
):
    grad = grad_ref[HALO:]
    count = grad.shape[0]
    last = jnp.where(inside_ref[0] > 0, halo_ref[...].astype(F32), 0.0)
    grad = jnp.concatenate([grad[: count - HALO], grad[count - HALO :] + last], axis=0)
    values = tokens_ref[...].astype(F32)
    scale = lax.rsqrt(jnp.mean(values * values, axis=1, keepdims=True) + EPS)
    scaled = grad * gain_ref[...]
    inner = jnp.mean(scaled * values, axis=1, keepdims=True)
    out[...] = middle_grad_ref[...] + scale * scaled - values * (scale * scale * scale * inner)
    both = (jnp.sum(grad * values * scale, axis=0, keepdims=True), gain_two_ref[...])
    lines_out[...] = pack_gains(both, lines_out.shape[1])


def gain_chunk(model, width):
    chunk = 128
    while chunk * 2 <= width:
        chunk *= 2
    while chunk > width:
        chunk //= 2
    return chunk


def gain_lines(model, width):
    return 4 * (model // gain_chunk(model, width))


def pack_gains(both, width):
    chunk = gain_chunk(both[0].shape[1], width)
    lines = []
    for value in both:
        high = value.astype(BF16).astype(F32)
        for term in (high, value - high):
            lines += [term[:, i : i + chunk] for i in range(0, term.shape[1], chunk)]
    lines = jnp.concatenate(lines, axis=0)
    if chunk < width:
        blank = jnp.zeros((lines.shape[0], width - chunk), F32)
        lines = jnp.concatenate([lines, blank], axis=1)
    return lines.astype(BF16)


def unpack_gains(lines, model):
    chunk = gain_chunk(model, lines.shape[1])
    many = model // chunk
    lines = lines.astype(F32)
    both = []
    for i in range(2):
        value = lines[2 * i * many : (2 * i + 1) * many] + lines[
            (2 * i + 1) * many : (2 * i + 2) * many
        ]
        both.append(
            jnp.concatenate([value[j : j + 1, :chunk] for j in range(many)], axis=1)
        )
    return both


def tokens_back(inside, grad, halo, tokens, gain, middle_grad, gain_two, width, after):
    count, model = tokens.shape
    return launch(
        tokens_kernel,
        [inside, grad, halo, tokens, gain.reshape(1, model), middle_grad, gain_two],
        [smem()] + [vmem()] * 6,
        0.1,
        after,
        out_shape=[
            jax.ShapeDtypeStruct((count, model), F32),
            jax.ShapeDtypeStruct((gain_lines(model, width), width), BF16),
        ],
        out_specs=[vmem()] * 2,
        name="tokens_back",
        vmem_mib=16,
    )


def adjoint_kernel(
    grad_ref,
    weight_ref,
    gated_ref,
    scan_ref,
    kept_ref,
    carry_ref,
    mask_ref,
    vec_ref,
    gate_back_out,
    adjoint_out,
    edge_out,
):
    into = mm(grad_ref[...], weight_ref[0, 0], 1, 0).astype(BF16).astype(F32)
    act, slope = gelu_parts(gated_ref[0].astype(F32))
    state = scan_ref[0, 1] + scan_ref[0, 0] * carry_ref[0, 0:1]
    gate_back_out[0] = (into * state * slope).astype(BF16)
    decay = jnp.exp(-STRENGTH * kept_ref[0, 0] * vec_ref[0, 7:8]) * mask_ref[:, 1:2]
    count = decay.shape[0]
    shifted = jnp.where(
        rows_index(decay.shape) < count - 1, pltpu.roll(decay, count - 1, 0), 1.0
    )
    product, value = scan_up(shifted, into * act)
    adjoint_out[0, 0] = product
    adjoint_out[0, 1] = value
    edge_out[0] = jnp.broadcast_to(decay[0:1] * value[0:1], edge_out.shape[1:])


def adjoint(grad, weights, gated, scan, kept, carry, mask, vec, through):
    shards, _, count, width = scan.shape
    model = grad.shape[1]

    def flat(*shape):
        return pl.BlockSpec(shape, lambda s: (0,) * len(shape))

    def at(*shape):
        return pl.BlockSpec((1,) + shape, lambda s: (s,) + (0,) * len(shape))

    return launch(
        adjoint_kernel,
        [grad, weights, gated, scan, kept, carry, mask, vec],
        [
            flat(count, model),
            pl.BlockSpec((1, 1, model, width), lambda s: (s, 2, 0, 0)),
            at(count, width),
            at(2, count, width),
            pl.BlockSpec((1, 1, count, width), lambda s: (s, 1, 0, 0)),
            at(8, width),
            flat(*mask.shape),
            at(8, width),
        ],
        0.1,
        carry=through,
        grid=(shards,),
        out_shape=[
            jax.ShapeDtypeStruct((shards, count, width), BF16),
            jax.ShapeDtypeStruct((shards, 2, count, width), F32),
            jax.ShapeDtypeStruct((shards, 8, width), F32),
        ],
        out_specs=[at(count, width), at(2, count, width), at(8, width)],
        name="mix_adjoint",
    )


def outer_kernel(groups, quads, core_ref, quad_ref, *rest):
    pairs, rest = rest[: 4 * groups], rest[4 * groups :]
    *rest, left, right, small, whole = rest
    if len(rest) in (3, 2 + quads):
        smalls, outs = rest[:2], rest[2:]
    else:
        smalls, outs = [], rest
    count = pairs[2].shape[1]
    shards = outs[0].shape[-3]
    block = left.shape[1] // quads

    def put(s, rows, member, values):
        if len(outs) == 1:
            outs[0][member, s, rows] = values
        else:
            outs[member][s, rows] = values

    for group in range(groups):
        left_ref, left_other, right_ref, right_other = pairs[4 * group : 4 * group + 4]
        left[:count] = left_ref[left_ref.shape[0] - count :]
        left[count:] = left_other[left_ref.shape[0] - count :]
        rows = slice(group * block, (group + 1) * block)
        for s in range(shards):
            right[:count] = right_ref[s]
            right[count:] = right_other[s]
            whole[...] = mm(left[...], right[...], 0, 0).astype(BF16)
            for member in range(quads):
                quad = member if len(outs) == 1 else quad_ref[0] ^ member
                start = quad * block
                if len(outs) > 1:
                    start = pl.multiple_of(start, block)
                put(s, rows, member, whole[pl.ds(start, block), :])
    if smalls:
        extra = outs[0].shape[-2] - groups * block
        rows = slice(groups * block, groups * block + extra)
        for s in range(shards):
            small[...] = (smalls[0][s].astype(F32) + smalls[1][s].astype(F32)).astype(BF16)
            for member in range(quads):
                quad = member if len(outs) == 1 else quad_ref[0] ^ member
                start = pl.multiple_of((quad * 2 + core_ref[0]) * extra, extra)
                put(s, rows, member, small[pl.ds(start, extra), :])


def outer(core, quad, quads, pairs, smalls=(), after=(), relative=False):
    shards, count, width = pairs[2].shape
    model = pairs[0].shape[1]
    groups = len(pairs) // 4
    rows = groups * model // quads + (TABLE // (2 * quads) if smalls else 0)
    shapes = [(shards, rows, width)] * quads if relative else [(quads, shards, rows, width)]
    return launch(
        functools.partial(outer_kernel, groups, quads),
        [core, quad, *pairs, *smalls],
        [smem()] * 2 + [vmem()] * (len(pairs) + len(smalls)),
        0.1,
        after,
        out_shape=[jax.ShapeDtypeStruct(shape, BF16) for shape in shapes],
        out_specs=[vmem()] * len(shapes),
        scratch_shapes=[
            pltpu.VMEM((2 * count, model), BF16),
            pltpu.VMEM((2 * count, width), BF16),
            pltpu.VMEM((TABLE, width), BF16),
            pltpu.VMEM((model, width), BF16),
        ],
        name="mix_outer",
    )


def mix_back_kernel(
    head,
    depth,
    gate_weight_ref,
    input_weight_ref,
    inputs_ref,
    gate_back_ref,
    kept_ref,
    scan_ref,
    adjoint_ref,
    carry_ref,
    mask_ref,
    gates_ref,
    vec_ref,
    edge_ref,
    *rest,
):
    backs, decays = rest[:depth], rest[depth : 2 * depth - 1]
    input_back_out, small_out, normed_grad_out, acc = rest[2 * depth - 1 :]
    step = pl.program_id(0)
    count = mask_ref.shape[0]
    width = vec_ref.shape[2]
    vec = vec_ref[0]
    incoming = backs[-1][0, 0:1]
    for back, edge in zip(backs[-2::-1], decays[::-1], strict=True):
        incoming = back[0, 0:1] + edge[0, 0:1] * incoming
    adj = adjoint_ref[0, 1] + adjoint_ref[0, 0] * incoming
    carry = carry_ref[0, 0:1]
    state = scan_ref[0, 1] + scan_ref[0, 0] * carry
    before = jnp.where(rows_index(state.shape) == 0, carry, pltpu.roll(state, 1, 0))
    conv, recall, admit = kept_ref[0, 0], kept_ref[0, 1], kept_ref[0, 2]
    speed = STRENGTH * vec[7:8]
    rate = recall * speed
    decay = jnp.exp(-rate)
    square = one_minus_exp(2.0 * rate)
    inverse = lax.rsqrt(square)
    sized = adj * (square * inverse)
    pulled = adj * admit
    log_grad = decay * (adj * before * mask_ref[:, 1:2] - pulled * conv * decay * inverse)
    recall_grad = -speed * log_grad * recall * (1.0 - recall)
    admit_grad = sized * conv * admit * (1.0 - admit)
    conv_grad = sized * admit
    recall_low = recall_grad.astype(BF16)
    admit_low = admit_grad.astype(BF16)
    gates = gates_ref[0].astype(F32)
    recall_weight = block_diagonal(gates[:head], head, BF16)
    admit_weight = block_diagonal(gates[head:], head, BF16)
    conv_grad = conv_grad + mm(recall_low, recall_weight, 1, 1) + mm(admit_low, admit_weight, 1, 1)
    wide = inputs_ref[0].astype(F32)
    blank = jnp.zeros((HALO, width), F32)
    reach = jnp.concatenate([blank, vec[0:1] * conv_grad], axis=0)
    tap_grads = [jnp.sum(conv_grad * wide[HALO:], axis=0, keepdims=True)]
    for shift in range(1, 4):
        masked = conv_grad * mask_ref[:, shift : shift + 1]
        moved = pltpu.roll(wide, shift, 0)[HALO:]
        tap_grads.append(jnp.sum(masked * moved, axis=0, keepdims=True))
        back = jnp.concatenate([blank, vec[shift : shift + 1] * masked], axis=0)
        reach = reach + pltpu.roll(back, count + HALO - shift, 0)
    input_back = reach.astype(BF16)
    conv_low = conv.astype(BF16)
    input_back_out[0] = input_back
    small_out[0, :head] = fold_diagonal(mm(conv_low, recall_low, 0, 0), head).astype(BF16)
    small_out[0, head : 2 * head] = fold_diagonal(mm(conv_low, admit_low, 0, 0), head).astype(BF16)
    rows = tap_grads + [
        jnp.sum(conv_grad, axis=0, keepdims=True),
        jnp.sum(recall_grad, axis=0, keepdims=True),
        jnp.sum(admit_grad, axis=0, keepdims=True),
        jnp.sum(recall * log_grad, axis=0, keepdims=True),
        edge_ref[0, 2:3],
    ]
    rows.append(jnp.zeros((TABLE - 2 * head - len(rows), width), F32))
    small_out[0, 2 * head :] = jnp.concatenate(rows, axis=0).astype(BF16)
    through_gate = mm(gate_back_ref[0], gate_weight_ref[0, 0], 1, 1)
    through_input = mm(input_back, input_weight_ref[0, 0], 1, 1)

    @pl.when(step == 0)
    def _():
        acc[...] = through_input

    @pl.when(step > 0)
    def _():
        acc[...] += through_input

    acc[HALO:] += through_gate

    @pl.when(step == pl.num_programs(0) - 1)
    def _():
        normed_grad_out[...] = acc[...]


def mix_back(
    weights, inputs, gate_back, kept, scan, adj, carry, mask, gates, vec, edge, backs, ahead, after
):
    shards, _, count, width = scan.shape
    model = weights.shape[2]
    head = gates.shape[1] // 2
    depth = len(backs)

    def flat(*shape):
        return pl.BlockSpec(shape, lambda s: (0,) * len(shape))

    def at(*shape):
        return pl.BlockSpec((1,) + shape, lambda s: (s,) + (0,) * len(shape))

    def ahead_spec(shift):
        return pl.BlockSpec((1, 8, width), lambda s: ((s + shift) % shards, 0, 0))

    return launch(
        functools.partial(mix_back_kernel, head, depth),
        [
            weights, weights, inputs, gate_back, kept, scan, adj, carry, mask, gates, vec,
            edge, *backs, *ahead,
        ],
        [
            pl.BlockSpec((1, 1, model, width), lambda s: (s, 0, 0, 0)),
            pl.BlockSpec((1, 1, model, width), lambda s: (s, 1, 0, 0)),
            at(count + HALO, width),
            at(count, width),
            at(3, count, width),
            at(2, count, width),
            at(2, count, width),
            at(8, width),
            flat(*mask.shape),
            at(2 * head, width),
            at(8, width),
            at(8, width),
        ]
        + [ahead_spec(i + 1) for i in range(depth)]
        + [ahead_spec(i + 1) for i in range(depth - 1)],
        0.1,
        after,
        grid=(shards,),
        out_shape=[
            jax.ShapeDtypeStruct((shards, count + HALO, width), BF16),
            jax.ShapeDtypeStruct((shards, TABLE, width), BF16),
            jax.ShapeDtypeStruct((count + HALO, model), F32),
        ],
        out_specs=[at(count + HALO, width), at(TABLE, width), flat(count + HALO, model)],
        scratch_shapes=[pltpu.VMEM((count + HALO, model), F32)],
        name="mix_back",
    )


def home_kernel(groups, shards, place_ref, *rest):
    parts, rest = rest[: groups * shards], rest[groups * shards :]
    if len(rest) == 1:
        (out,) = rest
        start = 0
        for group in range(groups):
            refs = parts[group * shards : (group + 1) * shards]
            size = refs[0].shape[0]
            total = refs[0][...].astype(F32)
            for ref in refs[1:]:
                total = total + ref[...].astype(F32)
            for quad in range(out.shape[0]):
                out[quad, start : start + size] = total.astype(BF16)
            start += size
        return
    grads_ref, out, lines = rest
    rows = parts[0].shape[0]
    size = rows - lines.shape[1]
    total = parts[0][:size].astype(F32)
    for ref in parts[1:]:
        total = total + ref[:size].astype(F32)
    total = total.astype(BF16)
    for s in range(shards):
        lines[s] = parts[s][size:].astype(F32)
    model = lines.shape[1] // 4 * gain_chunk(0, lines.shape[2])
    gains = None
    for owner in range(shards):
        which = lax.rem(owner - place_ref[0] + shards, shards)
        value = unpack_gains(lines[which], model)
        gains = value if gains is None else [a + b for a, b in zip(gains, value, strict=True)]
    gains = pack_gains(gains, lines.shape[2])
    for quad in range(out.shape[0]):
        out[quad, :size] = total
        out[quad, size:rows] = gains
        out[quad, rows:] = grads_ref[quad]


def home_sum(place, groups, extra, grads=None, after=(), quads=1):
    shards = len(groups[0])
    rows = sum(group[0].shape[0] for group in groups)
    width = groups[0][0].shape[1]
    inputs = [place, *[part for group in groups for part in group]]
    shape = (quads, rows, width)
    if grads is not None:
        inputs.append(grads)
        shape = (grads.shape[0], rows + grads.shape[1], width)
    return launch(
        functools.partial(home_kernel, len(groups), shards),
        inputs,
        [smem()] + [vmem()] * (len(inputs) - 1),
        0.1,
        after,
        out_shape=[jax.ShapeDtypeStruct(shape, BF16)],
        out_specs=[vmem()],
        scratch_shapes=[pltpu.VMEM((shards, extra, width), F32)] if extra else [],
        name="home_sum",
        vmem_mib=16,
    )[0]


def assemble_one_kernel(core_ref, own_ref, other_ref, gate_out, out_out, whole):
    quads, rows, _ = own_ref.shape
    block = rows // 2
    for quad in range(quads):
        for ref, who in ((own_ref, core_ref[0]), (other_ref, 1 - core_ref[0])):
            start = pl.multiple_of((quad * 2 + who) * block, block)
            gate_out[pl.ds(start, block), :] = ref[quad, :block].astype(F32)
            whole[pl.ds(start, block), :] = ref[quad, block:].astype(F32)
    out_out[...] = whole[...].T


def assemble_one(core, own, other):
    quads, rows, width = own.shape
    model = quads * rows
    return launch(
        assemble_one_kernel,
        [core, own, other],
        [smem(), vmem(), vmem()],
        0.1,
        out_shape=[
            jax.ShapeDtypeStruct((model, width), F32),
            jax.ShapeDtypeStruct((width, model), F32),
        ],
        out_specs=[vmem()] * 2,
        scratch_shapes=[pltpu.VMEM((model, width), F32)],
        name="assemble_one",
        vmem_mib=16,
    )


def assemble_kernel(
    rows_total,
    core_ref,
    own_ref,
    other_ref,
    decay_ref,
    input_out,
    recall_out,
    admit_out,
    recall_bias_out,
    admit_bias_out,
    taps_out,
    bias_out,
    decay_out,
    mean_out,
    gain_one_out,
    gain_two_out,
    *rest,
):
    *grads_out, small = rest
    quads, rows, width = other_ref.shape
    piece, hidden = grads_out[0].shape
    parts = hidden // (quads * width)
    for quad in range(quads):
        for part in range(3):
            for i in range(parts):
                start = rows + (part * parts + i) * piece
                first = (quad * parts + i) * width
                grads_out[part][:, first : first + width] = own_ref[
                    quad, start : start + piece
                ].astype(F32)
    model = input_out.shape[0]
    block = model // (2 * quads)
    extra = TABLE // (2 * quads)
    for quad in range(quads):
        for ref, who in ((own_ref, core_ref[0]), (other_ref, 1 - core_ref[0])):
            start = pl.multiple_of((quad * 2 + who) * block, block)
            input_out[pl.ds(start, block), :] = ref[quad, :block].astype(F32)
            start = pl.multiple_of((quad * 2 + who) * extra, extra)
            small[pl.ds(start, extra), :] = ref[quad, block : block + extra].astype(F32)
    heads, head, _ = recall_out.shape
    lines = small[2 * head : 2 * head + 16]
    for h in range(heads):
        cols = slice(h * head, (h + 1) * head)
        recall_out[h] = small[:head, cols]
        admit_out[h] = small[head : 2 * head, cols]
        recall_bias_out[h : h + 1] = lines[5:6, cols]
        admit_bias_out[h : h + 1] = lines[6:7, cols]
    taps_out[...] = lines[:4]
    bias_out[...] = lines[4]
    decay_out[...] = lines[7] * (STRENGTH * jax.nn.sigmoid(-decay_ref[...]))
    mean_out[...] = lines[8] * (1.0 / rows_total)
    gains = None
    for ref in (own_ref, other_ref):
        part = None
        for quad in range(quads):
            value = unpack_gains(ref[quad, block + extra : rows], model)
            part = value if part is None else [a + b for a, b in zip(part, value, strict=True)]
        gains = part if gains is None else [a + b for a, b in zip(gains, part, strict=True)]
    gain_one_out[...] = gains[0].reshape(model)
    gain_two_out[...] = gains[1].reshape(model)


def assemble(core, own, other, decay, model, heads, head, rows_total, piece):
    width = own.shape[2]
    hidden = own.shape[0] * (own.shape[1] - other.shape[1]) * width // (3 * piece)
    shapes = [
        (model, width),
        (heads, head, head),
        (heads, head, head),
        (heads, head),
        (heads, head),
        (4, width),
        (width,),
        (width,),
        (width,),
        (model,),
        (model,),
        (piece, hidden),
        (piece, hidden),
        (piece, hidden),
    ]
    return launch(
        functools.partial(assemble_kernel, rows_total),
        [core, own, other, decay],
        [smem(), vmem(), vmem(), vmem()],
        0.1,
        out_shape=[jax.ShapeDtypeStruct(shape, F32) for shape in shapes],
        out_specs=[vmem()] * len(shapes),
        scratch_shapes=[pltpu.VMEM((TABLE, width), F32)],
        name="assemble",
        vmem_mib=16,
    )


def on_device(
    tokens,
    doc_ids,
    cotangent,
    norm_gain,
    gate_proj,
    input_proj,
    conv_weight,
    conv_bias,
    recall_weight,
    recall_bias,
    admit_weight,
    admit_bias,
    decay_param,
    out_proj,
    mlp_gain,
    mlp_gate,
    mlp_up,
    mlp_down,
):
    count, model = tokens.shape
    width = gate_proj.shape[1]
    heads, head, _ = recall_weight.shape
    hidden_width = mlp_gate.shape[1]
    piece = mlp_gate.shape[0]
    quads = lax.axis_size("quad")
    shards = lax.axis_size("chan")
    group = 2 * quads
    quad = lax.axis_index("quad").astype(jnp.int32)
    core = lax.axis_index("core").astype(jnp.int32)
    place = lax.axis_index("chan").astype(jnp.int32)
    quad_one, core_one = quad.reshape(1), core.reshape(1)

    def hop(values, rel):
        return lax.ppermute(values, "quad", [(i, i ^ rel) for i in range(quads)])

    def swap(values):
        return lax.ppermute(values, "core", [(0, 1), (1, 0)])

    def along(values, shift):
        return lax.ppermute(values, "chan", [(i, (i + shift) % shards) for i in range(shards)])

    def share(values):
        every = jnp.broadcast_to(values[None], (quads,) + values.shape)
        return lax.all_to_all(every, "quad", 0, 0, tiled=True)

    slots = (quad * 2 + core).reshape(1)
    arriving = jnp.stack([(quad ^ rel) * 2 for rel in range(quads)])
    arriving = jnp.concatenate([arriving + core, arriving + 1 - core])

    def halves(values, made):
        if made:
            return made
        rows = values.shape[0]
        split = values.reshape(rows, quads, 2, model // group)
        return [
            lax.dynamic_index_in_dim(split, who, 2, False).reshape(rows, model // 2)
            for who in (core, 1 - core)
        ]

    ends = along(tokens[count - HALO :], 1)
    own_weights, own_table, pieces = prepare(
        slots,
        gate_proj,
        input_proj,
        out_proj,
        recall_weight,
        recall_bias,
        admit_weight,
        admit_bias,
        conv_weight,
        conv_bias,
        decay_param,
        group,
    )
    arrived = along(pieces, 1)
    normed, *made = norm(core_one, ends, tokens, norm_gain, group)

    offset = place * count
    spots = (offset + jnp.arange(count)) % LENGTH
    padded = jnp.concatenate([jnp.full((HALO,), -1, jnp.int32), doc_ids])
    here = lax.dynamic_slice_in_dim(padded, offset + HALO, count)
    columns = [jnp.ones((count,), F32)]
    for shift in range(1, 4):
        moved = lax.dynamic_slice_in_dim(padded, offset + HALO - shift, count)
        columns.append(((spots >= shift) & (here == moved)).astype(F32))
    columns += [jnp.zeros((count,), F32)] * 4
    mask = jnp.stack(columns, axis=1)

    own_width = hidden_width // quads
    slices = jnp.stack([mlp_gate, mlp_up, mlp_down])
    slices = slices.reshape(3, piece, quads, own_width).transpose(2, 0, 1, 3)
    def local(shard, weight_pieces, stacks, after=()):
        return mix_local(
            shard, shards, head, arriving, normed, mask, weight_pieces, stacks, after
        )

    normed_own, normed_other = halves(normed, made)
    normed_other = swap(normed_other)
    stacks, _ = local(0, [own_weights, own_table], None)
    (slices,) = fence([slices], [pieces])
    slices = lax.all_to_all(slices, "quad", 0, 0, tiled=True)
    near = quads // 2 + 1
    cots = [cotangent] + [hop(cotangent, rel) for rel in range(1, near)]
    gathered, waits, edges, shard_pieces = None, [normed_other, *cots[1:]], [stacks[5]], []
    for s in range(1, shards + 1):
        onward = [arrived] if s < shards else [cotangent]
        if s == min(2, shards - 1):
            onward.append(slices)
        if s == 1:
            arrived, *onward = fence(onward, waits)
        else:
            packed, arrived, *onward = pack(held, onward, [edges[s - 2]])
            stacks, _ = local(s - 1, [packed, swap(packed)], stacks)
            edges.append(stacks[5])
        if onward:
            gathered = lax.all_gather(onward[0], "chan", axis=0)
        if s == shards:
            cots += [hop(arrived, rel) for rel in range(near, quads)]
            break
        held = [arrived] + [hop(arrived, rel) for rel in range(1, quads)]
        if s < shards - 1:
            arrived = along(arrived, 1)
    weights, inputs, gated, kept, scan, edge, gates, vec = stacks
    edge, gathered = fence([edge, gathered], cots[near:])
    other_gathered = swap(gathered)
    depth = LENGTH // count - 1
    behind = [along(edge, i + 1) for i in range(depth)]
    carry, branch_in, middle, second, again = branch(
        scan, gated, weights, tokens, mlp_gain.reshape(1, model), behind, []
    )
    mlp_weights = arrange(core_one, gathered, other_gathered, [second])
    ahead = [along(edge, -(i + 1)) for i in range(depth - 1)]

    gate_grads, up_grads, hiddens, backs, seconds = [], [], [], [], []
    for rel in range(quads):
        if rel == 0:
            seconds.append(second)
        else:
            seconds.append(hop(second if rel < near else again, rel))
        gate_grad, up_grad, hidden, back, *carry_on = mlp_block(
            seconds[rel], cots[rel], mlp_weights,
            backs[-1:] if rel else [*ahead], [] if rel else [again],
        )
        if rel == 0:
            (again,) = carry_on
        gate_grads.append(gate_grad)
        up_grads.append(up_grad)
        hiddens.append(hidden)
        backs.append(back)
    backs = [hop(back, rel) if rel else back for rel, back in enumerate(backs)]
    own_grads, other_grads, results = mlp_grads(
        quad_one, core_one, mlp_weights, cots, seconds, gate_grads, up_grads, hiddens, shards
    )
    results = lax.all_to_all(results, "quad", 0, 0, tiled=True)
    middle_grad, branch_grad, gain_two, *made, own_grads, other_grads = middle_back(
        backs, middle, cotangent, mlp_gain, core_one, group, [], [own_grads, other_grads]
    )

    def spread(chip):
        return lax.all_to_all(chip, "quad", 0, 0, tiled=True)

    def add_up(arrived):
        return jnp.sum(arrived.astype(F32), axis=0)

    grad_own, grad_other = halves(branch_grad, made)
    gate_back, adj, edge_back, branch_in = adjoint(
        branch_grad, weights, gated, scan, kept, carry, mask, vec, [branch_in]
    )
    edges_back = [along(edge_back, -(i + 1)) for i in range(depth)]
    (chip_one,) = outer(
        core_one,
        quad_one,
        quads,
        [
            normed_own,
            normed_other,
            gate_back,
            swap(gate_back),
            grad_own,
            swap(grad_other),
            branch_in,
            swap(branch_in),
        ],
    )
    grads = add_pair(own_grads, swap(other_grads), [*edges_back, chip_one])
    (chip_one,) = fence([chip_one], [*edges_back, results, grads])
    grads = lax.psum_scatter(grads, "chan", scatter_dimension=0)

    def home(totals):
        return [totals[0]] + [along(totals[s].astype(BF16), -s) for s in range(1, shards)]

    arrived_one = spread(chip_one)
    input_back, small, normed_grad = mix_back(
        weights, inputs, gate_back, kept, scan, adj, carry, mask, gates, vec, edge, edges_back, ahead,
        [chip_one],
    )

    chip_two = outer(
        core_one,
        quad_one,
        quads,
        [normed_own, normed_other, input_back, swap(input_back)],
        [small, swap(small)],
        relative=True,
    )
    parts_two = [chip_two[0]] + [hop(chip_two[rel], rel) for rel in range(1, quads)]
    sum_one = add_up(arrived_one)
    (results,) = fence([results], [sum_one])
    block_out = (middle + jnp.sum(results.astype(F32), axis=0)).astype(BF16)
    halo_grad = along(normed_grad[:HALO].astype(BF16), -1)
    inside = ((place + 1) * count % LENGTH != 0).astype(jnp.int32).reshape(1)
    grad_tokens, lines = tokens_back(
        inside, normed_grad, halo_grad, tokens, norm_gain, middle_grad, gain_two, width, [sum_one]
    )
    extra = lines.shape[0]
    home_one = home(sum_one)
    parts_two[1:] = fence(parts_two[1:], [lines, block_out])
    totals = sum(part.astype(F32) for part in parts_two)
    one = home_sum(place.reshape(1), [home_one], 0, quads=quads)
    (one,) = fence([one], [totals, lines, block_out])
    own_one = spread(one)
    totals = jnp.concatenate(
        [totals, jnp.broadcast_to(lines.astype(F32)[None], (shards, extra, width))], axis=1
    )
    parts = own_width // width
    grads = grads.reshape(quads, 3, piece, parts, width).transpose(0, 1, 3, 2, 4)
    grads = grads.reshape(quads, 3 * parts * piece, width)
    two = home_sum(place.reshape(1), [home(totals)], extra, grads, [own_one])
    own_two = lax.all_to_all(two, "quad", 0, 0, tiled=True)
    size = totals.shape[1]
    grad_gate, grad_out = assemble_one(core_one, own_one, swap(own_one))
    (
        grad_input,
        grad_recall,
        grad_admit,
        grad_recall_bias,
        grad_admit_bias,
        grad_taps,
        grad_bias,
        grad_decay,
        gate_mean,
        gain_one,
        gain_two,
        *grads,
    ) = assemble(
        core_one,
        own_two,
        swap(own_two[:, :size]),
        decay_param,
        model,
        heads,
        head,
        count * group * shards,
        piece,
    )
    return (
        block_out,
        grad_tokens,
        gain_one,
        grad_gate,
        grad_input,
        grad_taps,
        grad_bias,
        grad_recall,
        grad_recall_bias,
        grad_admit,
        grad_admit_bias,
        grad_decay,
        grad_out,
        gain_two,
        grads[0],
        grads[1],
        grads[2],
        gate_mean,
    )


def solution(mesh):
    in_specs = (
        P(("quad", "core", "chan"), None),
        P(("quad", "core")),
        P(("quad", "core", "chan"), None),
        P(),
        P(None, "chan"),
        P(None, "chan"),
        P(None, "chan"),
        P("chan"),
        P("chan", None, None),
        P("chan", None),
        P("chan", None, None),
        P("chan", None),
        P("chan"),
        P("chan", None),
        P(),
        P(("quad", "core", "chan"), None),
        P(("quad", "core", "chan"), None),
        P(("quad", "core", "chan"), None),
    )
    out_specs = (
        P(("quad", "core", "chan"), None),
        P(("quad", "core", "chan"), None),
        P(),
        P(None, "chan"),
        P(None, "chan"),
        P(None, "chan"),
        P("chan"),
        P("chan", None, None),
        P("chan", None),
        P("chan", None, None),
        P("chan", None),
        P("chan"),
        P("chan", None),
        P(),
        P(("quad", "core", "chan"), None),
        P(("quad", "core", "chan"), None),
        P(("quad", "core", "chan"), None),
        P("chan"),
    )
    devices = mesh.devices
    quads, shards = devices.shape[0] // 2, devices.shape[1]
    split = jax.sharding.Mesh(devices.reshape(quads, 2, shards), ("quad", "core", "chan"))
    return jax.shard_map(
        on_device, mesh=split, in_specs=in_specs, out_specs=out_specs, check_vma=False
    )
```

```python
import functools

import jax
import jax.numpy as jnp
from jax import lax
from jax.experimental import pallas as pl
from jax.experimental.pallas import tpu as pltpu
from jax.sharding import PartitionSpec as P

LENGTH = 1024
EPS = 1e-06
STRENGTH = 8.0
HALO = 16
TABLE = 256
COST = 0.3
GELU_A = 0.7978845608028654
GELU_B = 0.044715
BF16 = jnp.bfloat16
F32 = jnp.float32
MIB = 1024 * 1024


def mm(left, right, left_dim, right_dim):
    return lax.dot_general(
        left, right, (((left_dim,), (right_dim,)), ((), ())), preferred_element_type=F32
    )


def gelu_parts(value):
    square = value * value
    th = jnp.tanh(GELU_A * value * (1.0 + GELU_B * square))
    half = 0.5 * (1.0 + th)
    slope = half + 0.5 * value * (1.0 - th * th) * (GELU_A * (1.0 + 3.0 * GELU_B * square))
    return value * half, slope


def gelu(value):
    th = jnp.tanh(GELU_A * value * (1.0 + GELU_B * value * value))
    return 0.5 * value * (1.0 + th)


def one_minus_exp(v):
    series = v * (
        1.0
        - v
        * (1 / 2)
        * (
            1.0
            - v
            * (1 / 3)
            * (1.0 - v * (1 / 4) * (1.0 - v * (1 / 5) * (1.0 - v * (1 / 6) * (1.0 - v * (1 / 7)))))
        )
    )
    return jnp.where(v < 0.4, series, 1.0 - jnp.exp(-v))


def rows_index(shape):
    return lax.broadcasted_iota(jnp.int32, shape, 0)


def scan_down(a, b):
    count = a.shape[0]
    index = rows_index(a.shape)
    step = 1
    while step < count:
        if step < 8:
            inside = index >= step
            a_prev = jnp.where(inside, pltpu.roll(a, step, 0), 1.0)
            b_prev = jnp.where(inside, pltpu.roll(b, step, 0), 0.0)
        else:
            a_prev = jnp.concatenate([jnp.ones_like(a[:step]), a[: count - step]], axis=0)
            b_prev = jnp.concatenate([jnp.zeros_like(b[:step]), b[: count - step]], axis=0)
        b = b + a * b_prev
        a = a * a_prev
        step *= 2
    return a, b


def scan_up(a, b):
    count = a.shape[0]
    index = rows_index(a.shape)
    step = 1
    while step < count:
        if step < 8:
            inside = index < count - step
            a_next = jnp.where(inside, pltpu.roll(a, count - step, 0), 1.0)
            b_next = jnp.where(inside, pltpu.roll(b, count - step, 0), 0.0)
        else:
            a_next = jnp.concatenate([a[step:], jnp.ones_like(a[:step])], axis=0)
            b_next = jnp.concatenate([b[step:], jnp.zeros_like(b[:step])], axis=0)
        b = b + a * b_next
        a = a * a_next
        step *= 2
    return a, b


def same_block(width, head):
    row = lax.broadcasted_iota(jnp.int32, (width, 1), 0) // head
    col = lax.broadcasted_iota(jnp.int32, (1, width), 1) // head
    return row == col


def block_diagonal(flat, head, dtype):
    width = flat.shape[1]
    tall = jnp.concatenate([flat] * (width // head), axis=0)
    shape = (width, width)
    del shape
    return jnp.where(same_block(width, head), tall, 0.0).astype(dtype)


def fold_diagonal(square, head):
    width = square.shape[0]
    kept = jnp.where(same_block(width, head), square, 0.0)
    total = kept[:head]
    for start in range(head, width, head):
        total = total + kept[start : start + head]
    return total


def vmem():
    return pl.BlockSpec(memory_space=pltpu.VMEM)


def smem():
    return pl.BlockSpec(memory_space=pltpu.SMEM)


def launch(
    kernel,
    inputs,
    in_specs,
    micros,
    after=(),
    carry=(),
    prefetch=0,
    grid=(),
    out_shape=(),
    out_specs=(),
    scratch_shapes=(),
    aliases=None,
    name=None,
    vmem_mib=60,
):
    count, extra, through = len(inputs), len(after), len(carry)
    made = len(out_shape)
    aliases = dict(aliases or {})
    for i in range(through):
        aliases[count + extra + i] = made + i

    def body(*refs):
        first = count + extra + through
        kernel(*refs[:count], *refs[first : first + made], *refs[first + made + through :])

    anywhere = pl.BlockSpec(memory_space=pl.ANY)
    return pl.pallas_call(
        body,
        out_shape=list(out_shape) + [jax.ShapeDtypeStruct(c.shape, c.dtype) for c in carry],
        grid_spec=pltpu.PrefetchScalarGridSpec(
            num_scalar_prefetch=prefetch,
            grid=grid,
            in_specs=list(in_specs) + [anywhere] * (extra + through),
            out_specs=list(out_specs) + [anywhere] * through,
            scratch_shapes=scratch_shapes,
        ),
        input_output_aliases=aliases,
        compiler_params=pltpu.CompilerParams(vmem_limit_bytes=vmem_mib * MIB),
        cost_estimate=pl.CostEstimate(
            flops=int(micros * 1.1e9 * COST), bytes_accessed=int(micros * 3.5e6 * COST), transcendentals=0
        ),
        name=name,
    )(*inputs, *after, *carry)


def split_features(core, source, own_out, other_out):
    half = own_out.shape[1]
    block = 128
    quads = half // block
    for quad in range(quads):
        for out, who in ((own_out, core), (other_out, 1 - core)):
            start = pl.multiple_of((quad * 2 + who) * block, block)
            out[:, quad * block : (quad + 1) * block] = source[:, pl.ds(start, block)]


def pack_kernel(*refs):
    *pieces, out = refs
    for i, ref in enumerate(pieces):
        out[i] = ref[0]


def pack(pieces, carry, after):
    return launch(
        pack_kernel,
        pieces,
        [vmem()] * len(pieces),
        0.1,
        after,
        carry,
        out_shape=[jax.ShapeDtypeStruct((len(pieces),) + pieces[0].shape[1:], pieces[0].dtype)],
        out_specs=[vmem()],
        name="pack",
        vmem_mib=8,
    )


def fence(carry, after=()):
    return launch(lambda *refs: None, [], [], 0.01, after, carry, name="fence", vmem_mib=60)


def prepare_kernel(
    slots_ref,
    gate_ref,
    input_ref,
    out_ref,
    recall_ref,
    recall_bias_ref,
    admit_ref,
    admit_bias_ref,
    taps_ref,
    bias_ref,
    decay_ref,
    weights,
    table_out,
    pieces_out,
    table,
):
    weights[0] = gate_ref[...]
    weights[1] = input_ref[...]
    weights[2] = out_ref[...].T
    heads, head, _ = recall_ref.shape
    for h in range(heads):
        cols = slice(h * head, (h + 1) * head)
        table[:head, cols] = recall_ref[h]
        table[head : 2 * head, cols] = admit_ref[h]
    side = jnp.concatenate
    lines = side(
        [
            taps_ref[...],
            bias_ref[...].reshape(1, -1),
            side([recall_bias_ref[h : h + 1] for h in range(heads)], axis=1),
            side([admit_bias_ref[h : h + 1] for h in range(heads)], axis=1),
            jax.nn.softplus(-decay_ref[...].reshape(1, -1)),
        ],
        axis=0,
    )
    high = lines.astype(BF16).astype(F32)
    rest = lines - high
    mid = rest.astype(BF16).astype(F32)
    table[2 * head : 2 * head + 8] = high
    table[2 * head + 8 : 2 * head + 16] = mid
    table[2 * head + 16 : 2 * head + 24] = rest - mid
    table[2 * head + 24 :] = jnp.zeros((table.shape[0] - 2 * head - 24, table.shape[1]), F32)
    table_out[...] = table[...].astype(BF16)
    count, rows, _ = pieces_out.shape
    block = pieces_block(weights.shape[1], rows)
    extra = rows - 3 * block
    for k in range(count):
        start = pl.multiple_of(slots_ref[k] * block, block)
        for part in range(3):
            pieces_out[k, part * block : (part + 1) * block] = weights[part, pl.ds(start, block), :]
        start = pl.multiple_of(slots_ref[k] * extra, extra)
        pieces_out[k, 3 * block :] = table_out[pl.ds(start, extra), :]

def norm_kernel(core_ref, ends_ref, tokens_ref, gain_ref, normed_out, *halves_out):
    for ref, rows in ((ends_ref, slice(0, HALO)), (tokens_ref, slice(HALO, None))):
        values = ref[...].astype(F32)
        scale = lax.rsqrt(jnp.mean(values * values, axis=1, keepdims=True) + EPS)
        normed_out[rows] = (values * scale * gain_ref[...]).astype(BF16)
    if halves_out:
        split_features(core_ref[0], normed_out, *halves_out)


def norm(core, ends, tokens, gain, group):
    count, model = tokens.shape
    halves = half_shapes(HALO + count, model, group)
    return launch(
        norm_kernel,
        [core, ends, tokens, gain.reshape(1, model)],
        [smem()] + [vmem()] * 3,
        0.1,
        out_shape=[jax.ShapeDtypeStruct((HALO + count, model), BF16)] + halves,
        out_specs=[vmem()] * (1 + len(halves)),
        name="norm",
        vmem_mib=16,
    )


def pieces_block(model, rows):
    return rows * model // (3 * model + TABLE)


def half_shapes(rows, model, group):
    return [jax.ShapeDtypeStruct((rows, model // 2), BF16)] * (2 if model // group == 128 else 0)


def prepare(slots, gate, inputs, out, recall, recall_bias, admit, admit_bias, taps, bias, decay, group):
    model, width = gate.shape
    rows = (3 * model + TABLE) // group
    return launch(
        prepare_kernel,
        [slots, gate, inputs, out, recall, recall_bias, admit, admit_bias, taps, bias, decay],
        [smem()] + [vmem()] * 10,
        0.1,
        out_shape=[
            jax.ShapeDtypeStruct((3, model, width), BF16),
            jax.ShapeDtypeStruct((TABLE, width), BF16),
            jax.ShapeDtypeStruct((slots.shape[0], rows, width), BF16),
        ],
        out_specs=[vmem()] * 3,
        scratch_shapes=[pltpu.VMEM((TABLE, width), F32)],
        name="prepare",
    )


def mix_local_kernel(own, head, counts, stacked, slots_ref, normed_ref, mask_ref, *rest):
    piece_refs, rest = rest[: len(counts)], rest[len(counts) :]
    weights, inputs_out, gated_out, kept_out, scan_out, edge_out, gates_out, vec_out, sums_out = (
        rest[stacked : stacked + 9]
    )
    (table,) = rest[stacked + 9 :]
    model = normed_ref.shape[1]
    if own:
        weights[0] = piece_refs[0][...]
        table[...] = piece_refs[1][...].astype(F32)
    else:
        number = 0
        for ref, many in zip(piece_refs, counts, strict=True):
            rows = ref.shape[1]
            block = pieces_block(model, rows)
            extra = rows - 3 * block
            for k in range(many):
                slot = slots_ref[number]
                number += 1
                start = pl.multiple_of(slot * block, block)
                for part in range(3):
                    weights[0, part, pl.ds(start, block), :] = ref[
                        k, part * block : (part + 1) * block
                    ]
                start = pl.multiple_of(slot * extra, extra)
                table[pl.ds(start, extra), :] = ref[k, 3 * block :].astype(F32)
    count = mask_ref.shape[0]
    vec = table[2 * head : 2 * head + 8] + (
        table[2 * head + 8 : 2 * head + 16] + table[2 * head + 16 : 2 * head + 24]
    )
    vec_out[0] = vec
    gates_out[0] = table[: 2 * head].astype(BF16)
    gated = mm(normed_ref[HALO:], weights[0, 0], 1, 0).astype(BF16)
    gated_out[0] = gated
    inputs = mm(normed_ref[...], weights[0, 1], 1, 0).astype(BF16)
    inputs_out[0] = inputs
    wide = inputs.astype(F32)
    conv = vec[4:5] + vec[0:1] * wide[HALO:]
    for shift in range(1, 4):
        moved = pltpu.roll(wide, shift, 0)[HALO:]
        conv = conv + vec[shift : shift + 1] * (moved * mask_ref[:, shift : shift + 1])
    low = conv.astype(BF16)
    recall_weight = block_diagonal(table[:head], head, BF16)
    admit_weight = block_diagonal(table[head : 2 * head], head, BF16)
    recall = jax.nn.sigmoid(mm(low, recall_weight, 1, 0) + vec[5:6])
    admit = jax.nn.sigmoid(mm(low, admit_weight, 1, 0) + vec[6:7])
    rate = STRENGTH * recall * vec[7:8]
    decay = jnp.exp(-rate)
    inject = jnp.sqrt(one_minus_exp(2.0 * rate)) * admit * conv
    product, state = scan_down(decay * mask_ref[:, 1:2], inject)
    kept_out[0, 0] = conv
    kept_out[0, 1] = recall
    kept_out[0, 2] = admit
    scan_out[0, 0] = product
    scan_out[0, 1] = state
    edge_out[0, 0:1] = product[count - 1 :]
    edge_out[0, 1:2] = state[count - 1 :]
    sums_out[0] = jnp.sum(decay, axis=0, keepdims=True)


def mix_local(shard, shards, head, slots, normed, mask, pieces, stacks, after=(), carry=()):
    count = mask.shape[0]
    model = normed.shape[1]
    width = pieces[0].shape[-1]
    own = shard == 0
    counts = [p.shape[0] for p in pieces]
    shapes = [
        ((shards, 3, model, width), BF16),
        ((shards, count + HALO, width), BF16),
        ((shards, count, width), BF16),
        ((shards, 3, count, width), F32),
        ((shards, 2, count, width), F32),
        ((shards, 2, width), F32),
        ((shards, 2 * head, width), BF16),
        ((shards, 8, width), F32),
        ((shards, 1, width), F32),
    ]

    def at(shape):
        tail = (0,) * (len(shape) - 1)
        return pl.BlockSpec((1,) + shape[1:], lambda i: (shard,) + tail)

    first = [slots, normed, mask, *pieces]
    in_specs = [smem()] + [vmem()] * (len(first) - 1)
    aliases = {}
    if stacks is not None:
        aliases = {len(first) + i: i for i in range(len(stacks))}
        in_specs += [pl.BlockSpec(memory_space=pl.ANY)] * len(stacks)
        first += list(stacks)
    outs = launch(
        functools.partial(mix_local_kernel, own, head, counts, len(aliases)),
        first,
        in_specs,
        5.7,
        after=after,
        carry=carry,
        grid=(1,),
        out_shape=[jax.ShapeDtypeStruct(shape, dtype) for shape, dtype in shapes],
        out_specs=[at(shape) for shape, _ in shapes],
        scratch_shapes=[pltpu.VMEM((TABLE, width), F32)],
        aliases=aliases,
        name="mix_local",
    )
    return outs[:9], outs[9:]


def carried(edges):
    total = edges[-1][0, 1:2]
    for edge in edges[-2::-1]:
        total = edge[0, 1:2] + edge[0, 0:1] * total
    return total


def branch_kernel(
    depth, scan_ref, gated_ref, weight_ref, resid_ref, gain_ref, *rest
):
    edges = rest[:depth]
    carry_out, branch_in_out, middle_out, second_out, again_out, acc = rest[depth:]
    step = pl.program_id(0)

    @pl.when(step == 0)
    def _():
        acc[...] = resid_ref[...].astype(F32)

    carry = carried(edges)
    carry_out[0] = jnp.broadcast_to(carry, carry_out.shape[1:])
    state = scan_ref[0, 1] + scan_ref[0, 0] * carry
    mixed = (gelu(gated_ref[0].astype(F32)) * state).astype(BF16)
    branch_in_out[0] = mixed
    acc[...] += mm(mixed, weight_ref[0, 0], 1, 1)

    @pl.when(step == pl.num_programs(0) - 1)
    def _():
        middle = acc[...]
        middle_out[...] = middle
        scale = lax.rsqrt(jnp.mean(middle * middle, axis=1, keepdims=True) + EPS)
        second = (middle * scale * gain_ref[...]).astype(BF16)
        second_out[...] = second
        again_out[...] = second


def branch(scan, gated, weights, tokens, gain, edges, after):
    shards, _, count, width = scan.shape
    model = tokens.shape[1]

    def edge_spec(shift):
        return pl.BlockSpec((1, 2, width), lambda s: ((s + shards - shift % shards) % shards, 0, 0))

    return launch(
        functools.partial(branch_kernel, len(edges)),
        [scan, gated, weights, tokens, gain, *edges],
        [
            pl.BlockSpec((1, 2, count, width), lambda s: (s, 0, 0, 0)),
            pl.BlockSpec((1, count, width), lambda s: (s, 0, 0)),
            pl.BlockSpec((1, 1, model, width), lambda s: (s, 2, 0, 0)),
            pl.BlockSpec((count, model), lambda s: (0, 0)),
            pl.BlockSpec((1, model), lambda s: (0, 0)),
        ]
        + [edge_spec(i + 1) for i in range(len(edges))],
        0.1,
        after,
        grid=(shards,),
        out_shape=[
            jax.ShapeDtypeStruct((shards, 8, width), F32),
            jax.ShapeDtypeStruct((shards, count, width), BF16),
            jax.ShapeDtypeStruct((count, model), F32),
            jax.ShapeDtypeStruct((count, model), BF16),
            jax.ShapeDtypeStruct((count, model), BF16),
        ],
        out_specs=[
            pl.BlockSpec((1, 8, width), lambda s: (s, 0, 0)),
            pl.BlockSpec((1, count, width), lambda s: (s, 0, 0)),
            pl.BlockSpec((count, model), lambda s: (0, 0)),
            pl.BlockSpec((count, model), lambda s: (0, 0)),
            pl.BlockSpec((count, model), lambda s: (0, 0)),
        ],
        scratch_shapes=[pltpu.VMEM((count, model), F32)],
        name="mix_branch",
    )


def arrange_kernel(core_ref, own_ref, other_ref, out_ref):
    shards, quads, _, piece, _ = own_ref.shape
    for ref, core in ((own_ref, core_ref[0]), (other_ref, 1 - core_ref[0])):
        for shard in range(shards):
            for quad in range(quads):
                start = pl.multiple_of(((quad * 2 + core) * shards + shard) * piece, piece)
                for part in range(3):
                    out_ref[part, pl.ds(start, piece), :] = ref[shard, quad, part]


def arrange(core, own, other, after):
    shards, quads, _, piece, width = own.shape
    if piece % 16:
        both = jnp.where(core[0] == 0, jnp.stack([own, other]), jnp.stack([other, own]))
        return both.transpose(3, 2, 0, 1, 4, 5).reshape(3, 2 * shards * quads * piece, width)
    return launch(
        arrange_kernel,
        [core, own, other],
        [smem(), vmem(), vmem()],
        0.1,
        after,
        out_shape=[jax.ShapeDtypeStruct((3, 2 * shards * quads * piece, width), BF16)],
        out_specs=[vmem()],
        name="mlp_arrange",
        vmem_mib=16,
    )[0]


def mlp_tiles(width):
    tile = 256 if width % 256 == 0 else width
    return [slice(start, start + tile) for start in range(0, width, tile)]


def mlp_kernel(
    second_ref,
    cot_ref,
    weight_ref,
    gate_grad_out,
    up_grad_out,
    hidden_out,
    back_out,
):
    second = second_ref[...]
    cot = cot_ref[...]
    total = None
    for cols in mlp_tiles(weight_ref.shape[2]):
        gate_weight, up_weight = weight_ref[0, :, cols], weight_ref[1, :, cols]
        gate = mm(second, gate_weight, 1, 0)
        upward = mm(second, up_weight, 1, 0)
        hidden_grad = mm(cot, weight_ref[2, :, cols], 1, 0)
        act, slope = gelu_parts(gate)
        hidden_out[:, cols] = (act * upward).astype(BF16)
        gate_grad = (hidden_grad * upward * slope).astype(BF16)
        up_grad = (hidden_grad * act).astype(BF16)
        gate_grad_out[:, cols] = gate_grad
        up_grad_out[:, cols] = up_grad
        back = mm(gate_grad, gate_weight, 1, 1) + mm(up_grad, up_weight, 1, 1)
        total = back if total is None else total + back
    back_out[...] = total.astype(BF16)


def mlp_block(second, cot, weights, after, carry):
    count, model = second.shape
    width = weights.shape[-1]
    wide = jax.ShapeDtypeStruct((count, width), BF16)
    return launch(
        mlp_kernel,
        [second, cot, weights],
        [vmem()] * 3,
        7.4,
        after,
        carry,
        out_shape=[wide, wide, wide, jax.ShapeDtypeStruct((count, model), BF16)],
        out_specs=[vmem()] * 4,
        name="mlp_block",
        vmem_mib=16,
    )


def mlp_grads_kernel(quads, quad_ref, core_ref, weight_ref, *rest):
    cots, rest = rest[:quads], rest[quads:]
    seconds, rest = rest[:quads], rest[quads:]
    gate_grads, rest = rest[:quads], rest[quads:]
    up_grads, rest = rest[:quads], rest[quads:]
    hiddens, rest = rest[:quads], rest[quads:]
    *grads_out, results_out, second, cot, left, whole_ref = rest
    count = seconds[0].shape[0]
    rows = [slice(rel * count, (rel + 1) * count) for rel in range(quads)]
    for rel in range(quads):
        second[rows[rel]] = seconds[rel][...]
        cot[rows[rel]] = cots[rel][...]
    total = None
    for cols in mlp_tiles(weight_ref.shape[2]):
        for part, (base, group) in enumerate(
            ((second, gate_grads), (second, up_grads), (cot, hiddens))
        ):
            for rel in range(quads):
                left[rows[rel]] = group[rel][:, cols]
            whole = mm(base[...], left[...], 0, 0).astype(BF16)
            if len(grads_out) == 1:
                grads_out[0][part, :, cols] = whole
                continue
            whole_ref[...] = whole
            shards, _, _, piece, _ = grads_out[0].shape
            for out, core in zip(grads_out, (core_ref[0], 1 - core_ref[0]), strict=True):
                for shard in range(shards):
                    for quad in range(quads):
                        start = pl.multiple_of(((quad * 2 + core) * shards + shard) * piece, piece)
                        out[shard, quad, part, :, cols] = whole_ref[pl.ds(start, piece), :]
        result = mm(left[...], weight_ref[2, :, cols], 1, 1)
        total = result if total is None else total + result
    for rel in range(quads):
        results_out[quad_ref[0] ^ rel] = total[rows[rel]].astype(BF16)


def mlp_grads(quad, core, weights, cots, seconds, gate_grads, up_grads, hiddens, shards):
    quads = len(seconds)
    count, model = seconds[0].shape
    width = weights.shape[2]
    tile = mlp_tiles(width)[0].stop
    piece = model // (quads * 2 * shards)
    shapes = [(shards, quads, 3, piece, width)] * 2 if piece % 16 == 0 else [(3, model, width)]
    *grads, results = launch(
        functools.partial(mlp_grads_kernel, quads),
        [quad, core, weights, *cots, *seconds, *gate_grads, *up_grads, *hiddens],
        [smem()] * 2 + [vmem()] * (1 + 5 * quads),
        15.0,
        out_shape=[jax.ShapeDtypeStruct(shape, BF16) for shape in shapes]
        + [jax.ShapeDtypeStruct((quads, count, model), BF16)],
        out_specs=[vmem()] * (1 + len(shapes)),
        scratch_shapes=[
            pltpu.VMEM((quads * count, model), BF16),
            pltpu.VMEM((quads * count, model), BF16),
            pltpu.VMEM((quads * count, tile), BF16),
            pltpu.VMEM((model, tile), BF16),
        ],
        name="mlp_grads",
        vmem_mib=32,
    )
    if piece % 16:
        both = grads[0].reshape(3, quads, 2, shards, piece, width).transpose(2, 3, 1, 0, 4, 5)
        grads = [lax.dynamic_index_in_dim(both, who, 0, False) for who in (core[0], 1 - core[0])]
    return *grads, results


def add_kernel(a_ref, b_ref, out_ref):
    out_ref[...] = (a_ref[...].astype(F32) + b_ref[...].astype(F32)).astype(BF16)


def add_pair(a, b, after=()):
    return launch(
        add_kernel,
        [a, b],
        [vmem()] * 2,
        0.1,
        after,
        out_shape=[jax.ShapeDtypeStruct(a.shape, BF16)],
        out_specs=[vmem()],
        name="add_pair",
        vmem_mib=16,
    )[0]


def middle_kernel(blocks, back_ref, *rest):
    (*backs, values_ref, cot_ref, gain_ref, core_ref), outs = rest[: blocks + 3], rest[blocks + 3 :]
    middle_grad_out, low_out, gain_out, *halves_out = outs
    grad = back_ref[...].astype(F32)
    for ref in backs:
        grad = grad + ref[...].astype(F32)
    values = values_ref[...]
    scale = lax.rsqrt(jnp.mean(values * values, axis=1, keepdims=True) + EPS)
    scaled = grad * gain_ref[...]
    inner = jnp.mean(scaled * values, axis=1, keepdims=True)
    total = cot_ref[...].astype(F32) + scale * scaled - values * (scale * scale * scale * inner)
    middle_grad_out[...] = total
    low_out[...] = total.astype(BF16)
    if halves_out:
        split_features(core_ref[0], low_out, *halves_out)
    gain_out[...] = jnp.sum(grad * values * scale, axis=0, keepdims=True)


def middle_back(backs, values, cot, gain, core, group, after, carry):
    count, model = values.shape
    halves = half_shapes(count, model, group)
    return launch(
        functools.partial(middle_kernel, len(backs)),
        [*backs, values, cot, gain.reshape(1, model), core],
        [vmem()] * (len(backs) + 3) + [smem()],
        0.1,
        after,
        carry,
        out_shape=[
            jax.ShapeDtypeStruct((count, model), F32),
            jax.ShapeDtypeStruct((count, model), BF16),
            jax.ShapeDtypeStruct((1, model), F32),
        ]
        + halves,
        out_specs=[vmem()] * (3 + len(halves)),
        name="middle_back",
        vmem_mib=16,
    )


def tokens_kernel(
    inside_ref, grad_ref, halo_ref, tokens_ref, gain_ref, middle_grad_ref, gain_two_ref, out, lines_out
):
    grad = grad_ref[HALO:]
    count = grad.shape[0]
    last = jnp.where(inside_ref[0] > 0, halo_ref[...].astype(F32), 0.0)
    grad = jnp.concatenate([grad[: count - HALO], grad[count - HALO :] + last], axis=0)
    values = tokens_ref[...].astype(F32)
    scale = lax.rsqrt(jnp.mean(values * values, axis=1, keepdims=True) + EPS)
    scaled = grad * gain_ref[...]
    inner = jnp.mean(scaled * values, axis=1, keepdims=True)
    out[...] = middle_grad_ref[...] + scale * scaled - values * (scale * scale * scale * inner)
    both = (jnp.sum(grad * values * scale, axis=0, keepdims=True), gain_two_ref[...])
    lines_out[...] = pack_gains(both, lines_out.shape[1])


def gain_chunk(model, width):
    chunk = 128
    while chunk * 2 <= width:
        chunk *= 2
    while chunk > width:
        chunk //= 2
    return chunk


def gain_lines(model, width):
    return 4 * (model // gain_chunk(model, width))


def pack_gains(both, width):
    chunk = gain_chunk(both[0].shape[1], width)
    lines = []
    for value in both:
        high = value.astype(BF16).astype(F32)
        for term in (high, value - high):
            lines += [term[:, i : i + chunk] for i in range(0, term.shape[1], chunk)]
    lines = jnp.concatenate(lines, axis=0)
    if chunk < width:
        blank = jnp.zeros((lines.shape[0], width - chunk), F32)
        lines = jnp.concatenate([lines, blank], axis=1)
    return lines.astype(BF16)


def unpack_gains(lines, model):
    chunk = gain_chunk(model, lines.shape[1])
    many = model // chunk
    lines = lines.astype(F32)
    both = []
    for i in range(2):
        value = lines[2 * i * many : (2 * i + 1) * many] + lines[
            (2 * i + 1) * many : (2 * i + 2) * many
        ]
        both.append(
            jnp.concatenate([value[j : j + 1, :chunk] for j in range(many)], axis=1)
        )
    return both


def tokens_back(inside, grad, halo, tokens, gain, middle_grad, gain_two, width, after):
    count, model = tokens.shape
    return launch(
        tokens_kernel,
        [inside, grad, halo, tokens, gain.reshape(1, model), middle_grad, gain_two],
        [smem()] + [vmem()] * 6,
        0.1,
        after,
        out_shape=[
            jax.ShapeDtypeStruct((count, model), F32),
            jax.ShapeDtypeStruct((gain_lines(model, width), width), BF16),
        ],
        out_specs=[vmem()] * 2,
        name="tokens_back",
        vmem_mib=16,
    )


def adjoint_kernel(
    grad_ref,
    weight_ref,
    gated_ref,
    scan_ref,
    kept_ref,
    carry_ref,
    mask_ref,
    vec_ref,
    gate_back_out,
    adjoint_out,
    edge_out,
):
    into = mm(grad_ref[...], weight_ref[0, 0], 1, 0).astype(BF16).astype(F32)
    act, slope = gelu_parts(gated_ref[0].astype(F32))
    state = scan_ref[0, 1] + scan_ref[0, 0] * carry_ref[0, 0:1]
    gate_back_out[0] = (into * state * slope).astype(BF16)
    decay = jnp.exp(-STRENGTH * kept_ref[0, 0] * vec_ref[0, 7:8]) * mask_ref[:, 1:2]
    count = decay.shape[0]
    shifted = jnp.where(
        rows_index(decay.shape) < count - 1, pltpu.roll(decay, count - 1, 0), 1.0
    )
    product, value = scan_up(shifted, into * act)
    adjoint_out[0, 0] = product
    adjoint_out[0, 1] = value
    edge_out[0] = decay[0:1] * value[0:1]


def adjoint(grad, weights, gated, scan, kept, carry, mask, vec, through):
    shards, _, count, width = scan.shape
    model = grad.shape[1]

    def flat(*shape):
        return pl.BlockSpec(shape, lambda s: (0,) * len(shape))

    def at(*shape):
        return pl.BlockSpec((1,) + shape, lambda s: (s,) + (0,) * len(shape))

    return launch(
        adjoint_kernel,
        [grad, weights, gated, scan, kept, carry, mask, vec],
        [
            flat(count, model),
            pl.BlockSpec((1, 1, model, width), lambda s: (s, 2, 0, 0)),
            at(count, width),
            at(2, count, width),
            pl.BlockSpec((1, 1, count, width), lambda s: (s, 1, 0, 0)),
            at(8, width),
            flat(*mask.shape),
            at(8, width),
        ],
        0.1,
        carry=through,
        grid=(shards,),
        out_shape=[
            jax.ShapeDtypeStruct((shards, count, width), BF16),
            jax.ShapeDtypeStruct((shards, 2, count, width), F32),
            jax.ShapeDtypeStruct((shards, 1, width), F32),
        ],
        out_specs=[at(count, width), at(2, count, width), at(1, width)],
        name="mix_adjoint",
    )


def outer_kernel(groups, quads, core_ref, quad_ref, *rest):
    pairs, rest = rest[: 4 * groups], rest[4 * groups :]
    *rest, left, right, small, whole = rest
    if len(rest) in (3, 2 + quads):
        smalls, outs = rest[:2], rest[2:]
    else:
        smalls, outs = [], rest
    count = pairs[2].shape[1]
    shards = outs[0].shape[-3]
    block = left.shape[1] // quads

    def put(s, rows, member, values):
        if len(outs) == 1:
            outs[0][member, s, rows] = values
        else:
            outs[member][s, rows] = values

    for group in range(groups):
        left_ref, left_other, right_ref, right_other = pairs[4 * group : 4 * group + 4]
        left[:count] = left_ref[left_ref.shape[0] - count :]
        left[count:] = left_other[left_ref.shape[0] - count :]
        rows = slice(group * block, (group + 1) * block)
        for s in range(shards):
            right[:count] = right_ref[s]
            right[count:] = right_other[s]
            whole[...] = mm(left[...], right[...], 0, 0).astype(BF16)
            for member in range(quads):
                quad = member if len(outs) == 1 else quad_ref[0] ^ member
                start = quad * block
                if len(outs) > 1:
                    start = pl.multiple_of(start, block)
                put(s, rows, member, whole[pl.ds(start, block), :])
    if smalls:
        extra = outs[0].shape[-2] - groups * block
        rows = slice(groups * block, groups * block + extra)
        for s in range(shards):
            small[...] = (smalls[0][s].astype(F32) + smalls[1][s].astype(F32)).astype(BF16)
            for member in range(quads):
                quad = member if len(outs) == 1 else quad_ref[0] ^ member
                start = pl.multiple_of((quad * 2 + core_ref[0]) * extra, extra)
                put(s, rows, member, small[pl.ds(start, extra), :])


def outer(core, quad, quads, pairs, smalls=(), after=(), relative=False):
    shards, count, width = pairs[2].shape
    model = pairs[0].shape[1]
    groups = len(pairs) // 4
    rows = groups * model // quads + (TABLE // (2 * quads) if smalls else 0)
    shapes = [(shards, rows, width)] * quads if relative else [(quads, shards, rows, width)]
    return launch(
        functools.partial(outer_kernel, groups, quads),
        [core, quad, *pairs, *smalls],
        [smem()] * 2 + [vmem()] * (len(pairs) + len(smalls)),
        0.1,
        after,
        out_shape=[jax.ShapeDtypeStruct(shape, BF16) for shape in shapes],
        out_specs=[vmem()] * len(shapes),
        scratch_shapes=[
            pltpu.VMEM((2 * count, model), BF16),
            pltpu.VMEM((2 * count, width), BF16),
            pltpu.VMEM((TABLE, width), BF16),
            pltpu.VMEM((model, width), BF16),
        ],
        name="mix_outer",
    )


def mix_back_kernel(
    head,
    depth,
    gate_weight_ref,
    input_weight_ref,
    inputs_ref,
    gate_back_ref,
    kept_ref,
    scan_ref,
    adjoint_ref,
    carry_ref,
    mask_ref,
    gates_ref,
    vec_ref,
    edge_ref,
    *rest,
):
    backs, decays = rest[:depth], rest[depth : 2 * depth - 1]
    input_back_out, small_out, normed_grad_out, acc = rest[2 * depth - 1 :]
    step = pl.program_id(0)
    count = mask_ref.shape[0]
    width = vec_ref.shape[2]
    vec = vec_ref[0]
    incoming = backs[-1][0, 0:1]
    for back, edge in zip(backs[-2::-1], decays[::-1], strict=True):
        incoming = back[0, 0:1] + edge[0, 0:1] * incoming
    adj = adjoint_ref[0, 1] + adjoint_ref[0, 0] * incoming
    carry = carry_ref[0, 0:1]
    state = scan_ref[0, 1] + scan_ref[0, 0] * carry
    before = jnp.where(rows_index(state.shape) == 0, carry, pltpu.roll(state, 1, 0))
    conv, recall, admit = kept_ref[0, 0], kept_ref[0, 1], kept_ref[0, 2]
    speed = STRENGTH * vec[7:8]
    rate = recall * speed
    decay = jnp.exp(-rate)
    square = one_minus_exp(2.0 * rate)
    inverse = lax.rsqrt(square)
    sized = adj * jnp.sqrt(square)
    pulled = adj * admit
    log_grad = decay * (adj * before * mask_ref[:, 1:2] - pulled * conv * decay * inverse)
    recall_grad = -speed * log_grad * recall * (1.0 - recall)
    admit_grad = sized * conv * admit * (1.0 - admit)
    conv_grad = sized * admit
    recall_low = recall_grad.astype(BF16)
    admit_low = admit_grad.astype(BF16)
    gates = gates_ref[0].astype(F32)
    recall_weight = block_diagonal(gates[:head], head, BF16)
    admit_weight = block_diagonal(gates[head:], head, BF16)
    conv_grad = conv_grad + mm(recall_low, recall_weight, 1, 1) + mm(admit_low, admit_weight, 1, 1)
    wide = inputs_ref[0].astype(F32)
    blank = jnp.zeros((HALO, width), F32)
    reach = jnp.concatenate([blank, vec[0:1] * conv_grad], axis=0)
    tap_grads = [jnp.sum(conv_grad * wide[HALO:], axis=0, keepdims=True)]
    for shift in range(1, 4):
        masked = conv_grad * mask_ref[:, shift : shift + 1]
        moved = pltpu.roll(wide, shift, 0)[HALO:]
        tap_grads.append(jnp.sum(masked * moved, axis=0, keepdims=True))
        back = jnp.concatenate([blank, vec[shift : shift + 1] * masked], axis=0)
        reach = reach + pltpu.roll(back, count + HALO - shift, 0)
    input_back = reach.astype(BF16)
    conv_low = conv.astype(BF16)
    input_back_out[0] = input_back
    small_out[0, :head] = fold_diagonal(mm(conv_low, recall_low, 0, 0), head).astype(BF16)
    small_out[0, head : 2 * head] = fold_diagonal(mm(conv_low, admit_low, 0, 0), head).astype(BF16)
    rows = tap_grads + [
        jnp.sum(conv_grad, axis=0, keepdims=True),
        jnp.sum(recall_grad, axis=0, keepdims=True),
        jnp.sum(admit_grad, axis=0, keepdims=True),
        jnp.sum(recall * log_grad, axis=0, keepdims=True),
        edge_ref[0],
    ]
    rows.append(jnp.zeros((TABLE - 2 * head - len(rows), width), F32))
    small_out[0, 2 * head :] = jnp.concatenate(rows, axis=0).astype(BF16)
    through_gate = mm(gate_back_ref[0], gate_weight_ref[0, 0], 1, 1)
    through_input = mm(input_back, input_weight_ref[0, 0], 1, 1)

    @pl.when(step == 0)
    def _():
        acc[...] = through_input

    @pl.when(step > 0)
    def _():
        acc[...] += through_input

    acc[HALO:] += through_gate

    @pl.when(step == pl.num_programs(0) - 1)
    def _():
        normed_grad_out[...] = acc[...]


def mix_back(
    weights, inputs, gate_back, kept, scan, adj, carry, mask, gates, vec, edge, backs, ahead, after
):
    shards, _, count, width = scan.shape
    model = weights.shape[2]
    head = gates.shape[1] // 2
    depth = len(backs)

    def flat(*shape):
        return pl.BlockSpec(shape, lambda s: (0,) * len(shape))

    def at(*shape):
        return pl.BlockSpec((1,) + shape, lambda s: (s,) + (0,) * len(shape))

    def ahead_spec(shift, rows=2):
        return pl.BlockSpec((1, rows, width), lambda s: ((s + shift) % shards, 0, 0))

    return launch(
        functools.partial(mix_back_kernel, head, depth),
        [
            weights, weights, inputs, gate_back, kept, scan, adj, carry, mask, gates, vec,
            edge, *backs, *ahead,
        ],
        [
            pl.BlockSpec((1, 1, model, width), lambda s: (s, 0, 0, 0)),
            pl.BlockSpec((1, 1, model, width), lambda s: (s, 1, 0, 0)),
            at(count + HALO, width),
            at(count, width),
            at(3, count, width),
            at(2, count, width),
            at(2, count, width),
            at(8, width),
            flat(*mask.shape),
            at(2 * head, width),
            at(8, width),
            at(1, width),
        ]
        + [ahead_spec(i + 1, 1) for i in range(depth)]
        + [ahead_spec(i + 1) for i in range(depth - 1)],
        0.1,
        after,
        grid=(shards,),
        out_shape=[
            jax.ShapeDtypeStruct((shards, count + HALO, width), BF16),
            jax.ShapeDtypeStruct((shards, TABLE, width), BF16),
            jax.ShapeDtypeStruct((count + HALO, model), F32),
        ],
        out_specs=[at(count + HALO, width), at(TABLE, width), flat(count + HALO, model)],
        scratch_shapes=[pltpu.VMEM((count + HALO, model), F32)],
        name="mix_back",
    )


def home_kernel(groups, shards, place_ref, *rest):
    parts, rest = rest[: groups * shards], rest[groups * shards :]
    if len(rest) == 1:
        (out,) = rest
        start = 0
        for group in range(groups):
            refs = parts[group * shards : (group + 1) * shards]
            size = refs[0].shape[0]
            total = refs[0][...].astype(F32)
            for ref in refs[1:]:
                total = total + ref[...].astype(F32)
            for quad in range(out.shape[0]):
                out[quad, start : start + size] = total.astype(BF16)
            start += size
        return
    grads_ref, out, lines = rest
    rows = parts[0].shape[0]
    size = rows - lines.shape[1]
    total = parts[0][:size].astype(F32)
    for ref in parts[1:]:
        total = total + ref[:size].astype(F32)
    total = total.astype(BF16)
    for s in range(shards):
        lines[s] = parts[s][size:].astype(F32)
    model = lines.shape[1] // 4 * gain_chunk(0, lines.shape[2])
    gains = None
    for owner in range(shards):
        which = lax.rem(owner - place_ref[0] + shards, shards)
        value = unpack_gains(lines[which], model)
        gains = value if gains is None else [a + b for a, b in zip(gains, value, strict=True)]
    gains = pack_gains(gains, lines.shape[2])
    for quad in range(out.shape[0]):
        out[quad, :size] = total
        out[quad, size:rows] = gains
        out[quad, rows:] = grads_ref[quad]


def home_sum(place, groups, extra, grads=None, after=(), quads=1):
    shards = len(groups[0])
    rows = sum(group[0].shape[0] for group in groups)
    width = groups[0][0].shape[1]
    inputs = [place, *[part for group in groups for part in group]]
    shape = (quads, rows, width)
    if grads is not None:
        inputs.append(grads)
        shape = (grads.shape[0], rows + grads.shape[1], width)
    return launch(
        functools.partial(home_kernel, len(groups), shards),
        inputs,
        [smem()] + [vmem()] * (len(inputs) - 1),
        0.1,
        after,
        out_shape=[jax.ShapeDtypeStruct(shape, BF16)],
        out_specs=[vmem()],
        scratch_shapes=[pltpu.VMEM((shards, extra, width), F32)] if extra else [],
        name="home_sum",
        vmem_mib=16,
    )[0]


def assemble_one_kernel(core_ref, own_ref, other_ref, gate_out, out_out, whole):
    quads, rows, _ = own_ref.shape
    block = rows // 2
    for quad in range(quads):
        for ref, who in ((own_ref, core_ref[0]), (other_ref, 1 - core_ref[0])):
            start = pl.multiple_of((quad * 2 + who) * block, block)
            gate_out[pl.ds(start, block), :] = ref[quad, :block].astype(F32)
            whole[pl.ds(start, block), :] = ref[quad, block:].astype(F32)
    out_out[...] = whole[...].T


def assemble_one(core, own, other):
    quads, rows, width = own.shape
    model = quads * rows
    return launch(
        assemble_one_kernel,
        [core, own, other],
        [smem(), vmem(), vmem()],
        0.1,
        out_shape=[
            jax.ShapeDtypeStruct((model, width), F32),
            jax.ShapeDtypeStruct((width, model), F32),
        ],
        out_specs=[vmem()] * 2,
        scratch_shapes=[pltpu.VMEM((model, width), F32)],
        name="assemble_one",
        vmem_mib=16,
    )


def assemble_kernel(
    rows_total,
    rows,
    core_ref,
    own_ref,
    other_ref,
    decay_ref,
    input_out,
    recall_out,
    admit_out,
    recall_bias_out,
    admit_bias_out,
    taps_out,
    bias_out,
    decay_out,
    mean_out,
    gain_one_out,
    gain_two_out,
    *rest,
):
    *grads_out, small = rest
    quads, _, width = other_ref.shape
    piece, hidden = grads_out[0].shape
    parts = hidden // (quads * width)
    for quad in range(quads):
        for part in range(3):
            for i in range(parts):
                start = rows + (part * parts + i) * piece
                first = (quad * parts + i) * width
                grads_out[part][:, first : first + width] = own_ref[
                    quad, start : start + piece
                ].astype(F32)
    model = input_out.shape[0]
    block = model // (2 * quads)
    extra = TABLE // (2 * quads)
    for quad in range(quads):
        for ref, who in ((own_ref, core_ref[0]), (other_ref, 1 - core_ref[0])):
            start = pl.multiple_of((quad * 2 + who) * block, block)
            input_out[pl.ds(start, block), :] = ref[quad, :block].astype(F32)
            start = pl.multiple_of((quad * 2 + who) * extra, extra)
            small[pl.ds(start, extra), :] = ref[quad, block : block + extra].astype(F32)
    heads, head, _ = recall_out.shape
    lines = small[2 * head : 2 * head + 16]
    for h in range(heads):
        cols = slice(h * head, (h + 1) * head)
        recall_out[h] = small[:head, cols]
        admit_out[h] = small[head : 2 * head, cols]
        recall_bias_out[h : h + 1] = lines[5:6, cols]
        admit_bias_out[h : h + 1] = lines[6:7, cols]
    taps_out[...] = lines[:4]
    bias_out[...] = lines[4]
    decay_out[...] = lines[7] * (STRENGTH * jax.nn.sigmoid(-decay_ref[...]))
    mean_out[...] = lines[8] * (1.0 / rows_total)
    gains = None
    for ref in (own_ref, other_ref):
        part = None
        for quad in range(quads):
            value = unpack_gains(ref[quad, block + extra : rows], model)
            part = value if part is None else [a + b for a, b in zip(part, value, strict=True)]
        gains = part if gains is None else [a + b for a, b in zip(gains, part, strict=True)]
    gain_one_out[...] = gains[0].reshape(model)
    gain_two_out[...] = gains[1].reshape(model)


def assemble(core, own, other, size, decay, model, heads, head, rows_total, piece):
    width = own.shape[2]
    hidden = own.shape[0] * (own.shape[1] - size) * width // (3 * piece)
    shapes = [
        (model, width),
        (heads, head, head),
        (heads, head, head),
        (heads, head),
        (heads, head),
        (4, width),
        (width,),
        (width,),
        (width,),
        (model,),
        (model,),
        (piece, hidden),
        (piece, hidden),
        (piece, hidden),
    ]
    return launch(
        functools.partial(assemble_kernel, rows_total, size),
        [core, own, other, decay],
        [smem(), vmem(), vmem(), vmem()],
        0.1,
        out_shape=[jax.ShapeDtypeStruct(shape, F32) for shape in shapes],
        out_specs=[vmem()] * len(shapes),
        scratch_shapes=[pltpu.VMEM((TABLE, width), F32)],
        name="assemble",
        vmem_mib=16,
    )


def on_device(
    tokens,
    doc_ids,
    cotangent,
    norm_gain,
    gate_proj,
    input_proj,
    conv_weight,
    conv_bias,
    recall_weight,
    recall_bias,
    admit_weight,
    admit_bias,
    decay_param,
    out_proj,
    mlp_gain,
    mlp_gate,
    mlp_up,
    mlp_down,
):
    count, model = tokens.shape
    width = gate_proj.shape[1]
    heads, head, _ = recall_weight.shape
    hidden_width = mlp_gate.shape[1]
    piece = mlp_gate.shape[0]
    quads = lax.axis_size("quad")
    shards = lax.axis_size("chan")
    group = 2 * quads
    quad = lax.axis_index("quad").astype(jnp.int32)
    core = lax.axis_index("core").astype(jnp.int32)
    place = lax.axis_index("chan").astype(jnp.int32)
    quad_one, core_one = quad.reshape(1), core.reshape(1)

    def hop(values, rel):
        return lax.ppermute(values, "quad", [(i, i ^ rel) for i in range(quads)])

    def swap(values):
        return lax.ppermute(values, "core", [(0, 1), (1, 0)])

    def along(values, shift):
        return lax.ppermute(values, "chan", [(i, (i + shift) % shards) for i in range(shards)])

    def share(values):
        every = jnp.broadcast_to(values[None], (quads,) + values.shape)
        return lax.all_to_all(every, "quad", 0, 0, tiled=True)

    slots = (quad * 2 + core).reshape(1)
    arriving = jnp.stack([(quad ^ rel) * 2 for rel in range(quads)])
    arriving = jnp.concatenate([arriving + core, arriving + 1 - core])

    def halves(values, made):
        if made:
            return made
        rows = values.shape[0]
        split = values.reshape(rows, quads, 2, model // group)
        return [
            lax.dynamic_index_in_dim(split, who, 2, False).reshape(rows, model // 2)
            for who in (core, 1 - core)
        ]

    ends = along(tokens[count - HALO :], 1)
    own_weights, own_table, pieces = prepare(
        slots,
        gate_proj,
        input_proj,
        out_proj,
        recall_weight,
        recall_bias,
        admit_weight,
        admit_bias,
        conv_weight,
        conv_bias,
        decay_param,
        group,
    )
    arrived = along(pieces, 1)
    normed, *made = norm(core_one, ends, tokens, norm_gain, group)

    offset = place * count
    spots = (offset + jnp.arange(count)) % LENGTH
    padded = jnp.concatenate([jnp.full((HALO,), -1, jnp.int32), doc_ids])
    here = lax.dynamic_slice_in_dim(padded, offset + HALO, count)
    columns = [jnp.ones((count,), F32)]
    for shift in range(1, 4):
        moved = lax.dynamic_slice_in_dim(padded, offset + HALO - shift, count)
        columns.append(((spots >= shift) & (here == moved)).astype(F32))
    columns += [jnp.zeros((count,), F32)] * 4
    mask = jnp.stack(columns, axis=1)

    own_width = hidden_width // quads
    slices = jnp.stack([mlp_gate, mlp_up, mlp_down])
    slices = slices.reshape(3, piece, quads, own_width).transpose(2, 0, 1, 3)
    def local(shard, weight_pieces, stacks, after=()):
        return mix_local(
            shard, shards, head, arriving, normed, mask, weight_pieces, stacks, after
        )

    normed_own, normed_other = halves(normed, made)
    normed_other = swap(normed_other)
    stacks, _ = local(0, [own_weights, own_table], None)
    (slices,) = fence([slices], [pieces])
    slices = lax.all_to_all(slices, "quad", 0, 0, tiled=True)
    near = quads // 2 + 1
    cots = [cotangent] + [hop(cotangent, rel) for rel in range(1, near)]
    gathered, waits, edges, shard_pieces = None, [normed_other, *cots[1:]], [stacks[5]], []
    for s in range(1, shards + 1):
        onward = [arrived] if s < shards else [cotangent]
        if s == min(2, shards - 1):
            onward.append(slices)
        if s == 1:
            arrived, *onward = fence(onward, waits)
        else:
            packed, arrived, *onward = pack(held, onward, [edges[s - 2]])
            stacks, _ = local(s - 1, [packed, swap(packed)], stacks)
            edges.append(stacks[5])
        if onward:
            gathered = lax.all_gather(onward[0], "chan", axis=0)
        if s == shards:
            cots += [hop(arrived, rel) for rel in range(near, quads)]
            break
        held = [arrived] + [hop(arrived, rel) for rel in range(1, quads)]
        if s < shards - 1:
            arrived = along(arrived, 1)
    weights, inputs, gated, kept, scan, edge, gates, vec, sums = stacks
    edge, gathered = fence([edge, gathered], cots[near:])
    other_gathered = swap(gathered)
    depth = LENGTH // count - 1
    behind = [along(edge, i + 1) for i in range(depth)]
    carry, branch_in, middle, second, again = branch(
        scan, gated, weights, tokens, mlp_gain.reshape(1, model), behind, []
    )
    mlp_weights = arrange(core_one, gathered, other_gathered, [second])
    ahead = [along(edge, -(i + 1)) for i in range(depth - 1)]

    gate_grads, up_grads, hiddens, backs, seconds = [], [], [], [], []
    for rel in range(quads):
        if rel == 0:
            seconds.append(second)
        else:
            seconds.append(hop(second if rel < near else again, rel))
        gate_grad, up_grad, hidden, back, *carry_on = mlp_block(
            seconds[rel], cots[rel], mlp_weights,
            backs[-1:] if rel else [*ahead], [] if rel else [again],
        )
        if rel == 0:
            (again,) = carry_on
        gate_grads.append(gate_grad)
        up_grads.append(up_grad)
        hiddens.append(hidden)
        backs.append(back)
    backs = [hop(back, rel) if rel else back for rel, back in enumerate(backs)]
    own_grads, other_grads, results = mlp_grads(
        quad_one, core_one, mlp_weights, cots, seconds, gate_grads, up_grads, hiddens, shards
    )
    results = lax.all_to_all(results, "quad", 0, 0, tiled=True)
    middle_grad, branch_grad, gain_two, *made, own_grads, other_grads = middle_back(
        backs, middle, cotangent, mlp_gain, core_one, group, [], [own_grads, other_grads]
    )

    def spread(chip):
        return lax.all_to_all(chip, "quad", 0, 0, tiled=True)

    def add_up(arrived):
        return jnp.sum(arrived.astype(F32), axis=0)

    grad_own, grad_other = halves(branch_grad, made)
    gate_back, adj, edge_back, branch_in = adjoint(
        branch_grad, weights, gated, scan, kept, carry, mask, vec, [branch_in]
    )
    edges_back = [along(edge_back, -(i + 1)) for i in range(depth)]
    (chip_one,) = outer(
        core_one,
        quad_one,
        quads,
        [
            normed_own,
            normed_other,
            gate_back,
            swap(gate_back),
            grad_own,
            swap(grad_other),
            branch_in,
            swap(branch_in),
        ],
    )
    grads = add_pair(own_grads, swap(other_grads), [*edges_back, chip_one])
    (chip_one,) = fence([chip_one], [*edges_back, results, grads])
    grads = lax.psum_scatter(grads, "chan", scatter_dimension=0)

    def home(totals):
        return [totals[0]] + [along(totals[s].astype(BF16), -s) for s in range(1, shards)]

    arrived_one = spread(chip_one)
    input_back, small, normed_grad = mix_back(
        weights, inputs, gate_back, kept, scan, adj, carry, mask, gates, vec, sums, edges_back, ahead,
        [chip_one],
    )

    chip_two = outer(
        core_one,
        quad_one,
        quads,
        [normed_own, normed_other, input_back, swap(input_back)],
        [small, swap(small)],
        relative=True,
    )
    parts_two = [chip_two[0]] + [hop(chip_two[rel], rel) for rel in range(1, quads)]
    sum_one = add_up(arrived_one)
    (results,) = fence([results], [sum_one])
    block_out = (middle + jnp.sum(results.astype(F32), axis=0)).astype(BF16)
    halo_grad = along(normed_grad[:HALO].astype(BF16), -1)
    inside = ((place + 1) * count % LENGTH != 0).astype(jnp.int32).reshape(1)
    grad_tokens, lines = tokens_back(
        inside, normed_grad, halo_grad, tokens, norm_gain, middle_grad, gain_two, width, [sum_one]
    )
    extra = lines.shape[0]
    home_one = home(sum_one)
    parts_two[1:] = fence(parts_two[1:], [lines, block_out])
    totals = sum(part.astype(F32) for part in parts_two)
    one = home_sum(place.reshape(1), [home_one], 0, quads=quads)
    (one,) = fence([one], [totals, lines, block_out])
    own_one = spread(one)
    totals = jnp.concatenate(
        [totals, jnp.broadcast_to(lines.astype(F32)[None], (shards, extra, width))], axis=1
    )
    parts = own_width // width
    grads = grads.reshape(quads, 3, piece, parts, width).transpose(0, 1, 3, 2, 4)
    grads = grads.reshape(quads, 3 * parts * piece, width)
    two = home_sum(place.reshape(1), [home(totals)], extra, grads, [own_one])
    own_two = lax.all_to_all(two, "quad", 0, 0, tiled=True)
    size = totals.shape[1]
    grad_gate, grad_out = assemble_one(core_one, own_one, swap(own_one))
    (
        grad_input,
        grad_recall,
        grad_admit,
        grad_recall_bias,
        grad_admit_bias,
        grad_taps,
        grad_bias,
        grad_decay,
        gate_mean,
        gain_one,
        gain_two,
        *grads,
    ) = assemble(
        core_one,
        own_two,
        swap(own_two),
        size,
        decay_param,
        model,
        heads,
        head,
        count * group * shards,
        piece,
    )
    return (
        block_out,
        grad_tokens,
        gain_one,
        grad_gate,
        grad_input,
        grad_taps,
        grad_bias,
        grad_recall,
        grad_recall_bias,
        grad_admit,
        grad_admit_bias,
        grad_decay,
        grad_out,
        gain_two,
        grads[0],
        grads[1],
        grads[2],
        gate_mean,
    )


def solution(mesh):
    in_specs = (
        P(("quad", "core", "chan"), None),
        P(("quad", "core")),
        P(("quad", "core", "chan"), None),
        P(),
        P(None, "chan"),
        P(None, "chan"),
        P(None, "chan"),
        P("chan"),
        P("chan", None, None),
        P("chan", None),
        P("chan", None, None),
        P("chan", None),
        P("chan"),
        P("chan", None),
        P(),
        P(("quad", "core", "chan"), None),
        P(("quad", "core", "chan"), None),
        P(("quad", "core", "chan"), None),
    )
    out_specs = (
        P(("quad", "core", "chan"), None),
        P(("quad", "core", "chan"), None),
        P(),
        P(None, "chan"),
        P(None, "chan"),
        P(None, "chan"),
        P("chan"),
        P("chan", None, None),
        P("chan", None),
        P("chan", None, None),
        P("chan", None),
        P("chan"),
        P("chan", None),
        P(),
        P(("quad", "core", "chan"), None),
        P(("quad", "core", "chan"), None),
        P(("quad", "core", "chan"), None),
        P("chan"),
    )
    devices = mesh.devices
    quads, shards = devices.shape[0] // 2, devices.shape[1]
    split = jax.sharding.Mesh(devices.reshape(quads, 2, shards), ("quad", "core", "chan"))
    return jax.shard_map(
        on_device, mesh=split, in_specs=in_specs, out_specs=out_specs, check_vma=False
    )
```
